32 devices in a mesh: rep: 16 (over z, y, core), shard: 2 (over x).
Axes of the slice: x: 2, y: 2, z: 4, core: 2. Of those that a mesh axis runs over, the one named last changes fastest.
Arguments:
- latents: bfloat16 [32, 256, 384], P(('rep', 'shard')), may hold values from -6 to 6
- timestep_embed: float32 [32, 384], P(('rep', 'shard')), may hold values from -3 to 3
- labels: int32 [32], P(('rep', 'shard')), may hold values from 0 to 1000
- counts: int32 [32], P(('rep', 'shard')), may hold values from 0 to 1, as said below
- class_table: bfloat16 [1001, 384], P(None, 'shard'), may hold values from -3 to 3
- ada_weight: bfloat16 [2, 384, 2304], P(None, 'shard'), may hold values from -0.3125 to 0.3125
- ada_bias: bfloat16 [2, 2304], P(None, 'shard'), may hold values from -2 to 2
- qkv_weight: bfloat16 [2, 384, 1152], P(None, 'shard'), may hold values from -0.3125 to 0.3125
- qv_bias: bfloat16 [2, 768], P(None, 'shard'), may hold values from -3 to 3
- out_weight: bfloat16 [2, 384, 384], P(None, 'shard'), may hold values from -0.625 to 0.625
- out_bias: bfloat16 [2, 384], P(None, 'shard'), may hold values from -3 to 3
- up_weight: bfloat16 [2, 384, 1536], P(None, 'shard'), may hold values from -0.3125 to 0.3125
- up_bias: bfloat16 [2, 1536], P(None, 'shard'), may hold values from -3 to 3
- down_weight: bfloat16 [2, 1536, 384], P(None, 'shard'), may hold values from -0.15625 to 0.15625
- down_bias: bfloat16 [2, 384], P(None, 'shard'), may hold values from -3 to 3
- cotangent: bfloat16 [32, 256, 384], P(('rep', 'shard')), may hold values from -6 to 6
Outputs:
- activations: bfloat16 [32, 256, 384], P(('rep', 'shard'))
- latents_grad: float32 [32, 256, 384], P(('rep', 'shard'))
- cond_grad: float32 [32, 384], P(('rep', 'shard'))
- table_grad: float32 [1001, 384], P(None, 'shard')
- ada_weight_grad: float32 [2, 384, 2304], P(None, 'shard')
- ada_bias_grad: float32 [2, 2304], P(None, 'shard')
- qkv_weight_grad: float32 [2, 384, 1152], P(None, 'shard')
- qv_bias_grad: float32 [2, 768], P(None, 'shard')
- out_weight_grad: float32 [2, 384, 384], P(None, 'shard')
- out_bias_grad: float32 [2, 384], P(None, 'shard')
- up_weight_grad: float32 [2, 384, 1536], P(None, 'shard')
- up_bias_grad: float32 [2, 1536], P(None, 'shard')
- down_weight_grad: float32 [2, 1536, 384], P(None, 'shard')
- down_bias_grad: float32 [2, 384], P(None, 'shard')
The draws below stay inside these ranges and needn't reach their ends.
Inputs may be any that keep to these rules, and one draw needn't show every extreme that they name: `counts`: whether a device's single slot holds a live latent (1) or not (0); some device holds 1 and some holds 0.
All inputs are finite; a program needn't handle non-finite values.
Results may differ from the reference program's by a relative error of at most 0.012.
Values may be sent and summed in bfloat16 or wider, within the bound.
No kernel may reach another device: no remote copies, remote signals or barrier semaphores. Data moves between devices by JAX's collectives and lax.ppermute only.
A program may use at most 128 MiB of HBM per device.

```python
import math
import jax
import jax.numpy as jnp
from jax import lax

D = 384
HEAD_DIM = 64
FF = 1536
CLASSES = 1001
TOK = 256
LAYERS = 2
SLOTS = 1
LATENTS = 32


def draw_counts(key, part):
    base_key = jax.random.fold_in(key, 11)
    key_one, key_two, key_three = jax.random.split(base_key, 3)
    devices = LATENTS // SLOTS
    drawn_counts = jax.random.randint(key_one, (devices,), SLOTS - 1, SLOTS + 1)
    upper_at = jax.random.randint(key_two, (), 0, devices)
    lower_at = (upper_at + 1 + jax.random.randint(key_three, (), 0, devices - 1)) % devices
    drawn_counts = drawn_counts.at[upper_at].set(SLOTS).at[lower_at].set(SLOTS - 1)
    return drawn_counts.astype(jnp.int32)


def place_ends(entries, own_key, low, top_value):
    shape = entries.shape
    spot = [jax.random.randint(jax.random.fold_in(own_key, axis), (), 0, shape[axis]) for axis in range(len(shape))]
    entries = entries.at[tuple(spot)].set(low)
    longest = shape.index(max(shape))
    spot[longest] = (spot[longest] + 1) % shape[longest]
    return entries.at[tuple(spot)].set(top_value)


def level_of(rng, shape, cuts, least, largest):
    gain = 1.0
    for position, blocks in cuts:
        steps = jax.random.uniform(jax.random.fold_in(jax.random.fold_in(rng, 6), position), (blocks,), jnp.float32, least / len(cuts), largest / len(cuts))
        gain = gain * jnp.repeat(jnp.exp(steps), shape[position] // blocks).reshape((-1,) + (1,) * (len(shape) - 1 - position))
    return gain


def normal_values(stream_key, extent, width, bound, pieces=(), kind=jnp.bfloat16):
    level = level_of(stream_key, extent, pieces, -0.22, 0.18) if pieces else 1.0
    entries = jax.random.normal(stream_key, extent, jnp.float32) * width * level
    return jnp.minimum(jnp.maximum(entries, -bound), bound).astype(kind)


def setup_inputs(seed: int = 0) -> dict:
    arg_keys = jax.random.split(jax.random.key(seed), 17)
    latents = normal_values(arg_keys[0], (LATENTS, TOK, D), 1.0, 6.0, ((0, 32),))
    timestep_embed = normal_values(arg_keys[1], (LATENTS, D), 0.5, 3.0, ((0, 32),), jnp.float32)
    labels = place_ends(jax.random.randint(arg_keys[2], (LATENTS,), 0, CLASSES), jax.random.fold_in(arg_keys[2], 1), 0, CLASSES - 1).astype(jnp.int32)
    counts = draw_counts(jax.random.fold_in(arg_keys[16], 71), 0)
    class_table = normal_values(arg_keys[4], (CLASSES, D), 0.5, 3.0, ((1, 2),))
    ada_weight = normal_values(arg_keys[5], (LAYERS, D, 6 * D), D ** -0.5, 0.3125, ((1, 2),))
    ada_bias = normal_values(arg_keys[6], (LAYERS, 6 * D), 0.3, 2.0, ((1, 2),))
    qkv_weight = normal_values(arg_keys[7], (LAYERS, D, 3 * D), D ** -0.5, 0.3125, ((1, 2),))
    qv_bias = normal_values(arg_keys[8], (LAYERS, 2 * D), 0.5, 3.0, ((1, 2),))
    out_weight = normal_values(arg_keys[9], (LAYERS, D, D), (D // 4) ** -0.5, 0.625, ((1, 2),))
    out_bias = normal_values(arg_keys[10], (LAYERS, D), 0.5, 3.0, ((1, 2),))
    up_weight = normal_values(arg_keys[11], (LAYERS, D, FF), D ** -0.5, 0.3125, ((1, 2),))
    up_bias = normal_values(arg_keys[12], (LAYERS, FF), 0.5, 3.0, ((1, 2),))
    down_weight = normal_values(arg_keys[13], (LAYERS, FF, D), FF ** -0.5, 0.15625, ((1, 2),))
    down_bias = normal_values(arg_keys[14], (LAYERS, D), 0.5, 3.0, ((1, 2),))
    cotangent = normal_values(arg_keys[15], (LATENTS, TOK, D), 1.0, 6.0, ((0, 32),))
    return dict(latents=latents, timestep_embed=timestep_embed, labels=labels, counts=counts, class_table=class_table, ada_weight=ada_weight, ada_bias=ada_bias, qkv_weight=qkv_weight, qv_bias=qv_bias, out_weight=out_weight, out_bias=out_bias, up_weight=up_weight, up_bias=up_bias, down_weight=down_weight, down_bias=down_bias, cotangent=cotangent)


norm_eps = 1e-06
gelu_coeff = math.sqrt(2.0 / math.pi)
gelu_cubic = 0.044715

def batched(formula, operand_a, operand_b):
    return jnp.einsum(formula, operand_a.astype(jnp.float32), operand_b.astype(jnp.float32))

def norm_rows(values):
    centered = values - lax.optimization_barrier(jnp.mean(values, axis=-1, keepdims=True))
    inv_dev = lax.rsqrt(lax.optimization_barrier(jnp.mean(centered * centered, axis=-1, keepdims=True)) + norm_eps)
    return (centered * inv_dev, inv_dev)

def norm_back(grad_normed, normed, inv_dev):
    return (grad_normed - lax.optimization_barrier(jnp.mean(grad_normed, axis=-1, keepdims=True)) - normed * lax.optimization_barrier(jnp.mean(grad_normed * normed, axis=-1, keepdims=True))) * inv_dev

def gelu_parts(pre_act):
    inner_arg = gelu_coeff * (pre_act + gelu_cubic * pre_act * pre_act * pre_act)
    tanh_val = jnp.tanh(inner_arg)
    value_out = 0.5 * pre_act * (1.0 + tanh_val)
    slope_out = 0.5 * (1.0 + tanh_val) + 0.5 * pre_act * (1.0 - tanh_val * tanh_val) * gelu_coeff * (1.0 + 3.0 * gelu_cubic * pre_act * pre_act)
    return (value_out, slope_out)

def layer_forward(stream, cond_act, layer_weights):
    w_ada, b_ada, w_qkv, b_qv, w_out, b_out, w_up, b_up, w_down, b_down = layer_weights
    slot_count, token_count, model_width = stream.shape
    head_count = model_width // HEAD_DIM
    row_count = slot_count * token_count
    shape_heads = (slot_count, token_count, head_count, HEAD_DIM)
    modul = jnp.dot(cond_act, w_ada, preferred_element_type=jnp.float32) + b_ada.astype(jnp.float32)
    shifts = tuple((modul[:, None, member * model_width:(member + 1) * model_width] for member in range(6)))
    normed, inv_one = norm_rows(stream)
    modulated = (normed * (1.0 + shifts[1]) + shifts[0]).astype(jnp.bfloat16).reshape(row_count, model_width)
    projected = jnp.dot(modulated, w_qkv, preferred_element_type=jnp.float32)
    bias_full = b_qv.astype(jnp.float32)
    query_heads = (projected[:, :model_width] + bias_full[:model_width]).astype(jnp.bfloat16).reshape(shape_heads)
    key_heads = projected[:, model_width:2 * model_width].astype(jnp.bfloat16).reshape(shape_heads)
    value_heads = (projected[:, 2 * model_width:] + bias_full[model_width:]).astype(jnp.bfloat16).reshape(shape_heads)
    scores = batched('sqhe,skhe->shqk', query_heads, key_heads) * HEAD_DIM ** (-0.5)
    row_top = lax.optimization_barrier(jnp.max(scores, axis=-1, keepdims=True))
    log_total = row_top + jnp.log(lax.optimization_barrier(jnp.sum(jnp.exp(scores - row_top), axis=-1, keepdims=True)))
    prob_bf = jnp.exp(scores - log_total).astype(jnp.bfloat16)
    attended = batched('shqk,skhe->sqhe', prob_bf, value_heads).astype(jnp.bfloat16).reshape(row_count, model_width)
    branch_attn = (jnp.dot(attended, w_out, preferred_element_type=jnp.float32) + b_out.astype(jnp.float32)).reshape(stream.shape)
    middle = stream + shifts[2] * branch_attn
    normed_two, inv_two = norm_rows(middle)
    mod_two = (normed_two * (1.0 + shifts[4]) + shifts[3]).astype(jnp.bfloat16).reshape(row_count, model_width)
    pre_act = jnp.dot(mod_two, w_up, preferred_element_type=jnp.float32) + b_up.astype(jnp.float32)
    act_value, act_slope = gelu_parts(pre_act)
    act_bf = act_value.astype(jnp.bfloat16)
    branch_mlp = (jnp.dot(act_bf, w_down, preferred_element_type=jnp.float32) + b_down.astype(jnp.float32)).reshape(stream.shape)
    output = middle + shifts[5] * branch_mlp
    kept_values = (shifts, normed, inv_one, modulated, query_heads, key_heads, value_heads, log_total, attended, branch_attn, normed_two, inv_two, mod_two, act_slope, act_bf, branch_mlp)
    return (output, kept_values)

def layer_backward(grad_out, cond_act, layer_weights, kept_values):
    w_ada, b_ada, w_qkv, b_qv, w_out, b_out, w_up, b_up, w_down, b_down = layer_weights
    shifts, normed, inv_one, modulated, query_heads, key_heads, value_heads, log_total, attended, branch_attn, normed_two, inv_two, mod_two, act_slope, act_bf, branch_mlp = kept_values
    slot_count, token_count, model_width = grad_out.shape
    row_count = slot_count * token_count
    grad_gate_mlp = lax.optimization_barrier(jnp.sum(grad_out * branch_mlp, axis=1))
    grad_branch = (grad_out * shifts[5]).reshape(row_count, model_width)
    branch_bf = grad_branch.astype(jnp.bfloat16)
    grad_w_down = jnp.dot(act_bf.T, branch_bf, preferred_element_type=jnp.float32)
    grad_b_down = lax.optimization_barrier(jnp.sum(grad_branch, axis=0))
    grad_pre = jnp.dot(branch_bf, w_down.T, preferred_element_type=jnp.float32) * act_slope
    pre_bf = grad_pre.astype(jnp.bfloat16)
    grad_w_up = jnp.dot(mod_two.T, pre_bf, preferred_element_type=jnp.float32)
    grad_b_up = lax.optimization_barrier(jnp.sum(grad_pre, axis=0))
    grad_mod_two = jnp.dot(pre_bf, w_up.T, preferred_element_type=jnp.float32).reshape(grad_out.shape)
    grad_shift_mlp = lax.optimization_barrier(jnp.sum(grad_mod_two, axis=1))
    grad_scale_mlp = lax.optimization_barrier(jnp.sum(grad_mod_two * normed_two, axis=1))
    grad_middle = grad_out + norm_back(grad_mod_two * (1.0 + shifts[4]), normed_two, inv_two)
    grad_gate_attn = lax.optimization_barrier(jnp.sum(grad_middle * branch_attn, axis=1))
    grad_battn = (grad_middle * shifts[2]).reshape(row_count, model_width)
    battn_bf = grad_battn.astype(jnp.bfloat16)
    grad_w_out = jnp.dot(attended.T, battn_bf, preferred_element_type=jnp.float32)
    grad_b_out = lax.optimization_barrier(jnp.sum(grad_battn, axis=0))
    grad_att = jnp.dot(battn_bf, w_out.T, preferred_element_type=jnp.float32).astype(jnp.bfloat16).reshape(query_heads.shape)
    scores = batched('sqhe,skhe->shqk', query_heads, key_heads) * HEAD_DIM ** (-0.5)
    prob_full = jnp.exp(scores - log_total)
    prob_bf = prob_full.astype(jnp.bfloat16)
    grad_prob = batched('sqhe,skhe->shqk', grad_att, value_heads)
    grad_values = batched('shqk,sqhe->skhe', prob_bf, grad_att).reshape(row_count, model_width)
    row_dot = lax.optimization_barrier(jnp.sum(prob_full * grad_prob, axis=-1, keepdims=True))
    grad_scores = (prob_full * (grad_prob - row_dot) * HEAD_DIM ** (-0.5)).astype(jnp.bfloat16)
    grad_queries = batched('shqk,skhe->sqhe', grad_scores, key_heads).reshape(row_count, model_width)
    grad_keys = batched('shqk,sqhe->skhe', grad_scores, query_heads).reshape(row_count, model_width)
    grad_proj = jnp.concatenate([grad_queries, grad_keys, grad_values], axis=1)
    proj_bf = grad_proj.astype(jnp.bfloat16)
    grad_b_qv = jnp.concatenate([lax.optimization_barrier(jnp.sum(grad_queries, axis=0)), lax.optimization_barrier(jnp.sum(grad_values, axis=0))])
    grad_w_qkv = jnp.dot(modulated.T, proj_bf, preferred_element_type=jnp.float32)
    grad_modul = jnp.dot(proj_bf, w_qkv.T, preferred_element_type=jnp.float32).reshape(grad_out.shape)
    grad_shift_attn = lax.optimization_barrier(jnp.sum(grad_modul, axis=1))
    grad_scale_attn = lax.optimization_barrier(jnp.sum(grad_modul * normed, axis=1))
    grad_stream = grad_middle + norm_back(grad_modul * (1.0 + shifts[1]), normed, inv_one)
    grad_vector = jnp.concatenate([grad_shift_attn, grad_scale_attn, grad_gate_attn, grad_shift_mlp, grad_scale_mlp, grad_gate_mlp], axis=1)
    vector_bf = grad_vector.astype(jnp.bfloat16)
    grad_w_ada = jnp.dot(cond_act.T, vector_bf, preferred_element_type=jnp.float32)
    grad_b_ada = lax.optimization_barrier(jnp.sum(grad_vector, axis=0))
    grad_cond = jnp.dot(vector_bf, w_ada.T, preferred_element_type=jnp.float32)
    return (grad_stream, grad_cond, (grad_w_ada, grad_b_ada, grad_w_qkv, grad_b_qv, grad_w_out, grad_b_out, grad_w_up, grad_b_up, grad_w_down, grad_b_down))

def device_pass(lat_block, temb_block, label_block, live_count, cot_block, table, stacks):
    slot_count = lat_block.shape[0]
    live_mask = (jnp.arange(slot_count) < live_count).astype(jnp.float32)
    one_hot = (label_block[:, None] == jnp.arange(table.shape[0])[None, :]).astype(jnp.bfloat16)
    condition = temb_block + jnp.dot(one_hot, table, preferred_element_type=jnp.float32)
    cond_sigmoid = jax.nn.sigmoid(condition)
    cond_act = (condition * cond_sigmoid).astype(jnp.bfloat16)
    stream = lat_block.astype(jnp.float32)
    kept_layers = []
    for layer_index in range(LAYERS):
        stream, kept_values = layer_forward(stream, cond_act, tuple((member[layer_index] for member in stacks)))
        kept_layers.append(kept_values)
    activations = (stream * live_mask[:, None, None]).astype(jnp.bfloat16)
    grad_stream = cot_block.astype(jnp.float32) * live_mask[:, None, None]
    grad_cond_total = jnp.zeros(condition.shape, jnp.float32)
    grads_by_layer = [None] * LAYERS
    for layer_index in reversed(range(LAYERS)):
        grad_stream, grad_cond, layer_grads = layer_backward(grad_stream, cond_act, tuple((member[layer_index] for member in stacks)), kept_layers[layer_index])
        grad_cond_total = grad_cond_total + grad_cond
        grads_by_layer[layer_index] = layer_grads
    cond_grad = grad_cond_total * cond_sigmoid * (1.0 + condition * (1.0 - cond_sigmoid))
    table_term = jnp.dot(one_hot.astype(jnp.float32).T, cond_grad, precision=lax.Precision.HIGHEST)
    stacked = tuple((jnp.stack([grads_by_layer[layer_index][member] for layer_index in range(LAYERS)]) for member in range(10)))
    return ((activations, grad_stream, cond_grad), (table_term,) + stacked)

def reference(latents, timestep_embed, labels, counts, class_table, ada_weight, ada_bias, qkv_weight, qv_bias, out_weight, out_bias, up_weight, up_bias, down_weight, down_bias, cotangent):
    stacks = (ada_weight, ada_bias, qkv_weight, qv_bias, out_weight, out_bias, up_weight, up_bias, down_weight, down_bias)
    devices = counts.shape[0]
    slot_count = latents.shape[0] // devices
    per_lat = latents.reshape(devices, slot_count, TOK, D)
    per_temb = timestep_embed.reshape(devices, slot_count, D)
    per_label = labels.reshape(devices, slot_count)
    per_cot = cotangent.reshape(devices, slot_count, TOK, D)
    running_init = (jnp.zeros(class_table.shape, jnp.float32),) + tuple((jnp.zeros(member.shape, jnp.float32) for member in stacks))

    def per_device(running, inputs):
        lat_block, temb_block, label_block, live_count, cot_block = inputs
        outputs, grad_terms = device_pass(lat_block, temb_block, label_block, live_count, cot_block, class_table, stacks)
        running = tuple((total + term for total, term in zip(running, grad_terms)))
        return (running, outputs)
    running, outputs = lax.scan(per_device, running_init, (per_lat, per_temb, per_label, counts, per_cot))
    activations = outputs[0].reshape(latents.shape)
    latents_grad = outputs[1].reshape(latents.shape)
    cond_grad = outputs[2].reshape(timestep_embed.shape)
    return (activations, latents_grad, cond_grad, running[0], running[1], running[2], running[3], running[4], running[5], running[6], running[7], running[8], running[9], running[10])
```

```python
import functools
import math

import jax
import jax.numpy as jnp
from jax import lax
from jax.experimental import pallas as pl
from jax.experimental.pallas import tpu as pltpu
from jax.sharding import PartitionSpec as P

D = 384
HEAD_DIM = 64
LAYERS = 2
F32 = jnp.float32
BF16 = jnp.bfloat16

norm_eps = 1e-06
gelu_coeff = math.sqrt(2.0 / math.pi)
gelu_cubic = 0.044715

VMEM = pl.BlockSpec(memory_space=pltpu.VMEM)
SMEM = pl.BlockSpec(memory_space=pltpu.SMEM)
HBM = pl.BlockSpec(memory_space=pl.ANY)
LIMIT = 48 * 1024 * 1024


def sds(shape, dtype):
    return jax.ShapeDtypeStruct(shape, dtype)


def norm_rows(values):
    centered = values - jnp.mean(values, axis=-1, keepdims=True)
    inv_dev = lax.rsqrt(jnp.mean(centered * centered, axis=-1, keepdims=True) + norm_eps)
    return (centered * inv_dev, inv_dev)


def norm_back(grad_normed, normed, inv_dev):
    return (
        grad_normed
        - jnp.mean(grad_normed, axis=-1, keepdims=True)
        - normed * jnp.mean(grad_normed * normed, axis=-1, keepdims=True)
    ) * inv_dev


def gelu_parts(pre_act):
    square = pre_act * pre_act
    inner_arg = gelu_coeff * pre_act * (1.0 + gelu_cubic * square)
    tanh_val = jnp.tanh(inner_arg)
    half_up = 0.5 * (1.0 + tanh_val)
    value_out = pre_act * half_up
    slope_out = half_up + 0.5 * pre_act * (1.0 - tanh_val * tanh_val) * (
        gelu_coeff + (3.0 * gelu_cubic * gelu_coeff) * square
    )
    return (value_out, slope_out)


def dot(a, b):
    return jnp.dot(a, b, preferred_element_type=F32)


def dot_nt(a, b):
    return lax.dot_general(a, b, (((1,), (1,)), ((), ())), preferred_element_type=F32)


def dot_tn(a, b):
    return lax.dot_general(a, b, (((0,), (0,)), ((), ())), preferred_element_type=F32)


def head_masks():
    lane = lax.broadcasted_iota(jnp.int32, (1, 2 * HEAD_DIM), 1)
    first = lane < HEAD_DIM
    return first, jnp.logical_not(first)


def keep_lanes(values, mask):
    return jnp.where(mask, values, jnp.zeros_like(values))


def rows_of(start, size):
    return pl.ds(pl.multiple_of(start, 16), size)


def attn_weight_copies(meta, layer, qkv_hbm, out_hbm, pieces, offsets, w_qkv, w_out, sems):
    half = qkv_hbm.shape[1]
    x = meta[0]
    copies = [
        (qkv_hbm.at[layer], w_qkv.at[rows_of(x * half, half), :]),
        (out_hbm.at[layer], w_out.at[rows_of(x * half, half), :]),
    ]
    for piece, offset in zip(pieces, offsets):
        size = piece.shape[0]
        start = (1 - x) * half + offset * size
        copies.append((piece.at[:, pl.ds(0, 3 * D)], w_qkv.at[rows_of(start, size), :]))
        copies.append((piece.at[:, pl.ds(3 * D, D)], w_out.at[rows_of(start, size), :]))
    return [pltpu.make_async_copy(s, d, sems.at[i]) for i, (s, d) in enumerate(copies)]


def mlp_weight_copies(meta, layer, up_hbm, down_hbm, pieces, offsets, w_up, w_down, sems):
    half = up_hbm.shape[1]
    tall = down_hbm.shape[1]
    blocks = tall // half
    x = meta[0]
    copies = [
        (up_hbm.at[layer], w_up.at[rows_of(x * half, half), :]),
        (down_hbm.at[layer], w_down.at[rows_of(x * tall, tall), :]),
    ]
    for piece, offset in zip(pieces, offsets):
        size = piece.shape[0] // 2
        start = (1 - x) * half + offset * size
        copies.append((piece.at[pl.ds(0, size), :], w_up.at[rows_of(start, size), :]))
        for b in range(blocks):
            start = (1 - x) * tall + offset * (blocks * size) + b * size
            copies.append(
                (
                    piece.at[pl.ds(size, size), pl.ds(b * D, D)],
                    w_down.at[rows_of(start, size), :],
                )
            )
    return [pltpu.make_async_copy(s, d, sems.at[i]) for i, (s, d) in enumerate(copies)]


def piece_offsets(meta, count, far):
    core, y, z = meta[1], meta[2], meta[3]
    if count == 2:
        return [core, 1 - core]
    near = z % 2 if far else y
    return [
        near * 2 + core,
        (1 - near) * 2 + core,
        near * 2 + (1 - core),
        (1 - near) * 2 + (1 - core),
    ]


def pack_attn_kernel(layer, far, parts, meta, qkv, out, send, sems):
    size = qkv.shape[1] // parts
    offset = piece_offsets(meta, parts, far)[0]
    rows = rows_of(offset * size, size)
    copies = [
        pltpu.make_async_copy(qkv.at[layer, rows, :], send.at[:, pl.ds(0, 3 * D)], sems.at[0]),
        pltpu.make_async_copy(out.at[layer, rows, :], send.at[:, pl.ds(3 * D, D)], sems.at[1]),
    ]
    for copy in copies:
        copy.start()
    for copy in copies:
        copy.wait()


def pack_attn(layer, far, parts, meta, qkv, out):
    size = qkv.shape[1] // parts
    return pl.pallas_call(
        functools.partial(pack_attn_kernel, layer, far, parts),
        out_shape=sds((size, 4 * D), BF16),
        in_specs=[SMEM, HBM, HBM],
        out_specs=HBM,
        scratch_shapes=[pltpu.SemaphoreType.DMA((2,))],
        name="pack_attn",
    )(meta, qkv, out)


def pack_mlp_kernel(layer, far, parts, meta, up, down, send, sems):
    size = up.shape[1] // parts
    blocks = down.shape[1] // up.shape[1]
    offset = piece_offsets(meta, parts, far)[0]
    copies = [
        pltpu.make_async_copy(
            up.at[layer, rows_of(offset * size, size), :], send.at[pl.ds(0, size), :], sems.at[0]
        )
    ]
    for b in range(blocks):
        rows = rows_of(offset * (blocks * size) + b * size, size)
        copies.append(
            pltpu.make_async_copy(
                down.at[layer, rows, :],
                send.at[pl.ds(size, size), pl.ds(b * D, D)],
                sems.at[1 + b],
            )
        )
    for copy in copies:
        copy.start()
    for copy in copies:
        copy.wait()


def pack_mlp(layer, far, parts, meta, up, down):
    size = up.shape[1] // parts
    return pl.pallas_call(
        functools.partial(pack_mlp_kernel, layer, far, parts),
        out_shape=sds((2 * size, 4 * D), BF16),
        in_specs=[SMEM, HBM, HBM],
        out_specs=HBM,
        scratch_shapes=[pltpu.SemaphoreType.DMA((8,))],
        name="pack_mlp",
    )(meta, up, down)


def attn_fwd_kernel(layer, far, count, *refs):
    meta, x_ref, vecs, qkv_hbm, out_hbm = refs[:5]
    pieces = refs[5 : 5 + count]
    modulated_out, qkv_out, prob_out, att_out, branch_out, middle_out = refs[5 + count : 11 + count]
    w_qkv, w_out, sems = refs[11 + count :]
    copies = attn_weight_copies(
        meta, layer, qkv_hbm, out_hbm, pieces, piece_offsets(meta, count, far), w_qkv, w_out, sems
    )
    for copy in copies:
        copy.start()
    stream = x_ref[...].astype(F32)
    normed, _ = norm_rows(stream)
    modulated = (normed * (1.0 + vecs[1:2, :]) + vecs[0:1, :]).astype(BF16)
    modulated_out[...] = modulated
    for copy in copies:
        copy.wait()
    for part in range(3):
        cols = slice(part * D, (part + 1) * D)
        value = dot(modulated, w_qkv[:, cols])
        if part == 0:
            value = value + vecs[6:7, :]
        if part == 2:
            value = value + vecs[7:8, :]
        qkv_out[:, cols] = value.astype(BF16)
    masks = head_masks()
    tokens = stream.shape[0]
    for pair in range(D // (2 * HEAD_DIM)):
        lanes = slice(pair * 2 * HEAD_DIM, (pair + 1) * 2 * HEAD_DIM)
        query = qkv_out[:, lanes]
        key = qkv_out[:, pair * 128 + D : (pair + 1) * 128 + D]
        value = qkv_out[:, pair * 128 + 2 * D : (pair + 1) * 128 + 2 * D]
        attended = None
        for member in range(2):
            head = 2 * pair + member
            scores = dot_nt(query, keep_lanes(key, masks[member])) * HEAD_DIM ** (-0.5)
            top = jnp.max(scores, axis=-1, keepdims=True)
            expo = jnp.exp(scores - top)
            prob = (expo * (1.0 / jnp.sum(expo, axis=-1, keepdims=True))).astype(BF16)
            prob_out[head * tokens : (head + 1) * tokens, :] = prob
            part = dot(prob, keep_lanes(value, masks[member]))
            attended = part if attended is None else attended + part
        att_out[:, lanes] = attended.astype(BF16)
    branch = dot(att_out[...], w_out[...]) + vecs[8:9, :]
    branch_out[...] = branch
    middle_out[...] = stream + vecs[2:3, :] * branch


def attn_fwd(layer, far, meta, x, vecs, qkv, out, pieces):
    tokens = x.shape[0]
    count = len(pieces)
    heads = D // HEAD_DIM
    return pl.pallas_call(
        functools.partial(attn_fwd_kernel, layer, far, count),
        out_shape=(
            sds((tokens, D), BF16),
            sds((tokens, 3 * D), BF16),
            sds((heads * tokens, tokens), BF16),
            sds((tokens, D), BF16),
            sds((tokens, D), F32),
            sds((tokens, D), F32),
        ),
        in_specs=[SMEM, VMEM, VMEM] + [HBM] * (2 + count),
        out_specs=(VMEM,) * 6,
        scratch_shapes=[
            pltpu.VMEM((D, 3 * D), BF16),
            pltpu.VMEM((D, D), BF16),
            pltpu.SemaphoreType.DMA((2 + 2 * count,)),
        ],
        compiler_params=pltpu.CompilerParams(vmem_limit_bytes=LIMIT),
        cost_estimate=pl.CostEstimate(flops=6 * 10**8, bytes_accessed=8 * 10**6, transcendentals=4 * 10**5),
        name="attn_fwd",
    )(meta, x, vecs, qkv, out, *pieces)


def mlp_fwd_kernel(layer, far, count, last, *refs):
    meta, middle_ref, vecs, up_hbm, down_hbm = refs[:5]
    pieces = refs[5 : 5 + count]
    x_out, mod_out, act_out, slope_out, branch_out = refs[5 + count : 10 + count]
    w_up, w_down, sems = refs[10 + count :]
    copies = mlp_weight_copies(
        meta, layer, up_hbm, down_hbm, pieces, piece_offsets(meta, count, far), w_up, w_down, sems
    )
    for copy in copies:
        copy.start()
    middle = middle_ref[...]
    normed, _ = norm_rows(middle)
    mod_two = (normed * (1.0 + vecs[4:5, :]) + vecs[3:4, :]).astype(BF16)
    mod_out[...] = mod_two
    for copy in copies:
        copy.wait()
    branch = None
    for part in range(4):
        cols = slice(part * D, (part + 1) * D)
        pre_act = dot(mod_two, w_up[:, cols]) + vecs[10 + part : 11 + part, :]
        value, slope = gelu_parts(pre_act)
        value = value.astype(BF16)
        act_out[:, cols] = value
        slope_out[:, cols] = slope.astype(BF16)
        term = dot(value, w_down[cols, :])
        branch = term if branch is None else branch + term
    branch = branch + vecs[9:10, :]
    branch_out[...] = branch
    result = middle + vecs[5:6, :] * branch
    if last:
        live = meta[4].astype(F32)
        result = result * live
    x_out[...] = result.astype(x_out.dtype)


def mlp_fwd(layer, far, last, meta, middle, vecs, up, down, pieces):
    tokens = middle.shape[0]
    count = len(pieces)
    return pl.pallas_call(
        functools.partial(mlp_fwd_kernel, layer, far, count, last),
        out_shape=(
            sds((tokens, D), BF16 if last else F32),
            sds((tokens, D), BF16),
            sds((tokens, 4 * D), BF16),
            sds((tokens, 4 * D), BF16),
            sds((tokens, D), F32),
        ),
        in_specs=[SMEM, VMEM, VMEM] + [HBM] * (2 + count),
        out_specs=(VMEM,) * 5,
        scratch_shapes=[
            pltpu.VMEM((D, 4 * D), BF16),
            pltpu.VMEM((4 * D, D), BF16),
            pltpu.SemaphoreType.DMA((2 + 5 * count,)),
        ],
        compiler_params=pltpu.CompilerParams(vmem_limit_bytes=LIMIT),
        cost_estimate=pl.CostEstimate(flops=6 * 10**8, bytes_accessed=8 * 10**6, transcendentals=4 * 10**5),
        name="mlp_fwd",
    )(meta, middle, vecs, up, down, *pieces)


def split_store(core, value, half, keep, send, rows):
    @pl.when(core == half)
    def _():
        keep[rows, :] = value

    @pl.when(core != half)
    def _():
        send[rows, :] = value


def mlp_bwd_kernel(layer, far, count, masked, extra, *refs):
    meta, grad_ref, vecs, middle_ref, branch_ref, act_ref, slope_ref, mod_ref = refs[:8]
    refs = refs[8:]
    if extra:
        ride, refs = refs[0], refs[1:]
    up_hbm, down_hbm = refs[:2]
    pieces = refs[2 : 2 + count]
    keep, send, grad_out, sums_out = refs[2 + count : 6 + count]
    w_up, w_down, pre_bf, sems = refs[6 + count :]
    copies = mlp_weight_copies(
        meta, layer, up_hbm, down_hbm, pieces, piece_offsets(meta, count, far), w_up, w_down, sems
    )
    for copy in copies:
        copy.start()
    core = meta[1]
    grad = grad_ref[...].astype(F32)
    if masked:
        grad = grad * meta[4].astype(F32)
    sums_out[...] = jnp.zeros_like(sums_out)
    sums_out[5:6, :] = jnp.sum(grad * branch_ref[...], axis=0, keepdims=True)
    grad_branch = grad * vecs[5:6, :]
    sums_out[9:10, :] = jnp.sum(grad_branch, axis=0, keepdims=True)
    branch_bf = grad_branch.astype(BF16)
    half = D // 2
    for part in range(4):
        value = dot_tn(act_ref[:, part * D : (part + 1) * D], branch_bf).astype(BF16)
        base = (part // 2) * 4 * half + 2 * half
        split_store(core, value, part % 2, keep, send, slice(base, base + D))
    for copy in copies:
        copy.wait()
    mod_two = mod_ref[...]
    grad_mod = None
    for part in range(4):
        cols = slice(part * D, (part + 1) * D)
        grad_pre = dot_nt(branch_bf, w_down[cols, :]) * slope_ref[:, cols].astype(F32)
        sums_out[10 + part : 11 + part, :] = jnp.sum(grad_pre, axis=0, keepdims=True)
        pre = grad_pre.astype(BF16)
        value = dot_tn(mod_two, pre).astype(BF16)
        for side in range(2):
            base = side * 4 * half + (part % 2) * half
            split_store(
                core,
                value[side * half : (side + 1) * half, :],
                part // 2,
                keep,
                send,
                slice(base, base + half),
            )
        term = dot_nt(pre, w_up[:, cols])
        grad_mod = term if grad_mod is None else grad_mod + term
    normed, inv_dev = norm_rows(middle_ref[...])
    sums_out[3:4, :] = jnp.sum(grad_mod, axis=0, keepdims=True)
    sums_out[4:5, :] = jnp.sum(grad_mod * normed, axis=0, keepdims=True)
    grad_out[...] = grad + norm_back(grad_mod * (1.0 + vecs[4:5, :]), normed, inv_dev)
    if extra:
        send[8 * half : 8 * half + 16, :] = ride[...]


def mlp_bwd(layer, far, masked, meta, grad, vecs, kept, up, down, pieces, ride=None):
    middle, mod_two, act, slope, branch = kept
    tokens = middle.shape[0]
    count = len(pieces)
    extra = 0 if ride is None else ride.shape[0]
    rides = () if ride is None else (ride,)
    return pl.pallas_call(
        functools.partial(mlp_bwd_kernel, layer, far, count, masked, extra),
        out_shape=(
            sds((4 * D, D), BF16),
            sds((4 * D + extra, D), BF16),
            sds((tokens, D), F32),
            sds((16, D), F32),
        ),
        in_specs=[SMEM] + [VMEM] * (7 + len(rides)) + [HBM] * (2 + count),
        out_specs=(VMEM,) * 4,
        scratch_shapes=[
            pltpu.VMEM((D, 4 * D), BF16),
            pltpu.VMEM((4 * D, D), BF16),
            pltpu.VMEM((16, D), BF16),
            pltpu.SemaphoreType.DMA((2 + 5 * count,)),
        ],
        compiler_params=pltpu.CompilerParams(vmem_limit_bytes=LIMIT),
        cost_estimate=pl.CostEstimate(flops=12 * 10**8, bytes_accessed=14 * 10**6, transcendentals=10**4),
        name="mlp_bwd",
    )(meta, grad, vecs, middle, branch, act, slope, mod_two, *rides, up, down, *pieces)


def attn_bwd_kernel(layer, far, count, extra, *refs):
    meta, grad_ref, vecs, x_ref, modulated_ref, qkv_ref, prob_ref, att_ref, branch_ref, part_sums = refs[:10]
    qkv_hbm, out_hbm = refs[10:12]
    pieces = refs[12 : 12 + count]
    keep, send, grad_out, sums_out = refs[12 + count : 16 + count]
    w_qkv, w_out, ga_ref, proj_ref, sems = refs[16 + count :]
    copies = attn_weight_copies(
        meta, layer, qkv_hbm, out_hbm, pieces, piece_offsets(meta, count, far), w_qkv, w_out, sems
    )
    for copy in copies:
        copy.start()
    core = meta[1]
    half = D // 2
    tokens = grad_ref.shape[0]
    sums = {}
    grad = grad_ref[...]
    sums[2] = jnp.sum(grad * branch_ref[...], axis=0, keepdims=True)
    grad_battn = grad * vecs[2:3, :]
    sums[8] = jnp.sum(grad_battn, axis=0, keepdims=True)
    battn_bf = grad_battn.astype(BF16)

    def store(value, block):
        for side in range(2):
            base = side * 2 * half + (block % 2) * half
            split_store(
                core,
                value[side * half : (side + 1) * half, :],
                block // 2,
                keep,
                send,
                slice(base, base + half),
            )

    store(dot_tn(att_ref[...], battn_bf).astype(BF16), 3)
    for copy in copies:
        copy.wait()
    ga_ref[...] = dot_nt(battn_bf, w_out[...]).astype(BF16)
    masks = head_masks()
    grad_q_sums, grad_v_sums = [], []
    for pair in range(D // (2 * HEAD_DIM)):
        lanes = slice(pair * 128, (pair + 1) * 128)
        query = qkv_ref[:, lanes]
        key = qkv_ref[:, pair * 128 + D : (pair + 1) * 128 + D]
        value = qkv_ref[:, pair * 128 + 2 * D : (pair + 1) * 128 + 2 * D]
        grad_att = ga_ref[:, lanes]
        grad_q = grad_k = grad_v = None
        for member in range(2):
            head = 2 * pair + member
            mask = masks[member]
            prob_bf = prob_ref[head * tokens : (head + 1) * tokens, :]
            prob = prob_bf.astype(F32)
            grad_prob = dot_nt(grad_att, keep_lanes(value, mask))
            term_v = dot_tn(prob_bf, keep_lanes(grad_att, mask))
            weighted = prob * grad_prob
            row_dot = jnp.sum(weighted, axis=-1, keepdims=True)
            grad_scores = ((weighted - prob * row_dot) * HEAD_DIM ** (-0.5)).astype(BF16)
            term_q = dot(grad_scores, keep_lanes(key, mask))
            term_k = dot_tn(grad_scores, keep_lanes(query, mask))
            grad_q = term_q if grad_q is None else grad_q + term_q
            grad_k = term_k if grad_k is None else grad_k + term_k
            grad_v = term_v if grad_v is None else grad_v + term_v
        grad_q_sums.append(jnp.sum(grad_q, axis=0, keepdims=True))
        grad_v_sums.append(jnp.sum(grad_v, axis=0, keepdims=True))
        proj_ref[:, lanes] = grad_q.astype(BF16)
        proj_ref[:, pair * 128 + D : (pair + 1) * 128 + D] = grad_k.astype(BF16)
        proj_ref[:, pair * 128 + 2 * D : (pair + 1) * 128 + 2 * D] = grad_v.astype(BF16)
    sums[6] = jnp.concatenate(grad_q_sums, axis=1)
    sums[7] = jnp.concatenate(grad_v_sums, axis=1)
    modulated = modulated_ref[...]
    for block in range(3):
        store(dot_tn(modulated, proj_ref[:, block * D : (block + 1) * D]).astype(BF16), block)
    grad_mod = dot_nt(proj_ref[...], w_qkv[...])
    normed, inv_dev = norm_rows(x_ref[...].astype(F32))
    sums[0] = jnp.sum(grad_mod, axis=0, keepdims=True)
    sums[1] = jnp.sum(grad_mod * normed, axis=0, keepdims=True)
    grad_out[...] = grad + norm_back(grad_mod * (1.0 + vecs[1:2, :]), normed, inv_dev)
    row = lax.broadcasted_iota(jnp.int32, (16, 1), 0)
    total = part_sums[...]
    for index, value in sums.items():
        total = jnp.where(row == index, value, total)
    total = total.astype(BF16)
    sums_out[...] = total
    if extra:
        send[4 * half : 4 * half + 16, :] = total


def attn_bwd(layer, far, extra, meta, grad, vecs, x, kept, part_sums, qkv, out, pieces):
    modulated, qkv_val, prob, att, branch = kept
    tokens = x.shape[0]
    count = len(pieces)
    return pl.pallas_call(
        functools.partial(attn_bwd_kernel, layer, far, count, extra),
        out_shape=(
            sds((2 * D, D), BF16),
            sds((2 * D + extra, D), BF16),
            sds((tokens, D), F32),
            sds((16, D), BF16),
        ),
        in_specs=[SMEM] + [VMEM] * 9 + [HBM] * (2 + count),
        out_specs=(VMEM,) * 4,
        scratch_shapes=[
            pltpu.VMEM((D, 3 * D), BF16),
            pltpu.VMEM((D, D), BF16),
            pltpu.VMEM((tokens, D), BF16),
            pltpu.VMEM((tokens, 3 * D), BF16),
            pltpu.SemaphoreType.DMA((2 + 2 * count,)),
        ],
        compiler_params=pltpu.CompilerParams(vmem_limit_bytes=LIMIT),
        cost_estimate=pl.CostEstimate(flops=14 * 10**8, bytes_accessed=14 * 10**6, transcendentals=10**4),
        name="attn_bwd",
    )(meta, grad, vecs, x, modulated, qkv_val, prob, att, branch, part_sums, qkv, out, *pieces)


def add_split_kernel(axis, extra, *refs):
    meta, keep, got = refs[:3]
    mine_out, send_out = refs[-2:]
    half = keep.shape[0] // 2
    place = meta[axis]
    mine, other = rows_of(place * half, half), rows_of((1 - place) * half, half)
    mine_out[0:half, :] = (keep[mine, :].astype(F32) + got[mine, :].astype(F32)).astype(BF16)
    send_out[0:half, :] = (keep[other, :].astype(F32) + got[other, :].astype(F32)).astype(BF16)
    if extra:
        rides = refs[3]
        send_out[half : half + extra, :] = rides[...]
        send_out[half + extra : half + 2 * extra, :] = got[2 * half : 2 * half + extra, :]


def add_split(axis, meta, keep, got, ride=None):
    half = keep.shape[0] // 2
    extra = 0 if ride is None else ride.shape[0]
    rides = () if ride is None else (ride,)
    return pl.pallas_call(
        functools.partial(add_split_kernel, axis, extra),
        out_shape=(sds((half, D), BF16), sds((half + 2 * extra, D), BF16)),
        in_specs=[SMEM] + [VMEM] * (2 + len(rides)),
        out_specs=(VMEM, VMEM),
        compiler_params=pltpu.CompilerParams(vmem_limit_bytes=LIMIT),
        cost_estimate=pl.CostEstimate(flops=10**6, bytes_accessed=2 * 10**6, transcendentals=0),
        name="add_split",
    )(meta, keep, got, *rides)


def add_spread_kernel(extra, *refs):
    meta, keep, got = refs[:3]
    mine_out = refs[-4]
    quarter = keep.shape[0] // 4
    z = meta[3]
    for step in range(4):
        rows = rows_of((z ^ step) * quarter, quarter)
        out = refs[step - 4]
        out[0:quarter, :] = (keep[rows, :].astype(F32) + got[rows, :].astype(F32)).astype(BF16)
        if extra:
            out[quarter : quarter + extra, :] = refs[3][...]
            out[quarter + extra : quarter + 2 * extra, :] = got[4 * quarter : 4 * quarter + extra, :]


def add_spread(meta, keep, got, ride=None):
    quarter = keep.shape[0] // 4
    extra = 0 if ride is None else ride.shape[0]
    rides = () if ride is None else (ride,)
    return pl.pallas_call(
        functools.partial(add_spread_kernel, extra),
        out_shape=(sds((quarter + 2 * extra, D), BF16),) * 4,
        in_specs=[SMEM] + [VMEM] * (2 + len(rides)),
        out_specs=(VMEM,) * 4,
        compiler_params=pltpu.CompilerParams(vmem_limit_bytes=LIMIT),
        cost_estimate=pl.CostEstimate(flops=10**6, bytes_accessed=2 * 10**6, transcendentals=0),
        name="add_spread",
    )(meta, keep, got, *rides)


def add_all_kernel(rows, extra, *refs):
    out = refs[4]
    total = refs[0][0:rows, :].astype(F32)
    for ref in refs[1:4]:
        total = total + ref[0:rows, :].astype(F32)
    out[...] = total.astype(BF16)
    if extra:
        for index in range(4):
            refs[5][index * extra : (index + 1) * extra, :] = refs[index][rows : rows + extra, :]


def add_all(parts, rows):
    extra = parts[0].shape[0] - rows
    shapes = (sds((rows, D), BF16),)
    if extra:
        shapes = shapes + (sds((4 * extra, D), BF16),)
    return pl.pallas_call(
        functools.partial(add_all_kernel, rows, extra),
        out_shape=shapes,
        in_specs=[VMEM] * 4,
        out_specs=(VMEM,) * len(shapes),
        compiler_params=pltpu.CompilerParams(vmem_limit_bytes=LIMIT),
        cost_estimate=pl.CostEstimate(flops=10**6, bytes_accessed=10**6, transcendentals=0),
        name="add_all",
    )(*parts)


def join_kernel(meta, *refs):
    out = refs[4]
    rows = refs[0].shape[0]
    z = meta[3]
    for step in range(4):
        out[rows_of((z ^ step) * rows, rows), :] = refs[step][...]


def join(meta, parts):
    return pl.pallas_call(
        join_kernel,
        out_shape=sds((4 * parts[0].shape[0], D), BF16),
        in_specs=[SMEM] + [VMEM] * 4,
        out_specs=VMEM,
        compiler_params=pltpu.CompilerParams(vmem_limit_bytes=LIMIT),
        cost_estimate=pl.CostEstimate(flops=10**6, bytes_accessed=10**6, transcendentals=0),
        name="join",
    )(meta, *parts)


def gather_rows(meta, refs, scratch):
    core, y = meta[1], meta[2]
    rows = refs[0].shape[0]
    for index, (c, v) in enumerate(((core, y), (core, 1 - y), (1 - core, y), (1 - core, 1 - y))):
        scratch[c, rows_of(v * rows, rows), :] = refs[index][...]


def attn_result_kernel(meta, *refs):
    qkv_out, out_out, scratch = refs[8:]
    half = D // 2
    for layer in range(LAYERS):
        gather_rows(meta, refs[4 * layer : 4 * layer + 4], scratch)
        for block in range(4):
            value = scratch[block // 2, (block % 2) * half : (block % 2 + 1) * half, :].astype(F32)
            if block < 3:
                qkv_out[layer, :, block * D : (block + 1) * D] = value
            else:
                out_out[layer, :, :] = value


def attn_result(meta, lower, upper):
    half = D // 2
    return pl.pallas_call(
        attn_result_kernel,
        out_shape=(sds((LAYERS, half, 3 * D), F32), sds((LAYERS, half, D), F32)),
        in_specs=[SMEM] + [VMEM] * 8,
        out_specs=(VMEM, VMEM),
        scratch_shapes=[pltpu.VMEM((2, 2 * half, D), BF16)],
        compiler_params=pltpu.CompilerParams(vmem_limit_bytes=LIMIT),
        cost_estimate=pl.CostEstimate(flops=10**6, bytes_accessed=4 * 10**6, transcendentals=0),
        name="attn_result",
    )(meta, *lower, *upper)


def mlp_result_kernel(meta, *refs):
    up_out, down_out, scratch = refs[8:]
    half = D // 2
    for layer in range(LAYERS):
        gather_rows(meta, refs[4 * layer : 4 * layer + 4], scratch)
        for block in range(4):
            value = scratch[block // 2, (block % 2) * half : (block % 2 + 1) * half, :].astype(F32)
            up_out[layer, :, block * D : (block + 1) * D] = value
        for core in range(2):
            down_out[layer, core * D : (core + 1) * D, :] = scratch[core, D : 2 * D, :].astype(F32)


def mlp_result(meta, lower, upper):
    half = D // 2
    return pl.pallas_call(
        mlp_result_kernel,
        out_shape=(sds((LAYERS, half, 4 * D), F32), sds((LAYERS, 2 * D, D), F32)),
        in_specs=[SMEM] + [VMEM] * 8,
        out_specs=(VMEM, VMEM),
        scratch_shapes=[pltpu.VMEM((2, 2 * D, D), BF16)],
        compiler_params=pltpu.CompilerParams(vmem_limit_bytes=LIMIT),
        cost_estimate=pl.CostEstimate(flops=10**6, bytes_accessed=8 * 10**6, transcendentals=0),
        name="mlp_result",
    )(meta, *lower, *upper)


def on_device(reps, *arguments):
    (
        latents,
        timestep_embed,
        labels,
        counts,
        class_table,
        ada_weight,
        ada_bias,
        qkv_weight,
        qv_bias,
        out_weight,
        out_bias,
        up_weight,
        up_bias,
        down_weight,
        down_bias,
        cotangent,
    ) = arguments
    half = D // 2
    rep = lax.axis_index("rep")
    x = lax.axis_index("shard")
    core, y, z = rep & 1, (rep >> 1) & 1, (rep >> 2) & 3
    meta = jnp.stack([x, core, y, z, jnp.minimum(counts[0], 1)]).astype(jnp.int32)

    def over_x(value):
        return lax.ppermute(value, "shard", [(0, 1), (1, 0)])

    def over_rep(value, distance):
        return lax.ppermute(value, "rep", [(r, r ^ distance) for r in range(reps)])

    CORE, Y, Z = 1, 2, 4

    bias_parts = (ada_bias, qv_bias, out_bias, up_bias, down_bias)
    own_bias = [member.astype(F32) for member in bias_parts]
    timestep_mine = lax.dynamic_slice(timestep_embed, (0, x * half), (1, half))
    timestep_other = lax.dynamic_slice(timestep_embed, (0, (1 - x) * half), (1, half))
    first = jnp.concatenate(
        [timestep_other[0], labels.astype(F32)] + [member.reshape(-1) for member in own_bias]
    )[None]
    got_first = over_x(first)[0]
    send_a0 = pack_attn(0, False, 2, meta, qkv_weight, out_weight)
    send_m0 = pack_mlp(0, False, 4, meta, up_weight, down_weight)
    send_a1 = pack_attn(1, False, 4, meta, qkv_weight, out_weight)
    send_m1 = pack_mlp(1, True, 4, meta, up_weight, down_weight)

    def fetch(send, distance):
        got = over_x(send)
        if distance is None:
            return [got, over_rep(got, CORE)]
        next_got = over_rep(got, distance)
        return [got, next_got, over_rep(got, CORE), over_rep(next_got, CORE)]

    pieces_a0 = fetch(send_a0, None)
    pieces_m0 = fetch(send_m0, Y)
    pieces_a1 = fetch(send_a1, Y)
    pieces_m1 = fetch(send_m1, Z)

    timestep_pair = jnp.concatenate([timestep_mine, got_first[None, :half]], axis=0)
    label_pair = jnp.stack([labels[0], got_first[half].astype(jnp.int32)])
    classes = class_table.shape[0]
    one_hot_pair = (label_pair[:, None] == jnp.arange(classes)[None, :]).astype(BF16)
    condition_pair = timestep_pair + dot(one_hot_pair, class_table)
    act_pair = (condition_pair * jax.nn.sigmoid(condition_pair)).astype(BF16)
    partial = jnp.einsum("nk,lkm->nlm", act_pair, ada_weight, preferred_element_type=F32)
    modul = partial[0] + over_x(partial[1])

    offset = half + 1
    full_bias = []
    for member in own_bias:
        size = member.size
        other = got_first[offset : offset + size].reshape(member.shape)
        offset += size
        full_bias.append(
            jnp.where(
                x == 0,
                jnp.concatenate([member, other], axis=1),
                jnp.concatenate([other, member], axis=1),
            )
        )
    vecs_all = jnp.concatenate(
        [
            (modul + full_bias[0]).reshape(LAYERS, 6, D),
            full_bias[1].reshape(LAYERS, 2, D),
            full_bias[2].reshape(LAYERS, 1, D),
            full_bias[4].reshape(LAYERS, 1, D),
            full_bias[3].reshape(LAYERS, 4, D),
            jnp.zeros((LAYERS, 2, D), F32),
        ],
        axis=1,
    )
    vecs = [vecs_all[layer] for layer in range(LAYERS)]

    def spread(value, axis_steps):
        parts = [value[None]]
        for step in axis_steps:
            parts.append(over_rep(value, step)[None])
        return jnp.concatenate(parts, axis=0)

    info = jnp.concatenate(
        [condition_pair, label_pair.astype(F32)[:, None], jnp.zeros((2, 63), F32)], axis=1
    )
    info = spread(info, [CORE])
    info = spread(info, [Y])
    info = spread(info, [Z, 2 * Z, 3 * Z])
    outer = reps // 16
    if outer > 1:
        info = spread(info, [16 * step for step in range(1, outer)])
    info = info.reshape(2 * reps, half + 64)

    stream = latents[0]
    attn_weights = (qkv_weight, out_weight)
    mlp_weights = (up_weight, down_weight)
    *kept_a0, middle0 = attn_fwd(0, False, meta, stream, vecs[0], *attn_weights, pieces_a0)
    stream1, *kept_m0 = mlp_fwd(0, False, False, meta, middle0, vecs[0], *mlp_weights, pieces_m0)
    *kept_a1, middle1 = attn_fwd(1, False, meta, stream1, vecs[1], *attn_weights, pieces_a1)
    activations, *kept_m1 = mlp_fwd(1, True, True, meta, middle1, vecs[1], *mlp_weights, pieces_m1)

    def reduce_chunk(keep, sent, ride=None):
        got = over_rep(sent, CORE)
        mine, send = add_split(0, meta, keep, got, ride)
        if ride is not None:
            ride = send[mine.shape[0] :]
        got = over_x(send)
        mine, send = add_split(2, meta, mine, got, ride)
        if ride is not None:
            ride = send[mine.shape[0] :]
        got = over_rep(send, Y)
        mine, *sends = add_spread(meta, mine, got, ride)
        rows = keep.shape[0] // 16
        parts = [mine] + [over_rep(send, Z * (1 + step)) for step, send in enumerate(sends)]
        mine, *rides = add_all(parts, rows)
        if outer > 1:
            total = mine.astype(F32)
            for step in range(1, outer):
                total = total + over_rep(mine, 16 * step).astype(F32)
            mine = total.astype(BF16)
        parts = [mine] + [over_rep(mine, Z * step) for step in range(1, 4)]
        mine = join(meta, parts)
        next_mine = over_rep(mine, Y)
        result = (mine, next_mine, over_rep(mine, CORE), over_rep(next_mine, CORE))
        if not rides:
            return result, None
        rides = rides[0]
        if outer > 1:
            rides = spread(rides, [16 * step for step in range(1, outer)])
        return result, rides

    keep, sent, grad, part_sums = mlp_bwd(
        1, True, True, meta, cotangent[0], vecs[1], (middle1, *kept_m1), *mlp_weights, pieces_m1
    )
    result_m1, _ = reduce_chunk(keep, sent)
    keep, sent, grad, sums1 = attn_bwd(
        1, False, 0, meta, grad, vecs[1], stream1, kept_a1, part_sums, *attn_weights, pieces_a1
    )
    result_a1, _ = reduce_chunk(keep, sent)
    keep, sent, grad, part_sums = mlp_bwd(
        0, False, False, meta, grad, vecs[0], (middle0, *kept_m0), *mlp_weights, pieces_m0, sums1
    )
    result_m0, rides1 = reduce_chunk(keep, sent, sums1)
    keep, sent, grad_stream, sums0 = attn_bwd(
        0, False, 16, meta, grad, vecs[0], stream, kept_a0, part_sums, *attn_weights, pieces_a0
    )
    result_a0, rides0 = reduce_chunk(keep, sent, sums0)

    up_grad, down_grad = mlp_result(meta, result_m0, result_m1)
    qkv_grad, out_grad = attn_result(meta, result_a0, result_a1)

    condition = info[:, :half]
    label_all = info[:, half].astype(jnp.int32)
    sigmoid = jax.nn.sigmoid(condition)
    act_all = (condition * sigmoid).astype(BF16)
    grad_cond = jnp.zeros_like(condition)
    ada_grads, sum_rows = [], []
    for layer, rides in enumerate((rides0, rides1)):
        rides = rides.reshape(outer * 8, 2, 2, 16, D).swapaxes(1, 2).reshape(2 * reps, 16, D)
        vectors = rides[:, :6].reshape(2 * reps, 6 * D)
        ada_grads.append(dot_tn(act_all, vectors))
        grad_cond = grad_cond + dot_nt(vectors, ada_weight[layer])
        sum_rows.append(jnp.sum(rides.astype(F32), axis=0))
    ada_grad = jnp.stack(ada_grads)
    cond_grads = grad_cond * sigmoid * (1.0 + condition * (1.0 - sigmoid))
    one_hot = (label_all[:, None] == jnp.arange(classes)[None, :]).astype(F32)
    table_grad = lax.dot_general(
        one_hot, cond_grads, (((0,), (0,)), ((), ())), precision=lax.Precision.HIGHEST
    )
    other_cond = over_x(cond_grads[1:2])
    cond_grad = jnp.where(
        x == 0,
        jnp.concatenate([cond_grads[0:1], other_cond], axis=1),
        jnp.concatenate([other_cond, cond_grads[0:1]], axis=1),
    )
    sums_all = jnp.stack(sum_rows)

    def bias_grad(low, high):
        whole = sums_all[:, low:high].reshape(LAYERS, (high - low) * D)
        return lax.dynamic_slice(whole, (0, x * (whole.shape[1] // 2)), (LAYERS, whole.shape[1] // 2))

    return (
        activations[None],
        grad_stream[None],
        cond_grad,
        table_grad,
        ada_grad,
        bias_grad(0, 6),
        qkv_grad,
        bias_grad(6, 8),
        out_grad,
        bias_grad(8, 9),
        up_grad,
        bias_grad(10, 14),
        down_grad,
        bias_grad(9, 10),
    )


def solution(mesh):
    reps = mesh.shape["rep"]
    both = ("rep", "shard")
    in_specs = (
        P(both, None, None),
        P(both, None),
        P(both),
        P(both),
        P(None, "shard"),
    ) + (P(None, "shard", None), P(None, "shard")) * 5 + (P(both, None, None),)
    out_specs = (
        P(both, None, None),
        P(both, None, None),
        P(both, None),
        P(None, "shard"),
    ) + (P(None, "shard", None), P(None, "shard")) * 5
    return jax.shard_map(
        functools.partial(on_device, reps),
        mesh=mesh,
        in_specs=in_specs,
        out_specs=out_specs,
        check_vma=False,
    )
```

```python
import functools
import math

import jax
import jax.numpy as jnp
from jax import lax
from jax.experimental import pallas as pl
from jax.experimental.pallas import tpu as pltpu
from jax.sharding import PartitionSpec as P

D = 384
HEAD_DIM = 64
LAYERS = 2
F32 = jnp.float32
BF16 = jnp.bfloat16

norm_eps = 1e-06
gelu_coeff = math.sqrt(2.0 / math.pi)
gelu_cubic = 0.044715

VMEM = pl.BlockSpec(memory_space=pltpu.VMEM)
SMEM = pl.BlockSpec(memory_space=pltpu.SMEM)
ANY = pl.BlockSpec(memory_space=pl.ANY)
HBM = pl.BlockSpec(memory_space=pltpu.HBM)
LIMIT = 16 * 1024 * 1024
SMALL = 8 * 1024 * 1024


def sds(shape, dtype):
    return jax.ShapeDtypeStruct(shape, dtype)


def norm_rows(values):
    centered = values - jnp.mean(values, axis=-1, keepdims=True)
    inv_dev = lax.rsqrt(jnp.mean(centered * centered, axis=-1, keepdims=True) + norm_eps)
    return (centered * inv_dev, inv_dev)


def norm_back(grad_normed, normed, inv_dev):
    return (
        grad_normed
        - jnp.mean(grad_normed, axis=-1, keepdims=True)
        - normed * jnp.mean(grad_normed * normed, axis=-1, keepdims=True)
    ) * inv_dev


def gelu_parts(pre_act):
    square = pre_act * pre_act
    inner_arg = gelu_coeff * pre_act * (1.0 + gelu_cubic * square)
    tanh_val = jnp.tanh(inner_arg)
    half_up = 0.5 * (1.0 + tanh_val)
    value_out = pre_act * half_up
    slope_out = half_up + 0.5 * pre_act * (1.0 - tanh_val * tanh_val) * (
        gelu_coeff + (3.0 * gelu_cubic * gelu_coeff) * square
    )
    return (value_out, slope_out)


def dot(a, b):
    return jnp.dot(a, b, preferred_element_type=F32)


def dot_nt(a, b):
    return lax.dot_general(a, b, (((1,), (1,)), ((), ())), preferred_element_type=F32)


def dot_tn(a, b):
    return lax.dot_general(a, b, (((0,), (0,)), ((), ())), preferred_element_type=F32)


def head_masks():
    lane = lax.broadcasted_iota(jnp.int32, (1, 2 * HEAD_DIM), 1)
    first = lane < HEAD_DIM
    return first, jnp.logical_not(first)


def keep_lanes(values, mask):
    return jnp.where(mask, values, jnp.zeros_like(values))


def rows_of(start, size):
    return pl.ds(pl.multiple_of(start, 16), size)


def attn_weight_copies(meta, layer, qkv_hbm, out_hbm, pieces, offsets, w_qkv, w_out, sems):
    half = qkv_hbm.shape[1]
    x = meta[0]
    copies = [
        (qkv_hbm.at[layer], w_qkv.at[rows_of(x * half, half), :]),
        (out_hbm.at[layer], w_out.at[rows_of(x * half, half), :]),
    ]
    for piece, offset in zip(pieces, offsets):
        size = piece.shape[0]
        start = (1 - x) * half + offset * size
        copies.append((piece.at[:, pl.ds(0, 3 * D)], w_qkv.at[rows_of(start, size), :]))
        copies.append((piece.at[:, pl.ds(3 * D, D)], w_out.at[rows_of(start, size), :]))
    return [pltpu.make_async_copy(s, d, sems.at[i]) for i, (s, d) in enumerate(copies)]


def mlp_weight_copies(meta, layer, up_hbm, down_hbm, pieces, offsets, w_up, w_down, sems):
    half = up_hbm.shape[1]
    tall = down_hbm.shape[1]
    blocks = tall // half
    x = meta[0]
    copies = [
        (up_hbm.at[layer], w_up.at[rows_of(x * half, half), :]),
        (down_hbm.at[layer], w_down.at[rows_of(x * tall, tall), :]),
    ]
    for piece, offset in zip(pieces, offsets):
        size = piece.shape[0] // 2
        start = (1 - x) * half + offset * size
        copies.append((piece.at[pl.ds(0, size), :], w_up.at[rows_of(start, size), :]))
        for b in range(blocks):
            start = (1 - x) * tall + offset * (blocks * size) + b * size
            copies.append(
                (
                    piece.at[pl.ds(size, size), pl.ds(b * D, D)],
                    w_down.at[rows_of(start, size), :],
                )
            )
    return [pltpu.make_async_copy(s, d, sems.at[i]) for i, (s, d) in enumerate(copies)]


def piece_offsets(meta, count, far):
    core, y, z = meta[1], meta[2], meta[3]
    if count == 2:
        return [core, 1 - core]
    near = z % 2 if far else y
    return [
        near * 2 + core,
        (1 - near) * 2 + core,
        near * 2 + (1 - core),
        (1 - near) * 2 + (1 - core),
    ]


def call(body, ins, in_specs, out_shape, out_specs, name, scratch=(), deps=(), **more):
    given, late = len(ins), len(deps)

    def kernel(*refs):
        body(*refs[:given], *refs[given + late :])

    return pl.pallas_call(
        kernel,
        out_shape=out_shape,
        in_specs=list(in_specs) + [ANY] * late,
        out_specs=out_specs,
        scratch_shapes=list(scratch),
        compiler_params=pltpu.CompilerParams(vmem_limit_bytes=SMALL),
        cost_estimate=pl.CostEstimate(flops=10**10, bytes_accessed=0, transcendentals=0),
        name=name,
        **more,
    )(*ins, *deps)


def pack_attn_into(send, parts, offset, qkv, out):
    size = qkv.shape[1] // parts
    rows = rows_of(offset * size, size)
    send[:, 0 : 3 * D] = qkv[0, rows, :]
    send[:, 3 * D : 4 * D] = out[0, rows, :]


def pack_mlp_into(send, layer, offset, up, down):
    size = up.shape[1] // 4
    blocks = down.shape[1] // up.shape[1]
    send[0:size, :] = up[layer, rows_of(offset * size, size), :]
    for b in range(blocks):
        rows = rows_of(offset * (blocks * size) + b * size, size)
        send[size : 2 * size, b * D : (b + 1) * D] = down[layer, rows, :]


def pack_first(meta, qkv, out):
    half = qkv.shape[1]

    def body(meta, qkv, out, send):
        pack_attn_into(send, 2, piece_offsets(meta, 2, False)[0], qkv, out)

    return pl.pallas_call(
        body,
        grid=(1,),
        out_shape=sds((half // 2, 4 * D), BF16),
        in_specs=[
            SMEM,
            pl.BlockSpec((1, half, 3 * D), lambda i: (0, 0, 0)),
            pl.BlockSpec((1, half, D), lambda i: (0, 0, 0)),
        ],
        out_specs=pl.BlockSpec((half // 2, 4 * D), lambda i: (0, 0)),
        compiler_params=pltpu.CompilerParams(vmem_limit_bytes=LIMIT),
        name="pack_first",
    )(meta, qkv, out)


def pack_rest(meta, qkv, out, up, down, info, deps):
    half = qkv.shape[1]
    size = half // 4

    def body(meta, qkv, out, up, down, *refs):
        send_m0, send_a1, send_m1, info_out = refs[-4:]
        info_out[...] = refs[0][...]
        pack_mlp_into(send_m0, 0, piece_offsets(meta, 4, False)[0], up, down)
        pack_attn_into(send_a1, 4, piece_offsets(meta, 4, False)[0], qkv, out)
        pack_mlp_into(send_m1, 1, piece_offsets(meta, 4, True)[0], up, down)

    whole = lambda i: (0, 0, 0)
    flat = lambda i: (0, 0)
    return pl.pallas_call(
        body,
        grid=(1,),
        out_shape=(
            sds((2 * size, 4 * D), BF16),
            sds((size, 4 * D), BF16),
            sds((2 * size, 4 * D), BF16),
            sds(info.shape, F32),
        ),
        in_specs=[
            SMEM,
            pl.BlockSpec((1, half, 3 * D), lambda i: (1, 0, 0)),
            pl.BlockSpec((1, half, D), lambda i: (1, 0, 0)),
            pl.BlockSpec(up.shape, whole),
            pl.BlockSpec(down.shape, whole),
            pl.BlockSpec(info.shape, flat),
        ]
        + [ANY] * len(deps),
        out_specs=(
            pl.BlockSpec((2 * size, 4 * D), flat),
            pl.BlockSpec((size, 4 * D), flat),
            pl.BlockSpec((2 * size, 4 * D), flat),
            pl.BlockSpec(info.shape, flat),
        ),
        compiler_params=pltpu.CompilerParams(vmem_limit_bytes=LIMIT),
        name="pack_rest",
    )(meta, qkv, out, up, down, info, *deps)


def first_message(timestep, labels, ada_bias, qv_bias, out_bias, up_bias, down_bias):
    ins = (timestep, ada_bias, qv_bias, out_bias, up_bias, down_bias)

    def body(labels, *refs):
        send, held, sems = refs[6], refs[7:13], refs[13]
        copies = [pltpu.make_async_copy(refs[i], held[i], sems.at[i]) for i in range(6)]
        for copy in copies:
            copy.start()
        send[...] = jnp.zeros_like(send)
        send[4:5, D : D + 128] = jnp.full((1, 128), labels[0], jnp.int32).astype(F32)
        for copy in copies:
            copy.wait()
        time, ada, qv, out, up, down = held
        send[0:2, 0 : 3 * D] = ada[...].astype(F32)
        send[0:2, 3 * D : 4 * D] = qv[...].astype(F32)
        send[2:4, 0 : 2 * D] = up[...].astype(F32)
        send[2:4, 2 * D : 2 * D + D // 2] = out[...].astype(F32)
        send[2:4, 1024 : 1024 + D // 2] = down[...].astype(F32)
        send[4:5, 0:D] = time[...]

    return call(
        body,
        (labels,) + ins,
        [SMEM] + [HBM] * 6,
        sds((8, 4 * D), F32),
        VMEM,
        "first_message",
        scratch=[pltpu.VMEM(member.shape, member.dtype) for member in ins]
        + [pltpu.SemaphoreType.DMA((6,))],
    )


def condition_kernel(meta, own, got, table_ref, ada_ref, info_out, mine_out, send_out, table, ada, sems):
    half = D // 2
    x = meta[0]
    copy = pltpu.make_async_copy(ada_ref, ada, sems.at[0])
    copy.start()
    classes = table_ref.shape[1]
    aligned = classes // 128 * 128
    table[:, aligned:] = jnp.zeros((half, table.shape[1] - aligned), BF16)
    table[:, 0:classes] = table_ref[...]
    row = lax.broadcasted_iota(jnp.int32, (8, 1), 0)
    timestep = jnp.where(row == 0, own[4:5, 0:D], got[4:5, 0:D])
    label = jnp.where(row == 0, own[4:5, D : D + 1], got[4:5, D : D + 1])
    timestep = jnp.where(x == 0, timestep[:, :half], timestep[:, half:])
    classes = lax.broadcasted_iota(jnp.int32, (8, table.shape[1]), 1).astype(F32)
    one_hot = jnp.where(classes == label, 1.0, 0.0).astype(BF16)
    condition = timestep + dot_nt(one_hot, table[...])
    act = (condition * (1.0 / (1.0 + jnp.exp(-condition)))).astype(BF16)
    info_out[:, 0:half] = condition[0:2, :]
    info_out[:, half:256] = jnp.zeros((2, 256 - half), F32)
    info_out[:, 256:384] = jnp.broadcast_to(label[0:2, :], (2, 128))
    copy.wait()
    for layer in range(LAYERS):
        part = dot(act, ada[layer])
        mine_out[layer : layer + 1, :] = part[0:1, :]
        send_out[layer : layer + 1, :] = part[1:2, :]


def condition_step(meta, own, got, table, ada):
    return call(
        condition_kernel,
        (meta, own, got, table.T, ada),
        [SMEM] + [VMEM] * 3 + [HBM],
        (sds((2, D), F32), sds((LAYERS, 6 * D), F32), sds((LAYERS, 6 * D), F32)),
        (VMEM,) * 3,
        "condition",
        scratch=[
            pltpu.VMEM((D // 2, -(-table.shape[0] // 128) * 128), BF16),
            pltpu.VMEM(ada.shape, BF16),
            pltpu.SemaphoreType.DMA((1,)),
        ],
    )


def vectors_kernel(meta, own, got, mine_part, got_part, out):
    x = meta[0]
    low = jnp.where(x == 0, own[...], got[...])
    high = jnp.where(x == 0, got[...], own[...])
    modul = mine_part[...] + got_part[...]
    half = D // 2
    out[...] = jnp.zeros_like(out)
    for layer in range(LAYERS):
        rows = slice(layer, layer + 1)
        for member in range(6):
            side = low if member < 3 else high
            col = (member % 3) * D
            out[layer, member : member + 1, :] = (
                modul[rows, member * D : (member + 1) * D] + side[rows, col : col + D]
            )
        out[layer, 6:7, :] = low[rows, 3 * D : 4 * D]
        out[layer, 7:8, :] = high[rows, 3 * D : 4 * D]
        rows = slice(2 + layer, 3 + layer)
        for index, start in ((8, 2 * D), (9, 1024)):
            out[layer, index : index + 1, :] = jnp.concatenate(
                [low[rows, start : start + half], high[rows, start : start + half]], axis=1
            )
        for index, side, col in ((10, low, 0), (11, low, D), (12, high, 0), (13, high, D)):
            out[layer, index : index + 1, :] = side[rows, col : col + D]


def vectors_step(meta, own, got, mine_part, got_part):
    return call(
        vectors_kernel,
        (meta, own, got, mine_part, got_part),
        [SMEM] + [VMEM] * 4,
        sds((LAYERS, 16, D), F32),
        VMEM,
        "vectors",
    )


def attn_fwd_kernel(layer, far, count, *refs):
    meta, x_ref, vecs, qkv_hbm, out_hbm = refs[:5]
    pieces = refs[5 : 5 + count]
    modulated_out, qkv_out, prob_out, att_out, branch_out, middle_out = refs[5 + count : 11 + count]
    w_qkv, w_out, sems = refs[11 + count :]
    copies = attn_weight_copies(
        meta, layer, qkv_hbm, out_hbm, pieces, piece_offsets(meta, count, far), w_qkv, w_out, sems
    )
    for copy in copies:
        copy.start()
    stream = x_ref[...].astype(F32)
    normed, _ = norm_rows(stream)
    modulated = (normed * (1.0 + vecs[1:2, :]) + vecs[0:1, :]).astype(BF16)
    modulated_out[...] = modulated
    for copy in copies:
        copy.wait()
    for part in range(3):
        cols = slice(part * D, (part + 1) * D)
        value = dot(modulated, w_qkv[:, cols])
        if part == 0:
            value = value + vecs[6:7, :]
        if part == 2:
            value = value + vecs[7:8, :]
        qkv_out[:, cols] = value.astype(BF16)
    masks = head_masks()
    tokens = stream.shape[0]
    for pair in range(D // (2 * HEAD_DIM)):
        lanes = slice(pair * 2 * HEAD_DIM, (pair + 1) * 2 * HEAD_DIM)
        query = qkv_out[:, lanes]
        key = qkv_out[:, pair * 128 + D : (pair + 1) * 128 + D]
        value = qkv_out[:, pair * 128 + 2 * D : (pair + 1) * 128 + 2 * D]
        attended = None
        for member in range(2):
            head = 2 * pair + member
            scores = dot_nt(query, keep_lanes(key, masks[member])) * HEAD_DIM ** (-0.5)
            top = jnp.max(scores, axis=-1, keepdims=True)
            expo = jnp.exp(scores - top)
            prob = (expo * (1.0 / jnp.sum(expo, axis=-1, keepdims=True))).astype(BF16)
            prob_out[head * tokens : (head + 1) * tokens, :] = prob
            part = dot(prob, keep_lanes(value, masks[member]))
            attended = part if attended is None else attended + part
        att_out[:, lanes] = attended.astype(BF16)
    branch = dot(att_out[...], w_out[...]) + vecs[8:9, :]
    branch_out[...] = branch
    middle_out[...] = stream + vecs[2:3, :] * branch


def attn_fwd(layer, far, meta, x, vecs, qkv, out, pieces):
    tokens = x.shape[0]
    count = len(pieces)
    heads = D // HEAD_DIM
    return pl.pallas_call(
        functools.partial(attn_fwd_kernel, layer, far, count),
        out_shape=(
            sds((tokens, D), BF16),
            sds((tokens, 3 * D), BF16),
            sds((heads * tokens, tokens), BF16),
            sds((tokens, D), BF16),
            sds((tokens, D), F32),
            sds((tokens, D), F32),
        ),
        in_specs=[SMEM, VMEM, VMEM] + [HBM] * 2 + [ANY] * count,
        out_specs=(VMEM,) * 6,
        scratch_shapes=[
            pltpu.VMEM((D, 3 * D), BF16),
            pltpu.VMEM((D, D), BF16),
            pltpu.SemaphoreType.DMA((2 + 2 * count,)),
        ],
        compiler_params=pltpu.CompilerParams(vmem_limit_bytes=LIMIT),
        cost_estimate=pl.CostEstimate(flops=10**10, bytes_accessed=0, transcendentals=0),
        name="attn_fwd",
    )(meta, x, vecs, qkv, out, *pieces)


def mlp_fwd_kernel(layer, far, count, last, late, *refs):
    refs = refs[:3] + refs[3 + late :]
    meta, middle_ref, vecs, up_hbm, down_hbm = refs[:5]
    pieces = refs[5 : 5 + count]
    x_out, mod_out, act_out, slope_out, branch_out = refs[5 + count : 10 + count]
    w_up, w_down, sems = refs[10 + count :]
    copies = mlp_weight_copies(
        meta, layer, up_hbm, down_hbm, pieces, piece_offsets(meta, count, far), w_up, w_down, sems
    )
    for copy in copies:
        copy.start()
    middle = middle_ref[...]
    normed, _ = norm_rows(middle)
    mod_two = (normed * (1.0 + vecs[4:5, :]) + vecs[3:4, :]).astype(BF16)
    mod_out[...] = mod_two
    for copy in copies:
        copy.wait()
    branch = None
    for part in range(4):
        cols = slice(part * D, (part + 1) * D)
        pre_act = dot(mod_two, w_up[:, cols]) + vecs[10 + part : 11 + part, :]
        value, slope = gelu_parts(pre_act)
        value = value.astype(BF16)
        act_out[:, cols] = value
        slope_out[:, cols] = slope.astype(BF16)
        term = dot(value, w_down[cols, :])
        branch = term if branch is None else branch + term
    branch = branch + vecs[9:10, :]
    branch_out[...] = branch
    result = middle + vecs[5:6, :] * branch
    if last:
        live = meta[4].astype(F32)
        result = result * live
    x_out[...] = result.astype(x_out.dtype)


def mlp_fwd(layer, far, last, meta, middle, vecs, up, down, pieces, deps=()):
    tokens = middle.shape[0]
    count = len(pieces)
    return pl.pallas_call(
        functools.partial(mlp_fwd_kernel, layer, far, count, last, len(deps)),
        out_shape=(
            sds((tokens, D), BF16 if last else F32),
            sds((tokens, D), BF16),
            sds((tokens, 4 * D), BF16),
            sds((tokens, 4 * D), BF16),
            sds((tokens, D), F32),
        ),
        in_specs=[SMEM, VMEM, VMEM] + [ANY] * len(deps) + [HBM] * 2 + [ANY] * count,
        out_specs=(VMEM,) * 5,
        scratch_shapes=[
            pltpu.VMEM((D, 4 * D), BF16),
            pltpu.VMEM((4 * D, D), BF16),
            pltpu.SemaphoreType.DMA((2 + 5 * count,)),
        ],
        compiler_params=pltpu.CompilerParams(vmem_limit_bytes=LIMIT),
        cost_estimate=pl.CostEstimate(flops=10**10, bytes_accessed=0, transcendentals=0),
        name="mlp_fwd",
    )(meta, middle, vecs, *deps, up, down, *pieces)


def split_store(core, value, half, keep, send, rows):
    @pl.when(core == half)
    def _():
        keep[rows, :] = value

    @pl.when(core != half)
    def _():
        send[rows, :] = value


def mlp_bwd_kernel(layer, far, count, masked, late, *refs):
    meta, grad_ref, vecs, middle_ref, branch_ref, act_ref, slope_ref, mod_ref = refs[:8]
    refs = refs[8 + late :]
    up_hbm, down_hbm = refs[:2]
    pieces = refs[2 : 2 + count]
    keep, send, grad_out, sums_out = refs[2 + count : 6 + count]
    w_up, w_down, pre_bf, sems = refs[6 + count :]
    copies = mlp_weight_copies(
        meta, layer, up_hbm, down_hbm, pieces, piece_offsets(meta, count, far), w_up, w_down, sems
    )
    for copy in copies:
        copy.start()
    core = meta[1]
    grad = grad_ref[...].astype(F32)
    if masked:
        grad = grad * meta[4].astype(F32)
    sums_out[...] = jnp.zeros_like(sums_out)
    sums_out[5:6, :] = jnp.sum(grad * branch_ref[...], axis=0, keepdims=True)
    grad_branch = grad * vecs[5:6, :]
    sums_out[9:10, :] = jnp.sum(grad_branch, axis=0, keepdims=True)
    branch_bf = grad_branch.astype(BF16)
    half = D // 2
    for part in range(4):
        value = dot_tn(act_ref[:, part * D : (part + 1) * D], branch_bf).astype(BF16)
        base = (part // 2) * 4 * half + 2 * half
        split_store(core, value, part % 2, keep, send, slice(base, base + D))
    for copy in copies:
        copy.wait()
    mod_two = mod_ref[...]
    grad_mod = None
    for part in range(4):
        cols = slice(part * D, (part + 1) * D)
        grad_pre = dot_nt(branch_bf, w_down[cols, :]) * slope_ref[:, cols].astype(F32)
        sums_out[10 + part : 11 + part, :] = jnp.sum(grad_pre, axis=0, keepdims=True)
        pre = grad_pre.astype(BF16)
        value = dot_tn(mod_two, pre).astype(BF16)
        for side in range(2):
            base = side * 4 * half + (part % 2) * half
            split_store(
                core,
                value[side * half : (side + 1) * half, :],
                part // 2,
                keep,
                send,
                slice(base, base + half),
            )
        term = dot_nt(pre, w_up[:, cols])
        grad_mod = term if grad_mod is None else grad_mod + term
    normed, inv_dev = norm_rows(middle_ref[...])
    sums_out[3:4, :] = jnp.sum(grad_mod, axis=0, keepdims=True)
    sums_out[4:5, :] = jnp.sum(grad_mod * normed, axis=0, keepdims=True)
    grad_out[...] = grad + norm_back(grad_mod * (1.0 + vecs[4:5, :]), normed, inv_dev)


def mlp_bwd(layer, far, masked, meta, grad, vecs, kept, up, down, pieces, deps=()):
    middle, mod_two, act, slope, branch = kept
    tokens = middle.shape[0]
    count = len(pieces)
    late = len(deps)
    return pl.pallas_call(
        functools.partial(mlp_bwd_kernel, layer, far, count, masked, late),
        out_shape=(
            sds((4 * D, D), BF16),
            sds((4 * D, D), BF16),
            sds((tokens, D), F32),
            sds((16, D), F32),
        ),
        in_specs=[SMEM] + [VMEM] * 7 + [ANY] * late + [HBM] * 2 + [ANY] * count,
        out_specs=(VMEM,) * 4,
        scratch_shapes=[
            pltpu.VMEM((D, 4 * D), BF16),
            pltpu.VMEM((4 * D, D), BF16),
            pltpu.VMEM((16, D), BF16),
            pltpu.SemaphoreType.DMA((2 + 5 * count,)),
        ],
        compiler_params=pltpu.CompilerParams(vmem_limit_bytes=LIMIT),
        cost_estimate=pl.CostEstimate(flops=10**10, bytes_accessed=0, transcendentals=0),
        name="mlp_bwd",
    )(meta, grad, vecs, middle, branch, act, slope, mod_two, *deps, up, down, *pieces)


def attn_bwd_kernel(layer, far, count, extra, late, *refs):
    meta, grad_ref, vecs, x_ref, modulated_ref, qkv_ref, prob_ref, att_ref, branch_ref, part_sums = refs[:10]
    refs = refs[:10] + refs[10 + late :]
    qkv_hbm, out_hbm = refs[10:12]
    pieces = refs[12 : 12 + count]
    keep, send, grad_out, sums_out = refs[12 + count : 16 + count]
    w_qkv, w_out, ga_ref, proj_ref, sems = refs[16 + count :]
    copies = attn_weight_copies(
        meta, layer, qkv_hbm, out_hbm, pieces, piece_offsets(meta, count, far), w_qkv, w_out, sems
    )
    for copy in copies:
        copy.start()
    core = meta[1]
    half = D // 2
    tokens = grad_ref.shape[0]
    sums = {}
    grad = grad_ref[...]
    sums[2] = jnp.sum(grad * branch_ref[...], axis=0, keepdims=True)
    grad_battn = grad * vecs[2:3, :]
    sums[8] = jnp.sum(grad_battn, axis=0, keepdims=True)
    battn_bf = grad_battn.astype(BF16)

    def store(value, block):
        for side in range(2):
            base = side * 2 * half + (block % 2) * half
            split_store(
                core,
                value[side * half : (side + 1) * half, :],
                block // 2,
                keep,
                send,
                slice(base, base + half),
            )

    store(dot_tn(att_ref[...], battn_bf).astype(BF16), 3)
    for copy in copies:
        copy.wait()
    ga_ref[...] = dot_nt(battn_bf, w_out[...]).astype(BF16)
    masks = head_masks()
    grad_q_sums, grad_v_sums = [], []
    for pair in range(D // (2 * HEAD_DIM)):
        lanes = slice(pair * 128, (pair + 1) * 128)
        query = qkv_ref[:, lanes]
        key = qkv_ref[:, pair * 128 + D : (pair + 1) * 128 + D]
        value = qkv_ref[:, pair * 128 + 2 * D : (pair + 1) * 128 + 2 * D]
        grad_att = ga_ref[:, lanes]
        grad_q = grad_k = grad_v = None
        for member in range(2):
            head = 2 * pair + member
            mask = masks[member]
            prob_bf = prob_ref[head * tokens : (head + 1) * tokens, :]
            prob = prob_bf.astype(F32)
            grad_prob = dot_nt(grad_att, keep_lanes(value, mask))
            term_v = dot_tn(prob_bf, keep_lanes(grad_att, mask))
            weighted = prob * grad_prob
            row_dot = jnp.sum(weighted, axis=-1, keepdims=True)
            grad_scores = ((weighted - prob * row_dot) * HEAD_DIM ** (-0.5)).astype(BF16)
            term_q = dot(grad_scores, keep_lanes(key, mask))
            term_k = dot_tn(grad_scores, keep_lanes(query, mask))
            grad_q = term_q if grad_q is None else grad_q + term_q
            grad_k = term_k if grad_k is None else grad_k + term_k
            grad_v = term_v if grad_v is None else grad_v + term_v
        grad_q_sums.append(jnp.sum(grad_q, axis=0, keepdims=True))
        grad_v_sums.append(jnp.sum(grad_v, axis=0, keepdims=True))
        proj_ref[:, lanes] = grad_q.astype(BF16)
        proj_ref[:, pair * 128 + D : (pair + 1) * 128 + D] = grad_k.astype(BF16)
        proj_ref[:, pair * 128 + 2 * D : (pair + 1) * 128 + 2 * D] = grad_v.astype(BF16)
    sums[6] = jnp.concatenate(grad_q_sums, axis=1)
    sums[7] = jnp.concatenate(grad_v_sums, axis=1)
    modulated = modulated_ref[...]
    for block in range(3):
        store(dot_tn(modulated, proj_ref[:, block * D : (block + 1) * D]).astype(BF16), block)
    grad_mod = dot_nt(proj_ref[...], w_qkv[...])
    normed, inv_dev = norm_rows(x_ref[...].astype(F32))
    sums[0] = jnp.sum(grad_mod, axis=0, keepdims=True)
    sums[1] = jnp.sum(grad_mod * normed, axis=0, keepdims=True)
    grad_out[...] = grad + norm_back(grad_mod * (1.0 + vecs[1:2, :]), normed, inv_dev)
    row = lax.broadcasted_iota(jnp.int32, (16, 1), 0)
    total = part_sums[...]
    for index, value in sums.items():
        total = jnp.where(row == index, value, total)
    total = total.astype(BF16)
    sums_out[...] = total
    if extra:
        send[4 * half : 4 * half + 16, :] = total


def attn_bwd(layer, far, extra, meta, grad, vecs, x, kept, part_sums, qkv, out, pieces, deps=()):
    modulated, qkv_val, prob, att, branch = kept
    tokens = x.shape[0]
    count = len(pieces)
    return pl.pallas_call(
        functools.partial(attn_bwd_kernel, layer, far, count, extra, len(deps)),
        out_shape=(
            sds((2 * D, D), BF16),
            sds((2 * D + extra, D), BF16),
            sds((tokens, D), F32),
            sds((16, D), BF16),
        ),
        in_specs=[SMEM] + [VMEM] * 9 + [ANY] * len(deps) + [HBM] * 2 + [ANY] * count,
        out_specs=(VMEM,) * 4,
        scratch_shapes=[
            pltpu.VMEM((D, 3 * D), BF16),
            pltpu.VMEM((D, D), BF16),
            pltpu.VMEM((tokens, D), BF16),
            pltpu.VMEM((tokens, 3 * D), BF16),
            pltpu.SemaphoreType.DMA((2 + 2 * count,)),
        ],
        compiler_params=pltpu.CompilerParams(vmem_limit_bytes=LIMIT),
        cost_estimate=pl.CostEstimate(flops=10**10, bytes_accessed=0, transcendentals=0),
        name="attn_bwd",
    )(meta, grad, vecs, x, modulated, qkv_val, prob, att, branch, part_sums, *deps, qkv, out, *pieces)


def add_rows(a, a_rows, b, b_rows):
    return (a[a_rows, :].astype(F32) + b[b_rows, :].astype(F32)).astype(BF16)


def first_split(meta, keep, got, sums, deps):
    half = keep.shape[0] // 2
    extra = 0 if sums is None else sums.shape[0]

    def body(meta, keep, got, *refs):
        mine_out, send_out = refs[-2:]
        x = meta[0]
        mine, other = rows_of(x * half, half), rows_of((1 - x) * half, half)
        mine_out[...] = add_rows(keep, mine, got, mine)
        send_out[0:half, :] = add_rows(keep, other, got, other)
        if extra:
            own, far = refs[0][...], got[2 * half : 2 * half + extra, :]
            lanes = D // 2
            low = jnp.concatenate([own[:, :lanes], far[:, :lanes]], axis=1)
            high = jnp.concatenate([own[:, lanes:], far[:, lanes:]], axis=1)
            send_out[half : half + extra, :] = jnp.where(meta[1] == 0, low, high)

    rides = () if sums is None else (sums,)
    return call(
        body,
        (meta, keep, got) + rides,
        [SMEM] + [VMEM] * (2 + len(rides)),
        (sds((half, D), BF16), sds((half + extra, D), BF16)),
        (VMEM, VMEM),
        "first_split",
        deps=deps,
    )


def next_split(axis, meta, keep, sent, got, deps):
    whole = keep.shape[0]
    half = whole // 2
    extra = got.shape[0] - whole

    def body(meta, keep, sent, got, mine_out, send_out):
        place = meta[axis]
        mine, other = rows_of(place * half, half), rows_of((1 - place) * half, half)
        mine_out[...] = add_rows(keep, mine, got, mine)
        send_out[0:half, :] = add_rows(keep, other, got, other)
        if extra:
            send_out[half : half + extra, :] = sent[whole : whole + extra, :]
            send_out[half + extra : half + 2 * extra, :] = got[whole : whole + extra, :]

    return call(
        body,
        (meta, keep, sent, got),
        [SMEM] + [VMEM] * 3,
        (sds((half, D), BF16), sds((half + 2 * extra, D), BF16)),
        (VMEM, VMEM),
        "next_split",
        deps=deps,
    )


def add_join(keep, sent, got, rows, last, deps):
    extra = got.shape[0] - rows

    def body(keep, sent, got, *outs):
        everything = slice(0, rows)
        outs[0][0:rows, :] = add_rows(keep, everything, got, everything)
        if extra:
            out, start = (outs[1], 0) if last else (outs[0], rows)
            out[start : start + extra, :] = sent[rows : rows + extra, :]
            out[start + extra : start + 2 * extra, :] = got[rows : rows + extra, :]

    out_shape = (sds((rows + (0 if last else 2 * extra), D), BF16),)
    if last and extra:
        out_shape = out_shape + (sds((2 * extra, D), BF16),)
    return call(
        body,
        (keep, sent, got),
        [VMEM] * 3,
        out_shape,
        (VMEM,) * len(out_shape),
        "add_join",
        deps=deps,
    )


def join(meta, mine, got, deps):
    rows = mine.shape[0]

    def body(meta, mine, got, out):
        low = meta[5]
        out[rows_of(low * rows, rows), :] = mine[...]
        out[rows_of((1 - low) * rows, rows), :] = got[...]

    return call(
        body, (meta, mine, got), [SMEM, VMEM, VMEM], sds((2 * rows, D), BF16), VMEM, "join", deps=deps
    )


def gather_rows(meta, refs, scratch):
    core, y = meta[1], meta[2]
    rows = refs[0].shape[0]
    for index, (c, v) in enumerate(((core, y), (core, 1 - y), (1 - core, y), (1 - core, 1 - y))):
        scratch[c, rows_of(v * rows, rows), :] = refs[index][...]


def attn_result(layer, meta, parts, before, deps):
    half = D // 2

    def body(meta, *refs):
        qkv_out, out_out, scratch = refs[-3:]
        gather_rows(meta, refs[:4], scratch)
        for block in range(4):
            value = scratch[block // 2, (block % 2) * half : (block % 2 + 1) * half, :].astype(F32)
            if block < 3:
                qkv_out[0, :, block * D : (block + 1) * D] = value
            else:
                out_out[0, :, :] = value

    return result_call(
        body,
        (meta, *parts),
        before,
        ((LAYERS, half, 3 * D), (LAYERS, half, D)),
        layer,
        (2, 2 * half, D),
        "attn_result",
        deps,
    )


def mlp_result(layer, meta, parts, before, deps):
    half = D // 2

    def body(meta, *refs):
        up_out, down_out, scratch = refs[-3:]
        gather_rows(meta, refs[:4], scratch)
        for block in range(4):
            value = scratch[block // 2, (block % 2) * half : (block % 2 + 1) * half, :].astype(F32)
            up_out[0, :, block * D : (block + 1) * D] = value
        for core in range(2):
            down_out[0, core * D : (core + 1) * D, :] = scratch[core, D : 2 * D, :].astype(F32)

    return result_call(
        body,
        (meta, *parts),
        before,
        ((LAYERS, half, 4 * D), (LAYERS, 2 * D, D)),
        layer,
        (2, 2 * D, D),
        "mlp_result",
        deps,
    )


def result_call(body, ins, before, shapes, layer, scratch, name, deps):
    given, count = len(ins), len(shapes)

    def kernel(*refs):
        rest = refs[given + len(before) + len(deps) :]
        outs, blocks, held, sems = rest[:count], rest[count : 2 * count], rest[-2], rest[-1]
        body(*refs[:given], *blocks, held)
        copies = [
            pltpu.make_async_copy(blocks[i], outs[i].at[pl.ds(layer, 1)], sems.at[i])
            for i in range(count)
        ]
        for copy in copies:
            copy.start()
        for copy in copies:
            copy.wait()

    return pl.pallas_call(
        kernel,
        out_shape=tuple(sds(shape, F32) for shape in shapes),
        in_specs=[SMEM] + [VMEM] * (given - 1) + [HBM] * len(before) + [ANY] * len(deps),
        out_specs=(HBM,) * count,
        scratch_shapes=[pltpu.VMEM((1,) + shape[1:], F32) for shape in shapes]
        + [pltpu.VMEM(scratch, BF16), pltpu.SemaphoreType.DMA((count,))],
        input_output_aliases={given + index: index for index in range(len(before))},
        compiler_params=pltpu.CompilerParams(vmem_limit_bytes=LIMIT),
        cost_estimate=pl.CostEstimate(flops=10**10, bytes_accessed=0, transcendentals=0),
        name=name,
    )(*ins, *before, *deps)


def silu_bf16(condition):
    return (condition * (1.0 / (1.0 + jnp.exp(-condition)))).astype(BF16)


def ada_result(layer, meta, info, rides, far, ada_weight, before, deps):
    slots = rides.shape[0] // 16
    half = D // 2

    def kernel(meta, info, rides, far, ada_hbm, *refs):
        ada_hbm_out, cond_out, sums_out, own_f32, far_f32, ada, ada_out, sems = refs[-8:]
        load = pltpu.make_async_copy(ada_hbm.at[pl.ds(layer, 1)], ada, sems.at[0])
        load.start()
        for block in range(D // 128):
            lanes = slice(block * 128, (block + 1) * 128)
            own_f32[block, :, :] = rides[:, lanes].astype(F32)
            far_f32[block, :, :] = far[:, lanes].astype(F32)
        act = silu_bf16(info[:, 0:half])
        first = meta[1] == 0
        grad_cond = jnp.zeros((2 * slots, half), F32)
        load.wait()
        sums_out[...] = jnp.zeros_like(sums_out)
        for row in range(14):
            mine, other = (
                jnp.concatenate(
                    [held[block, pl.ds(row, slots, stride=16), :] for block in range(D // 128)], axis=1
                )
                for held in (own_f32, far_f32)
            )
            vectors = []
            for one, two in (
                (mine[:, :half], other[:, half:]),
                (mine[:, half:], other[:, :half]),
            ):
                vectors.append(
                    jnp.concatenate([jnp.where(first, one, two), jnp.where(first, two, one)], axis=1)
                )
            both = jnp.concatenate(vectors, axis=0)
            sums_out[row : row + 1, :] = jnp.sum(both, axis=0, keepdims=True)
            if row < 6:
                cols = slice(row * D, (row + 1) * D)
                both = both.astype(BF16)
                ada_out[0, :, cols] = dot_tn(act, both)
                grad_cond = grad_cond + dot_nt(both, ada[0, :, cols])
        store = pltpu.make_async_copy(ada_out, ada_hbm_out.at[pl.ds(layer, 1)], sems.at[1])
        store.start()
        cond_out[...] = grad_cond
        store.wait()

    shape = ada_weight.shape
    return pl.pallas_call(
        kernel,
        out_shape=(sds(shape, F32), sds((2 * slots, half), F32), sds((16, D), F32)),
        in_specs=[SMEM, VMEM, VMEM, VMEM] + [HBM] * (1 + len(before)) + [ANY] * len(deps),
        out_specs=(HBM, VMEM, VMEM),
        scratch_shapes=[pltpu.VMEM((D // 128, 16 * slots, 128), F32)] * 2
        + [
            pltpu.VMEM((1,) + shape[1:], BF16),
            pltpu.VMEM((1,) + shape[1:], F32),
            pltpu.SemaphoreType.DMA((2,)),
        ],
        input_output_aliases={5: 0} if before else {},
        compiler_params=pltpu.CompilerParams(vmem_limit_bytes=LIMIT),
        cost_estimate=pl.CostEstimate(flops=10**10, bytes_accessed=0, transcendentals=0),
        name="ada_result",
    )(meta, info, rides, far, ada_weight, *before, *deps)


def condition_result(meta, info, conds, sums, classes, deps):
    half = D // 2

    def body(meta, info, cond0, cond1, sums0, sums1, *outs):
        table, mine, send, ada, qv, out, up, down = outs
        condition = info[:, 0:half]
        sigmoid = 1.0 / (1.0 + jnp.exp(-condition))
        grads = (cond0[...] + cond1[...]) * sigmoid * (1.0 + condition * (1.0 - sigmoid))
        mine[...] = grads[0:1, :]
        send[...] = grads[1:2, :]
        labels = info[:, 256:257]
        count = -(-classes // 128) * 128
        numbers = lax.broadcasted_iota(jnp.int32, (info.shape[0], count), 1).astype(F32)
        one_hot = jnp.where(numbers == labels, 1.0, 0.0)
        total = lax.dot_general(
            grads,
            one_hot,
            (((0,), (0,)), ((), ())),
            precision=lax.Precision.HIGHEST,
            preferred_element_type=F32,
        )
        table[...] = total[:, 0:classes]
        low = meta[0] == 0
        for layer, rows in enumerate((sums0, sums1)):
            at = slice(layer, layer + 1)

            def pick(one, two):
                return jnp.where(low, rows[one : one + 1, :], rows[two : two + 1, :])

            for index in range(3):
                ada[at, index * D : (index + 1) * D] = pick(index, index + 3)
            qv[at, :] = pick(6, 7)
            for index in range(2):
                up[at, index * D : (index + 1) * D] = pick(10 + index, 12 + index)
            for ref, row in ((out, 8), (down, 9)):
                value = rows[row : row + 1, :]
                ref[at, :] = jnp.where(low, value[:, :half], value[:, half:])

    shapes = (
        (half, classes),
        (1, half),
        (1, half),
        (LAYERS, 3 * D),
        (LAYERS, D),
        (LAYERS, half),
        (LAYERS, 2 * D),
        (LAYERS, half),
    )
    return call(
        body,
        (meta, info, *conds, *sums),
        [SMEM] + [VMEM] * 5,
        tuple(sds(shape, F32) for shape in shapes),
        (VMEM,) * len(shapes),
        "condition_result",
        deps=deps,
    )


def both_halves(meta, mine, other):
    def body(meta, mine, other, out):
        low = meta[0] == 0
        a, b = mine[...], other[...]
        out[...] = jnp.concatenate([jnp.where(low, a, b), jnp.where(low, b, a)], axis=1)

    return call(
        body, (meta, mine, other), [SMEM, VMEM, VMEM], sds((1, D), F32), VMEM, "both_halves"
    )


def on_device(reps, *arguments):
    (
        latents,
        timestep_embed,
        labels,
        counts,
        class_table,
        ada_weight,
        ada_bias,
        qkv_weight,
        qv_bias,
        out_weight,
        out_bias,
        up_weight,
        up_bias,
        down_weight,
        down_bias,
        cotangent,
    ) = arguments
    half = D // 2
    rep = lax.axis_index("rep")
    x = lax.axis_index("shard")
    core, y, z = rep & 1, (rep >> 1) & 1, (rep >> 2) & 3
    meta = jnp.stack([x, core, y, z, jnp.minimum(counts[0], 1), z & 1]).astype(jnp.int32)

    def over_x(value):
        return lax.ppermute(value, "shard", [(0, 1), (1, 0)])

    def over_rep(value, distance):
        return lax.ppermute(value, "rep", [(r, r ^ distance) for r in range(reps)])

    CORE, Y, Z = 1, 2, 4

    first = first_message(timestep_embed, labels, ada_bias, qv_bias, out_bias, up_bias, down_bias)
    got_first = over_x(first)
    send_a0 = pack_first(meta, qkv_weight, out_weight)
    classes = class_table.shape[0]
    info, mine_part, send_part = condition_step(meta, first, got_first, class_table, ada_weight)
    send_m0, send_a1, send_m1, info = pack_rest(
        meta, qkv_weight, out_weight, up_weight, down_weight, info, (send_part,)
    )

    def fetch(send, distance):
        got = over_x(send)
        if distance is None:
            return [got, over_rep(got, CORE)]
        next_got = over_rep(got, distance)
        return [got, next_got, over_rep(got, CORE), over_rep(next_got, CORE)]

    pieces_a0 = fetch(send_a0, None)
    vecs_all = vectors_step(meta, first, got_first, mine_part, over_x(send_part))
    pieces_m0 = fetch(send_m0, Y)
    pieces_a1 = fetch(send_a1, Y)
    pieces_m1 = fetch(send_m1, Z)
    vecs = [vecs_all[layer] for layer in range(LAYERS)]

    distances = [Z]
    while 2 * distances[-1] < reps:
        distances.append(2 * distances[-1])
    for distance in [Y] + distances + [CORE]:
        info = jnp.concatenate([info, over_rep(info, distance)], axis=0)

    stream = latents[0]
    attn_weights = (qkv_weight, out_weight)
    mlp_weights = (up_weight, down_weight)
    *kept_a0, middle0 = attn_fwd(0, False, meta, stream, vecs[0], *attn_weights, pieces_a0)
    stream1, *kept_m0 = mlp_fwd(
        0, False, False, meta, middle0, vecs[0], *mlp_weights, pieces_m0, (info,)
    )
    *kept_a1, middle1 = attn_fwd(1, False, meta, stream1, vecs[1], *attn_weights, pieces_a1)
    activations, *kept_m1 = mlp_fwd(1, True, True, meta, middle1, vecs[1], *mlp_weights, pieces_m1)

    last = [activations]

    def deps():
        return (last[0],)

    def ran(result):
        last[0] = result[-1] if isinstance(result, (tuple, list)) else result
        return result

    def reduce_chunk(keep, sent, sums):
        got = over_rep(sent, CORE)
        yield
        keep, sent = ran(first_split(meta, keep, got, sums, deps()))
        got = over_x(sent)
        yield
        keep, sent = ran(next_split(2, meta, keep, sent, got, deps()))
        got = over_rep(sent, Y)
        yield
        steps = distances
        if sums is None:
            keep, sent = ran(next_split(5, meta, keep, sent, got, deps()))
            got = over_rep(sent, Z)
            steps = distances[1:]
            yield
        rows = keep.shape[0]
        for distance in steps:
            (sent,) = ran(add_join(keep, sent, got, rows, False, deps()))
            keep = sent
            got = over_rep(sent, distance)
            yield
        mine, *rides = ran(add_join(keep, sent, got, rows, True, deps()))
        if sums is None:
            got = over_rep(mine, Z)
            yield
            mine = ran(join(meta, mine, got, deps()))
        next_mine = over_rep(mine, Y)
        result = (mine, next_mine, over_rep(mine, CORE), over_rep(next_mine, CORE))
        if rides:
            rides = (rides[0], over_rep(rides[0], CORE))
        yield result, rides

    def advance(chunk, times=1):
        result = None
        for _ in range(times):
            result = next(chunk)
        return result

    more = len(distances) - 1

    keep, sent, grad, part_sums = mlp_bwd(
        1, True, True, meta, cotangent[0], vecs[1], (middle1, *kept_m1), *mlp_weights, pieces_m1, deps()
    )
    m1 = reduce_chunk(keep, sent, None)
    advance(m1)
    keep, sent, grad, sums1 = ran(
        attn_bwd(
            1, False, 16, meta, grad, vecs[1], stream1, kept_a1, part_sums, *attn_weights, pieces_a1
        )
    )
    a1 = reduce_chunk(keep, sent, sums1)
    advance(a1)
    advance(m1)
    keep, sent, grad, part_sums = ran(
        mlp_bwd(
            0, False, False, meta, grad, vecs[0], (middle0, *kept_m0), *mlp_weights, pieces_m0, deps()
        )
    )
    m0 = reduce_chunk(keep, sent, None)
    advance(m0)
    advance(a1)
    keep, sent, grad_stream, sums0 = ran(
        attn_bwd(
            0,
            False,
            16,
            meta,
            grad,
            vecs[0],
            stream,
            kept_a0,
            part_sums,
            *attn_weights,
            pieces_a0,
            deps(),
        )
    )
    a0 = reduce_chunk(keep, sent, sums0)
    advance(a0)
    for chunk in (m1, m0, a1, a0, m1, a1):
        advance(chunk)
    advance(m1, more)
    advance(m0)
    advance(a1, more)
    advance(a0)
    advance(m1)
    advance(m0)
    advance(a0)
    result_m1, _ = advance(m1)
    advance(m0, more)
    result_a1, rides1 = advance(a1)
    advance(a0, more)
    ada_grad, cond1, sums1 = ran(ada_result(1, meta, info, *rides1, ada_weight, (), deps()))
    mlp_grads = ran(mlp_result(1, meta, result_m1, (), deps()))
    advance(m0)
    result_m0, _ = advance(m0)
    result_a0, rides0 = advance(a0)
    attn_grads = ran(attn_result(1, meta, result_a1, (), deps()))
    ada_grad, cond0, sums0 = ran(ada_result(0, meta, info, *rides0, ada_weight, (ada_grad,), deps()))
    table_grad, mine_cond, send_cond, *bias_grads = ran(
        condition_result(meta, info, (cond0, cond1), (sums0, sums1), classes, deps())
    )
    other_cond = over_x(send_cond)
    up_grad, down_grad = ran(mlp_result(0, meta, result_m0, mlp_grads, deps()))
    qkv_grad, out_grad = ran(attn_result(0, meta, result_a0, attn_grads, deps()))
    cond_grad = both_halves(meta, mine_cond, other_cond)
    ada_b, qv_b, out_b, up_b, down_b = bias_grads

    return (
        activations[None],
        grad_stream[None],
        cond_grad,
        table_grad.T,
        ada_grad,
        ada_b,
        qkv_grad,
        qv_b,
        out_grad,
        out_b,
        up_grad,
        up_b,
        down_grad,
        down_b,
    )


def solution(mesh):
    reps = mesh.shape["rep"]
    both = ("rep", "shard")
    in_specs = (
        P(both, None, None),
        P(both, None),
        P(both),
        P(both),
        P(None, "shard"),
    ) + (P(None, "shard", None), P(None, "shard")) * 5 + (P(both, None, None),)
    out_specs = (
        P(both, None, None),
        P(both, None, None),
        P(both, None),
        P(None, "shard"),
    ) + (P(None, "shard", None), P(None, "shard")) * 5
    return jax.shard_map(
        functools.partial(on_device, reps),
        mesh=mesh,
        in_specs=in_specs,
        out_specs=out_specs,
        check_vma=False,
    )
```

```python
import functools
import math

import jax
import jax.numpy as jnp
from jax import lax
from jax.experimental import pallas as pl
from jax.experimental.pallas import tpu as pltpu
from jax.sharding import PartitionSpec as P

D = 384
HEAD_DIM = 64
LAYERS = 2
F32 = jnp.float32
BF16 = jnp.bfloat16

norm_eps = 1e-06
gelu_coeff = math.sqrt(2.0 / math.pi)
gelu_cubic = 0.044715

VMEM = pl.BlockSpec(memory_space=pltpu.VMEM)
SMEM = pl.BlockSpec(memory_space=pltpu.SMEM)
ANY = pl.BlockSpec(memory_space=pl.ANY)
HBM = pl.BlockSpec(memory_space=pltpu.HBM)
LIMIT = 16 * 1024 * 1024
SMALL = 8 * 1024 * 1024
WIDE = 56 * 1024 * 1024


def sds(shape, dtype):
    return jax.ShapeDtypeStruct(shape, dtype)


def norm_rows(values):
    centered = values - jnp.mean(values, axis=-1, keepdims=True)
    inv_dev = lax.rsqrt(jnp.mean(centered * centered, axis=-1, keepdims=True) + norm_eps)
    return (centered * inv_dev, inv_dev)


def norm_back(grad_normed, normed, inv_dev):
    return (
        grad_normed
        - jnp.mean(grad_normed, axis=-1, keepdims=True)
        - normed * jnp.mean(grad_normed * normed, axis=-1, keepdims=True)
    ) * inv_dev


def gelu_parts(pre_act):
    square = pre_act * pre_act
    inner_arg = gelu_coeff * pre_act * (1.0 + gelu_cubic * square)
    tanh_val = jnp.tanh(inner_arg)
    half_up = 0.5 * (1.0 + tanh_val)
    value_out = pre_act * half_up
    slope_out = half_up + 0.5 * pre_act * (1.0 - tanh_val * tanh_val) * (
        gelu_coeff + (3.0 * gelu_cubic * gelu_coeff) * square
    )
    return (value_out, slope_out)


def dot(a, b):
    return jnp.dot(a, b, preferred_element_type=F32)


def dot_nt(a, b):
    return lax.dot_general(a, b, (((1,), (1,)), ((), ())), preferred_element_type=F32)


def dot_tn(a, b):
    return lax.dot_general(a, b, (((0,), (0,)), ((), ())), preferred_element_type=F32)


def head_masks():
    lane = lax.broadcasted_iota(jnp.int32, (1, 2 * HEAD_DIM), 1)
    first = lane < HEAD_DIM
    return first, jnp.logical_not(first)


def keep_lanes(values, mask):
    return jnp.where(mask, values, jnp.zeros_like(values))


def rows_of(start, size):
    return pl.ds(pl.multiple_of(start, 16), size)


def attn_weight_copies(meta, layer, qkv_hbm, out_hbm, pieces, offsets, w_qkv, w_out, sems):
    half = qkv_hbm.shape[1]
    x = meta[0]
    copies = [
        (qkv_hbm.at[layer], w_qkv.at[rows_of(x * half, half), :]),
        (out_hbm.at[layer], w_out.at[rows_of(x * half, half), :]),
    ]
    for piece, offset in zip(pieces, offsets):
        size = piece.shape[0]
        start = (1 - x) * half + offset * size
        copies.append((piece.at[:, pl.ds(0, 3 * D)], w_qkv.at[rows_of(start, size), :]))
        copies.append((piece.at[:, pl.ds(3 * D, D)], w_out.at[rows_of(start, size), :]))
    return [pltpu.make_async_copy(s, d, sems.at[i]) for i, (s, d) in enumerate(copies)]


def mlp_weight_copies(meta, layer, up_hbm, down_hbm, pieces, offsets, w_up, w_down, sems):
    half = up_hbm.shape[1]
    tall = down_hbm.shape[1]
    blocks = tall // half
    x = meta[0]
    copies = [
        (up_hbm.at[layer], w_up.at[rows_of(x * half, half), :]),
        (down_hbm.at[layer], w_down.at[rows_of(x * tall, tall), :]),
    ]
    for piece, offset in zip(pieces, offsets):
        size = piece.shape[0] // 2
        start = (1 - x) * half + offset * size
        copies.append((piece.at[pl.ds(0, size), :], w_up.at[rows_of(start, size), :]))
        for b in range(blocks):
            start = (1 - x) * tall + offset * (blocks * size) + b * size
            copies.append(
                (
                    piece.at[pl.ds(size, size), pl.ds(b * D, D)],
                    w_down.at[rows_of(start, size), :],
                )
            )
    return [pltpu.make_async_copy(s, d, sems.at[i]) for i, (s, d) in enumerate(copies)]


def piece_offsets(meta, count, far):
    core, y, z = meta[1], meta[2], meta[3]
    if count == 2:
        return [core, 1 - core]
    near = z % 2 if far else y
    return [
        near * 2 + core,
        (1 - near) * 2 + core,
        near * 2 + (1 - core),
        (1 - near) * 2 + (1 - core),
    ]


def call(body, ins, in_specs, out_shape, out_specs, name, scratch=(), deps=(), limit=SMALL, **more):
    given, late = len(ins), len(deps)

    def kernel(*refs):
        body(*refs[:given], *refs[given + late :])

    return pl.pallas_call(
        kernel,
        out_shape=out_shape,
        in_specs=list(in_specs) + [ANY] * late,
        out_specs=out_specs,
        scratch_shapes=list(scratch),
        compiler_params=pltpu.CompilerParams(vmem_limit_bytes=limit),
        cost_estimate=pl.CostEstimate(flops=10000000000, bytes_accessed=0, transcendentals=0),
        name=name,
        **more,
    )(*ins, *deps)


def pack_attn_copies(send, layer, parts, offset, qkv, out):
    size = qkv.shape[1] // parts
    rows = rows_of(offset * size, size)
    return [
        (qkv.at[layer, rows, :], send.at[:, pl.ds(0, 3 * D)]),
        (out.at[layer, rows, :], send.at[:, pl.ds(3 * D, D)]),
    ]


def pack_mlp_copies(send, layer, offset, up, down):
    size = up.shape[1] // 4
    blocks = down.shape[1] // up.shape[1]
    copies = [(up.at[layer, rows_of(offset * size, size), :], send.at[pl.ds(0, size), :])]
    for b in range(blocks):
        rows = rows_of(offset * (blocks * size) + b * size, size)
        copies.append((down.at[layer, rows, :], send.at[pl.ds(size, size), pl.ds(b * D, D)]))
    return copies


def pack(layer, far, parts, meta, qkv, out, up, down, deps, name):
    half = qkv.shape[1]
    size = half // 4

    def body(meta, qkv, out, up, down, send_attn, send_mlp, sems):
        copies = pack_attn_copies(send_attn, layer, parts, piece_offsets(meta, parts, False)[0], qkv, out)
        copies += pack_mlp_copies(send_mlp, layer, piece_offsets(meta, 4, far)[0], up, down)
        copies = [pltpu.make_async_copy(s, d, sems.at[i]) for i, (s, d) in enumerate(copies)]
        for copy in copies:
            copy.start()
        for copy in copies:
            copy.wait()

    return call(
        body,
        (meta, qkv, out, up, down),
        [SMEM] + [HBM] * 4,
        (sds((half // parts, 4 * D), BF16), sds((2 * size, 4 * D), BF16)),
        (VMEM, VMEM),
        name,
        scratch=[pltpu.SemaphoreType.DMA((8,))],
        deps=deps,
        limit=WIDE,
    )


def first_message(timestep, labels, ada_bias, qv_bias, out_bias, up_bias, down_bias):
    ins = (timestep, ada_bias, qv_bias, out_bias, up_bias, down_bias)

    def body(labels, *refs):
        send, held, sems = refs[6], refs[7:13], refs[13]
        copies = [pltpu.make_async_copy(refs[i], held[i], sems.at[i]) for i in range(6)]
        for copy in copies:
            copy.start()
        send[...] = jnp.zeros_like(send)
        send[4:5, D : D + 128] = jnp.full((1, 128), labels[0], jnp.int32).astype(F32)
        for copy in copies:
            copy.wait()
        time, ada, qv, out, up, down = held
        send[0:2, 0 : 3 * D] = ada[...].astype(F32)
        send[0:2, 3 * D : 4 * D] = qv[...].astype(F32)
        send[2:4, 0 : 2 * D] = up[...].astype(F32)
        send[2:4, 2 * D : 2 * D + D // 2] = out[...].astype(F32)
        send[2:4, 1024 : 1024 + D // 2] = down[...].astype(F32)
        send[4:5, 0:D] = time[...]

    return call(
        body,
        (labels,) + ins,
        [SMEM] + [HBM] * 6,
        sds((8, 4 * D), F32),
        VMEM,
        "first_message",
        scratch=[pltpu.VMEM(member.shape, member.dtype) for member in ins]
        + [pltpu.SemaphoreType.DMA((6,))],
        limit=WIDE,
    )


def condition_kernel(meta, own, got, table_ref, ada_ref, mine_out, send_out, table, ada, sems):
    half = D // 2
    x = meta[0]
    copy = pltpu.make_async_copy(ada_ref, ada, sems.at[0])
    copy.start()
    classes = table_ref.shape[1]
    aligned = classes // 128 * 128
    table[:, aligned:] = jnp.zeros((half, table.shape[1] - aligned), BF16)
    table[:, 0:classes] = table_ref[...]
    row = lax.broadcasted_iota(jnp.int32, (8, 1), 0)
    timestep = jnp.where(row == 0, own[4:5, 0:D], got[4:5, 0:D])
    label = jnp.where(row == 0, own[4:5, D : D + 1], got[4:5, D : D + 1])
    timestep = jnp.where(x == 0, timestep[:, :half], timestep[:, half:])
    classes = lax.broadcasted_iota(jnp.int32, (8, table.shape[1]), 1).astype(F32)
    one_hot = jnp.where(classes == label, 1.0, 0.0).astype(BF16)
    condition = timestep + dot_nt(one_hot, table[...])
    act = (condition * (1.0 / (1.0 + jnp.exp(-condition)))).astype(BF16)
    for ref, index in ((mine_out, 0), (send_out, 1)):
        ref[2:3, 0:half] = condition[index : index + 1, :]
        ref[2:3, half:] = jnp.zeros((1, 6 * D - half), F32)
    copy.wait()
    for layer in range(LAYERS):
        part = dot(act, ada[layer])
        mine_out[layer : layer + 1, :] = part[0:1, :]
        send_out[layer : layer + 1, :] = part[1:2, :]


def condition_step(meta, own, got, table, ada, deps):
    return call(
        condition_kernel,
        (meta, own, got, table.T, ada),
        [SMEM] + [VMEM] * 3 + [HBM],
        (sds((LAYERS + 1, 6 * D), F32),) * 2,
        (VMEM,) * 2,
        "condition",
        scratch=[
            pltpu.VMEM((D // 2, -(-table.shape[0] // 128) * 128), BF16),
            pltpu.VMEM(ada.shape, BF16),
            pltpu.SemaphoreType.DMA((1,)),
        ],
        deps=deps,
        limit=WIDE,
    )


def vectors_kernel(meta, own, got, mine_part, got_part, out):
    x = meta[0]
    low = jnp.where(x == 0, own[...], got[...])
    high = jnp.where(x == 0, got[...], own[...])
    modul = mine_part[...] + got_part[...]
    half = D // 2
    mine_cond, got_cond = mine_part[2:3, 0:half], got_part[2:3, 0:half]
    condition = jnp.concatenate(
        [jnp.where(x == 0, mine_cond, got_cond), jnp.where(x == 0, got_cond, mine_cond)], axis=1
    )
    label = jnp.broadcast_to(own[4:5, D : D + 1], (1, D))
    for layer in range(LAYERS):
        out[layer, 14:15, :] = condition
        out[layer, 15:16, :] = label
        rows = slice(layer, layer + 1)
        for member in range(6):
            side = low if member < 3 else high
            col = (member % 3) * D
            out[layer, member : member + 1, :] = (
                modul[rows, member * D : (member + 1) * D] + side[rows, col : col + D]
            )
        out[layer, 6:7, :] = low[rows, 3 * D : 4 * D]
        out[layer, 7:8, :] = high[rows, 3 * D : 4 * D]
        rows = slice(2 + layer, 3 + layer)
        for index, start in ((8, 2 * D), (9, 1024)):
            out[layer, index : index + 1, :] = jnp.concatenate(
                [low[rows, start : start + half], high[rows, start : start + half]], axis=1
            )
        for index, side, col in ((10, low, 0), (11, low, D), (12, high, 0), (13, high, D)):
            out[layer, index : index + 1, :] = side[rows, col : col + D]


def vectors_step(meta, own, got, mine_part, got_part):
    return call(
        vectors_kernel,
        (meta, own, got, mine_part, got_part),
        [SMEM] + [VMEM] * 4,
        sds((LAYERS, 16, D), F32),
        VMEM,
        "vectors",
    )


def attn_fwd_kernel(layer, far, count, *refs):
    meta, x_ref, vecs, qkv_hbm, out_hbm = refs[:5]
    pieces = refs[5 : 5 + count]
    modulated_out, qkv_out, prob_out, att_out, branch_out, middle_out = refs[5 + count : 11 + count]
    w_qkv, w_out, sems = refs[11 + count :]
    copies = attn_weight_copies(
        meta, layer, qkv_hbm, out_hbm, pieces, piece_offsets(meta, count, far), w_qkv, w_out, sems
    )
    for copy in copies:
        copy.start()
    stream = x_ref[...].astype(F32)
    normed, _ = norm_rows(stream)
    modulated = (normed * (1.0 + vecs[1:2, :]) + vecs[0:1, :]).astype(BF16)
    modulated_out[...] = modulated
    for copy in copies:
        copy.wait()
    for part in range(3):
        cols = slice(part * D, (part + 1) * D)
        value = dot(modulated, w_qkv[:, cols])
        if part == 0:
            value = value + vecs[6:7, :]
        if part == 2:
            value = value + vecs[7:8, :]
        qkv_out[:, cols] = value.astype(BF16)
    masks = head_masks()
    tokens = stream.shape[0]
    for pair in range(D // (2 * HEAD_DIM)):
        lanes = slice(pair * 2 * HEAD_DIM, (pair + 1) * 2 * HEAD_DIM)
        query = qkv_out[:, lanes]
        key = qkv_out[:, pair * 128 + D : (pair + 1) * 128 + D]
        value = qkv_out[:, pair * 128 + 2 * D : (pair + 1) * 128 + 2 * D]
        attended = None
        for member in range(2):
            head = 2 * pair + member
            scores = dot_nt(query, keep_lanes(key, masks[member])) * HEAD_DIM ** (-0.5)
            top = jnp.max(scores, axis=-1, keepdims=True)
            expo = jnp.exp(scores - top)
            prob = (expo * (1.0 / jnp.sum(expo, axis=-1, keepdims=True))).astype(BF16)
            prob_out[head * tokens : (head + 1) * tokens, :] = prob
            part = dot(prob, keep_lanes(value, masks[member]))
            attended = part if attended is None else attended + part
        att_out[:, lanes] = attended.astype(BF16)
    branch = dot(att_out[...], w_out[...]) + vecs[8:9, :]
    branch_out[...] = branch
    middle_out[...] = stream + vecs[2:3, :] * branch


def attn_fwd(layer, far, meta, x, vecs, qkv, out, pieces):
    tokens = x.shape[0]
    count = len(pieces)
    heads = D // HEAD_DIM
    return pl.pallas_call(
        functools.partial(attn_fwd_kernel, layer, far, count),
        out_shape=(
            sds((tokens, D), BF16),
            sds((tokens, 3 * D), BF16),
            sds((heads * tokens, tokens), BF16),
            sds((tokens, D), BF16),
            sds((tokens, D), F32),
            sds((tokens, D), F32),
        ),
        in_specs=[SMEM, VMEM, VMEM] + [HBM] * 2 + [ANY] * count,
        out_specs=(VMEM,) * 6,
        scratch_shapes=[
            pltpu.VMEM((D, 3 * D), BF16),
            pltpu.VMEM((D, D), BF16),
            pltpu.SemaphoreType.DMA((2 + 2 * count,)),
        ],
        compiler_params=pltpu.CompilerParams(vmem_limit_bytes=LIMIT),
        cost_estimate=pl.CostEstimate(flops=10000000000, bytes_accessed=0, transcendentals=0),
        name="attn_fwd",
    )(meta, x, vecs, qkv, out, *pieces)


def mlp_fwd_kernel(layer, far, count, last, late, *refs):
    refs = refs[:3] + refs[3 + late :]
    meta, middle_ref, vecs, up_hbm, down_hbm = refs[:5]
    pieces = refs[5 : 5 + count]
    x_out, mod_out, act_out, slope_out, branch_out = refs[5 + count : 10 + count]
    w_up, w_down, sems = refs[10 + count :]
    copies = mlp_weight_copies(
        meta, layer, up_hbm, down_hbm, pieces, piece_offsets(meta, count, far), w_up, w_down, sems
    )
    for copy in copies:
        copy.start()
    middle = middle_ref[...]
    normed, _ = norm_rows(middle)
    mod_two = (normed * (1.0 + vecs[4:5, :]) + vecs[3:4, :]).astype(BF16)
    mod_out[...] = mod_two
    for copy in copies:
        copy.wait()
    branch = None
    for part in range(4):
        cols = slice(part * D, (part + 1) * D)
        pre_act = dot(mod_two, w_up[:, cols]) + vecs[10 + part : 11 + part, :]
        value, slope = gelu_parts(pre_act)
        value = value.astype(BF16)
        act_out[:, cols] = value
        slope_out[:, cols] = slope.astype(BF16)
        term = dot(value, w_down[cols, :])
        branch = term if branch is None else branch + term
    branch = branch + vecs[9:10, :]
    branch_out[...] = branch
    result = middle + vecs[5:6, :] * branch
    if last:
        live = meta[4].astype(F32)
        result = result * live
    x_out[...] = result.astype(x_out.dtype)


def mlp_fwd(layer, far, last, meta, middle, vecs, up, down, pieces, deps=()):
    tokens = middle.shape[0]
    count = len(pieces)
    return pl.pallas_call(
        functools.partial(mlp_fwd_kernel, layer, far, count, last, len(deps)),
        out_shape=(
            sds((tokens, D), BF16 if last else F32),
            sds((tokens, D), BF16),
            sds((tokens, 4 * D), BF16),
            sds((tokens, 4 * D), BF16),
            sds((tokens, D), F32),
        ),
        in_specs=[SMEM, VMEM, VMEM] + [ANY] * len(deps) + [HBM] * 2 + [ANY] * count,
        out_specs=(VMEM,) * 5,
        scratch_shapes=[
            pltpu.VMEM((D, 4 * D), BF16),
            pltpu.VMEM((4 * D, D), BF16),
            pltpu.SemaphoreType.DMA((2 + 5 * count,)),
        ],
        compiler_params=pltpu.CompilerParams(vmem_limit_bytes=LIMIT),
        cost_estimate=pl.CostEstimate(flops=10000000000, bytes_accessed=0, transcendentals=0),
        name="mlp_fwd",
    )(meta, middle, vecs, *deps, up, down, *pieces)


def split_store(core, value, half, keep, send, rows):
    @pl.when(core == half)
    def _():
        keep[rows, :] = value

    @pl.when(core != half)
    def _():
        send[rows, :] = value


def mlp_bwd_kernel(layer, far, count, masked, late, *refs):
    meta, grad_ref, vecs, middle_ref, branch_ref, act_ref, slope_ref, mod_ref = refs[:8]
    refs = refs[8 + late :]
    up_hbm, down_hbm = refs[:2]
    pieces = refs[2 : 2 + count]
    keep, send, grad_out, sums_out = refs[2 + count : 6 + count]
    w_up, w_down, pre_bf, sems = refs[6 + count :]
    copies = mlp_weight_copies(
        meta, layer, up_hbm, down_hbm, pieces, piece_offsets(meta, count, far), w_up, w_down, sems
    )
    for copy in copies:
        copy.start()
    core = meta[1]
    grad = grad_ref[...].astype(F32)
    if masked:
        grad = grad * meta[4].astype(F32)
    sums_out[...] = jnp.zeros_like(sums_out)
    sums_out[5:6, :] = jnp.sum(grad * branch_ref[...], axis=0, keepdims=True)
    grad_branch = grad * vecs[5:6, :]
    sums_out[9:10, :] = jnp.sum(grad_branch, axis=0, keepdims=True)
    branch_bf = grad_branch.astype(BF16)
    half = D // 2
    for part in range(4):
        value = dot_tn(act_ref[:, part * D : (part + 1) * D], branch_bf).astype(BF16)
        base = (part // 2) * 4 * half + 2 * half
        split_store(core, value, part % 2, keep, send, slice(base, base + D))
    for copy in copies:
        copy.wait()
    mod_two = mod_ref[...]
    grad_mod = None
    for part in range(4):
        cols = slice(part * D, (part + 1) * D)
        grad_pre = dot_nt(branch_bf, w_down[cols, :]) * slope_ref[:, cols].astype(F32)
        sums_out[10 + part : 11 + part, :] = jnp.sum(grad_pre, axis=0, keepdims=True)
        pre = grad_pre.astype(BF16)
        value = dot_tn(mod_two, pre).astype(BF16)
        for side in range(2):
            base = side * 4 * half + (part % 2) * half
            split_store(
                core,
                value[side * half : (side + 1) * half, :],
                part // 2,
                keep,
                send,
                slice(base, base + half),
            )
        term = dot_nt(pre, w_up[:, cols])
        grad_mod = term if grad_mod is None else grad_mod + term
    normed, inv_dev = norm_rows(middle_ref[...])
    sums_out[3:4, :] = jnp.sum(grad_mod, axis=0, keepdims=True)
    sums_out[4:5, :] = jnp.sum(grad_mod * normed, axis=0, keepdims=True)
    grad_out[...] = grad + norm_back(grad_mod * (1.0 + vecs[4:5, :]), normed, inv_dev)


def mlp_bwd(layer, far, masked, meta, grad, vecs, kept, up, down, pieces, deps=()):
    middle, mod_two, act, slope, branch = kept
    tokens = middle.shape[0]
    count = len(pieces)
    late = len(deps)
    return pl.pallas_call(
        functools.partial(mlp_bwd_kernel, layer, far, count, masked, late),
        out_shape=(
            sds((4 * D, D), BF16),
            sds((4 * D, D), BF16),
            sds((tokens, D), F32),
            sds((16, D), F32),
        ),
        in_specs=[SMEM] + [VMEM] * 7 + [ANY] * late + [HBM] * 2 + [ANY] * count,
        out_specs=(VMEM,) * 4,
        scratch_shapes=[
            pltpu.VMEM((D, 4 * D), BF16),
            pltpu.VMEM((4 * D, D), BF16),
            pltpu.VMEM((16, D), BF16),
            pltpu.SemaphoreType.DMA((2 + 5 * count,)),
        ],
        compiler_params=pltpu.CompilerParams(vmem_limit_bytes=LIMIT),
        cost_estimate=pl.CostEstimate(flops=10000000000, bytes_accessed=0, transcendentals=0),
        name="mlp_bwd",
    )(meta, grad, vecs, middle, branch, act, slope, mod_two, *deps, up, down, *pieces)


def attn_bwd_kernel(layer, far, count, extra, late, *refs):
    meta, grad_ref, vecs, x_ref, modulated_ref, qkv_ref, prob_ref, att_ref, branch_ref, part_sums = refs[:10]
    refs = refs[:10] + refs[10 + late :]
    qkv_hbm, out_hbm = refs[10:12]
    pieces = refs[12 : 12 + count]
    keep, send, grad_out, sums_out = refs[12 + count : 16 + count]
    w_qkv, w_out, ga_ref, proj_ref, sems = refs[16 + count :]
    copies = attn_weight_copies(
        meta, layer, qkv_hbm, out_hbm, pieces, piece_offsets(meta, count, far), w_qkv, w_out, sems
    )
    for copy in copies:
        copy.start()
    core = meta[1]
    half = D // 2
    tokens = grad_ref.shape[0]
    sums = {}
    grad = grad_ref[...]
    sums[2] = jnp.sum(grad * branch_ref[...], axis=0, keepdims=True)
    grad_battn = grad * vecs[2:3, :]
    sums[8] = jnp.sum(grad_battn, axis=0, keepdims=True)
    battn_bf = grad_battn.astype(BF16)

    def store(value, block):
        for side in range(2):
            base = side * 2 * half + (block % 2) * half
            split_store(
                core,
                value[side * half : (side + 1) * half, :],
                block // 2,
                keep,
                send,
                slice(base, base + half),
            )

    store(dot_tn(att_ref[...], battn_bf).astype(BF16), 3)
    for copy in copies:
        copy.wait()
    ga_ref[...] = dot_nt(battn_bf, w_out[...]).astype(BF16)
    masks = head_masks()
    grad_q_sums, grad_v_sums = [], []
    for pair in range(D // (2 * HEAD_DIM)):
        lanes = slice(pair * 128, (pair + 1) * 128)
        query = qkv_ref[:, lanes]
        key = qkv_ref[:, pair * 128 + D : (pair + 1) * 128 + D]
        value = qkv_ref[:, pair * 128 + 2 * D : (pair + 1) * 128 + 2 * D]
        grad_att = ga_ref[:, lanes]
        grad_q = grad_k = grad_v = None
        for member in range(2):
            head = 2 * pair + member
            mask = masks[member]
            prob_bf = prob_ref[head * tokens : (head + 1) * tokens, :]
            prob = prob_bf.astype(F32)
            grad_prob = dot_nt(grad_att, keep_lanes(value, mask))
            term_v = dot_tn(prob_bf, keep_lanes(grad_att, mask))
            weighted = prob * grad_prob
            row_dot = jnp.sum(weighted, axis=-1, keepdims=True)
            grad_scores = ((weighted - prob * row_dot) * HEAD_DIM ** (-0.5)).astype(BF16)
            term_q = dot(grad_scores, keep_lanes(key, mask))
            term_k = dot_tn(grad_scores, keep_lanes(query, mask))
            grad_q = term_q if grad_q is None else grad_q + term_q
            grad_k = term_k if grad_k is None else grad_k + term_k
            grad_v = term_v if grad_v is None else grad_v + term_v
        grad_q_sums.append(jnp.sum(grad_q, axis=0, keepdims=True))
        grad_v_sums.append(jnp.sum(grad_v, axis=0, keepdims=True))
        proj_ref[:, lanes] = grad_q.astype(BF16)
        proj_ref[:, pair * 128 + D : (pair + 1) * 128 + D] = grad_k.astype(BF16)
        proj_ref[:, pair * 128 + 2 * D : (pair + 1) * 128 + 2 * D] = grad_v.astype(BF16)
    sums[6] = jnp.concatenate(grad_q_sums, axis=1)
    sums[7] = jnp.concatenate(grad_v_sums, axis=1)
    modulated = modulated_ref[...]
    for block in range(3):
        store(dot_tn(modulated, proj_ref[:, block * D : (block + 1) * D]).astype(BF16), block)
    grad_mod = dot_nt(proj_ref[...], w_qkv[...])
    normed, inv_dev = norm_rows(x_ref[...].astype(F32))
    sums[0] = jnp.sum(grad_mod, axis=0, keepdims=True)
    sums[1] = jnp.sum(grad_mod * normed, axis=0, keepdims=True)
    grad_out[...] = grad + norm_back(grad_mod * (1.0 + vecs[1:2, :]), normed, inv_dev)
    if layer == 1:
        high = vecs[14:15, :].astype(BF16).astype(F32)
        sums[14], sums[15] = high, vecs[14:15, :] - high
    else:
        high = jnp.floor(vecs[15:16, :] * (1.0 / 32.0))
        sums[14], sums[15] = high, vecs[15:16, :] - high * 32.0
    row = lax.broadcasted_iota(jnp.int32, (16, 1), 0)
    total = part_sums[...]
    for index, value in sums.items():
        total = jnp.where(row == index, value, total)
    total = total.astype(BF16)
    sums_out[...] = total
    if extra:
        send[4 * half : 4 * half + 16, :] = total


def attn_bwd(layer, far, extra, meta, grad, vecs, x, kept, part_sums, qkv, out, pieces, deps=()):
    modulated, qkv_val, prob, att, branch = kept
    tokens = x.shape[0]
    count = len(pieces)
    return pl.pallas_call(
        functools.partial(attn_bwd_kernel, layer, far, count, extra, len(deps)),
        out_shape=(
            sds((2 * D, D), BF16),
            sds((2 * D + extra, D), BF16),
            sds((tokens, D), F32),
            sds((16, D), BF16),
        ),
        in_specs=[SMEM] + [VMEM] * 9 + [ANY] * len(deps) + [HBM] * 2 + [ANY] * count,
        out_specs=(VMEM,) * 4,
        scratch_shapes=[
            pltpu.VMEM((D, 3 * D), BF16),
            pltpu.VMEM((D, D), BF16),
            pltpu.VMEM((tokens, D), BF16),
            pltpu.VMEM((tokens, 3 * D), BF16),
            pltpu.SemaphoreType.DMA((2 + 2 * count,)),
        ],
        compiler_params=pltpu.CompilerParams(vmem_limit_bytes=LIMIT),
        cost_estimate=pl.CostEstimate(flops=10000000000, bytes_accessed=0, transcendentals=0),
        name="attn_bwd",
    )(meta, grad, vecs, x, modulated, qkv_val, prob, att, branch, part_sums, *deps, qkv, out, *pieces)


def add_rows(a, a_rows, b, b_rows):
    return (a[a_rows, :].astype(F32) + b[b_rows, :].astype(F32)).astype(BF16)


def first_split(meta, keep, got, sums, deps):
    half = keep.shape[0] // 2
    extra = 0 if sums is None else sums.shape[0]

    def body(meta, keep, got, *refs):
        mine_out, send_out = refs[-2:]
        x = meta[0]
        mine, other = rows_of(x * half, half), rows_of((1 - x) * half, half)
        mine_out[...] = add_rows(keep, mine, got, mine)
        send_out[0:half, :] = add_rows(keep, other, got, other)
        if extra:
            own, far = refs[0][...], got[2 * half : 2 * half + extra, :]
            lanes = D // 2
            low = jnp.concatenate([own[:, :lanes], far[:, :lanes]], axis=1)
            high = jnp.concatenate([own[:, lanes:], far[:, lanes:]], axis=1)
            send_out[half : half + extra, :] = jnp.where(meta[1] == 0, low, high)

    rides = () if sums is None else (sums,)
    return call(
        body,
        (meta, keep, got) + rides,
        [SMEM] + [VMEM] * (2 + len(rides)),
        (sds((half, D), BF16), sds((half + extra, D), BF16)),
        (VMEM, VMEM),
        "first_split",
        deps=deps,
    )


def next_split(axis, meta, keep, sent, got, deps):
    whole = keep.shape[0]
    half = whole // 2
    extra = got.shape[0] - whole

    def body(meta, keep, sent, got, mine_out, send_out):
        place = meta[axis]
        mine, other = rows_of(place * half, half), rows_of((1 - place) * half, half)
        mine_out[...] = add_rows(keep, mine, got, mine)
        send_out[0:half, :] = add_rows(keep, other, got, other)
        if extra:
            send_out[half : half + extra, :] = sent[whole : whole + extra, :]
            send_out[half + extra : half + 2 * extra, :] = got[whole : whole + extra, :]

    return call(
        body,
        (meta, keep, sent, got),
        [SMEM] + [VMEM] * 3,
        (sds((half, D), BF16), sds((half + 2 * extra, D), BF16)),
        (VMEM, VMEM),
        "next_split",
        deps=deps,
    )


def add_join(keep, sent, got, rows, last, deps):
    extra = got.shape[0] - rows

    def body(keep, sent, got, *outs):
        everything = slice(0, rows)
        outs[0][0:rows, :] = add_rows(keep, everything, got, everything)
        if extra:
            out, start = (outs[1], 0) if last else (outs[0], rows)
            out[start : start + extra, :] = sent[rows : rows + extra, :]
            out[start + extra : start + 2 * extra, :] = got[rows : rows + extra, :]

    out_shape = (sds((rows + (0 if last else 2 * extra), D), BF16),)
    if last and extra:
        out_shape = out_shape + (sds((2 * extra, D), BF16),)
    return call(
        body,
        (keep, sent, got),
        [VMEM] * 3,
        out_shape,
        (VMEM,) * len(out_shape),
        "add_join",
        deps=deps,
    )


def join(meta, mine, got, deps):
    rows = mine.shape[0]

    def body(meta, mine, got, out):
        low = meta[5]
        out[rows_of(low * rows, rows), :] = mine[...]
        out[rows_of((1 - low) * rows, rows), :] = got[...]

    return call(
        body, (meta, mine, got), [SMEM, VMEM, VMEM], sds((2 * rows, D), BF16), VMEM, "join", deps=deps
    )


def gather_rows(meta, refs, scratch):
    core, y = meta[1], meta[2]
    rows = refs[0].shape[0]
    for index, (c, v) in enumerate(((core, y), (core, 1 - y), (1 - core, y), (1 - core, 1 - y))):
        scratch[c, rows_of(v * rows, rows), :] = refs[index][...]


def attn_result(layer, meta, parts, before, deps):
    half = D // 2

    def body(meta, *refs):
        qkv_out, out_out, scratch = refs[-3:]
        gather_rows(meta, refs[:4], scratch)
        for block in range(4):
            value = scratch[block // 2, (block % 2) * half : (block % 2 + 1) * half, :].astype(F32)
            if block < 3:
                qkv_out[0, :, block * D : (block + 1) * D] = value
            else:
                out_out[0, :, :] = value

    return result_call(
        body,
        (meta, *parts),
        before,
        ((LAYERS, half, 3 * D), (LAYERS, half, D)),
        layer,
        (2, 2 * half, D),
        "attn_result",
        deps,
    )


def mlp_result(layer, meta, parts, before, deps):
    half = D // 2

    def body(meta, *refs):
        up_out, down_out, scratch = refs[-3:]
        gather_rows(meta, refs[:4], scratch)
        for block in range(4):
            value = scratch[block // 2, (block % 2) * half : (block % 2 + 1) * half, :].astype(F32)
            up_out[0, :, block * D : (block + 1) * D] = value
        for core in range(2):
            down_out[0, core * D : (core + 1) * D, :] = scratch[core, D : 2 * D, :].astype(F32)

    return result_call(
        body,
        (meta, *parts),
        before,
        ((LAYERS, half, 4 * D), (LAYERS, 2 * D, D)),
        layer,
        (2, 2 * D, D),
        "mlp_result",
        deps,
    )


def result_call(body, ins, before, shapes, layer, scratch, name, deps):
    given, count = len(ins), len(shapes)

    def kernel(*refs):
        rest = refs[given + len(before) + len(deps) :]
        outs, blocks, held, sems = rest[:count], rest[count + 1 : 2 * count + 1], rest[-2], rest[-1]
        rest[count][...] = jnp.zeros((8, 128), F32)
        body(*refs[:given], *blocks, held)
        copies = [
            pltpu.make_async_copy(blocks[i], outs[i].at[pl.ds(layer, 1)], sems.at[i])
            for i in range(count)
        ]
        for copy in copies:
            copy.start()
        for copy in copies:
            copy.wait()

    return pl.pallas_call(
        kernel,
        out_shape=tuple(sds(shape, F32) for shape in shapes) + (sds((8, 128), F32),),
        in_specs=[SMEM] + [VMEM] * (given - 1) + [HBM] * len(before) + [ANY] * len(deps),
        out_specs=(HBM,) * count + (VMEM,),
        scratch_shapes=[pltpu.VMEM((1,) + shape[1:], F32) for shape in shapes]
        + [pltpu.VMEM(scratch, BF16), pltpu.SemaphoreType.DMA((count,))],
        input_output_aliases={given + index: index for index in range(len(before))},
        compiler_params=pltpu.CompilerParams(vmem_limit_bytes=LIMIT),
        cost_estimate=pl.CostEstimate(flops=100000000, bytes_accessed=0, transcendentals=0),
        name=name,
    )(*ins, *before, *deps)


def silu_bf16(condition):
    return (condition * (1.0 / (1.0 + jnp.exp(-condition)))).astype(BF16)


def ada_result(layer, meta, condition, rides, far, ada_weight, before, deps):
    given = () if condition is None else (condition,)
    slots = rides.shape[0] // 16
    half = D // 2

    def kernel(meta, rides, far, ada_hbm, *refs):
        ada_hbm_out, cond_out, known_out, sums_out, own_f32, far_f32, ada, ada_out, sems = refs[-9:]
        load = pltpu.make_async_copy(ada_hbm.at[pl.ds(layer, 1)], ada, sems.at[0])
        load.start()
        for block in range(D // 128):
            lanes = slice(block * 128, (block + 1) * 128)
            own_f32[block, :, :] = rides[:, lanes].astype(F32)
            far_f32[block, :, :] = far[:, lanes].astype(F32)
        first = meta[1] == 0
        grad_cond = jnp.zeros((2 * slots, half), F32)
        load.wait()
        sums_out[...] = jnp.zeros_like(sums_out)

        def latents_row(row):
            mine, other = (
                jnp.concatenate(
                    [held[block, pl.ds(row, slots, stride=16), :] for block in range(D // 128)], axis=1
                )
                for held in (own_f32, far_f32)
            )
            vectors = []
            for one, two in (
                (mine[:, :half], other[:, half:]),
                (mine[:, half:], other[:, :half]),
            ):
                vectors.append(
                    jnp.concatenate([jnp.where(first, one, two), jnp.where(first, two, one)], axis=1)
                )
            return jnp.concatenate(vectors, axis=0)

        if layer == 1:
            known = latents_row(14) + latents_row(15)
            known = jnp.where(meta[0] == 0, known[:, :half], known[:, half:])
            act = silu_bf16(known)
        else:
            known = (latents_row(14) * 32.0 + latents_row(15))[:, :half]
            act = silu_bf16(refs[0][...])
        known_out[...] = known
        for row in range(14):
            both = latents_row(row)
            sums_out[row : row + 1, :] = jnp.sum(both, axis=0, keepdims=True)
            if row < 6:
                cols = slice(row * D, (row + 1) * D)
                both = both.astype(BF16)
                ada_out[0, :, cols] = dot_tn(act, both)
                grad_cond = grad_cond + dot_nt(both, ada[0, :, cols])
        store = pltpu.make_async_copy(ada_out, ada_hbm_out.at[pl.ds(layer, 1)], sems.at[1])
        store.start()
        cond_out[...] = grad_cond
        store.wait()

    shape = ada_weight.shape
    return pl.pallas_call(
        kernel,
        out_shape=(sds(shape, F32),) + (sds((2 * slots, half), F32),) * 2 + (sds((16, D), F32),),
        in_specs=[SMEM, VMEM, VMEM, HBM]
        + [VMEM] * len(given)
        + [HBM] * len(before)
        + [ANY] * len(deps),
        out_specs=(HBM, VMEM, VMEM, VMEM),
        scratch_shapes=[pltpu.VMEM((D // 128, 16 * slots, 128), F32)] * 2
        + [
            pltpu.VMEM((1,) + shape[1:], BF16),
            pltpu.VMEM((1,) + shape[1:], F32),
            pltpu.SemaphoreType.DMA((2,)),
        ],
        input_output_aliases={4 + len(given): 0} if before else {},
        compiler_params=pltpu.CompilerParams(vmem_limit_bytes=LIMIT),
        cost_estimate=pl.CostEstimate(flops=100000000, bytes_accessed=0, transcendentals=0),
        name="ada_result",
    )(meta, rides, far, ada_weight, *given, *before, *deps)


def condition_result(meta, condition, labels, conds, sums, classes, deps):
    half = D // 2

    def body(meta, condition, labels, cond0, cond1, sums0, sums1, *outs):
        table, mine, send, ada, qv, out, up, down = outs
        condition = condition[...]
        sigmoid = 1.0 / (1.0 + jnp.exp(-condition))
        grads = (cond0[...] + cond1[...]) * sigmoid * (1.0 + condition * (1.0 - sigmoid))
        mine[...] = grads[0:1, :]
        send[...] = grads[1:2, :]
        labels = labels[:, 0:1]
        count = -(-classes // 128) * 128
        numbers = lax.broadcasted_iota(jnp.int32, (condition.shape[0], count), 1).astype(F32)
        one_hot = jnp.where(numbers == labels, 1.0, 0.0)
        total = lax.dot_general(
            grads,
            one_hot,
            (((0,), (0,)), ((), ())),
            precision=lax.Precision.HIGHEST,
            preferred_element_type=F32,
        )
        table[...] = total[:, 0:classes]
        low = meta[0] == 0
        for layer, rows in enumerate((sums0, sums1)):
            at = slice(layer, layer + 1)

            def pick(one, two):
                return jnp.where(low, rows[one : one + 1, :], rows[two : two + 1, :])

            for index in range(3):
                ada[at, index * D : (index + 1) * D] = pick(index, index + 3)
            qv[at, :] = pick(6, 7)
            for index in range(2):
                up[at, index * D : (index + 1) * D] = pick(10 + index, 12 + index)
            for ref, row in ((out, 8), (down, 9)):
                value = rows[row : row + 1, :]
                ref[at, :] = jnp.where(low, value[:, :half], value[:, half:])

    shapes = (
        (half, classes),
        (1, half),
        (1, half),
        (LAYERS, 3 * D),
        (LAYERS, D),
        (LAYERS, half),
        (LAYERS, 2 * D),
        (LAYERS, half),
    )
    return call(
        body,
        (meta, condition, labels, *conds, *sums),
        [SMEM] + [VMEM] * 6,
        tuple(sds(shape, F32) for shape in shapes),
        (VMEM,) * len(shapes),
        "condition_result",
        deps=deps,
    )


def both_halves(meta, mine, other):
    def body(meta, mine, other, out):
        low = meta[0] == 0
        a, b = mine[...], other[...]
        out[...] = jnp.concatenate([jnp.where(low, a, b), jnp.where(low, b, a)], axis=1)

    return call(
        body, (meta, mine, other), [SMEM, VMEM, VMEM], sds((1, D), F32), VMEM, "both_halves"
    )


def on_device(reps, *arguments):
    (
        latents,
        timestep_embed,
        labels,
        counts,
        class_table,
        ada_weight,
        ada_bias,
        qkv_weight,
        qv_bias,
        out_weight,
        out_bias,
        up_weight,
        up_bias,
        down_weight,
        down_bias,
        cotangent,
    ) = arguments
    half = D // 2
    rep = lax.axis_index("rep")
    x = lax.axis_index("shard")
    core, y, z = rep & 1, (rep >> 1) & 1, (rep >> 2) & 3
    meta = jnp.stack([x, core, y, z, jnp.minimum(counts[0], 1), z & 1]).astype(jnp.int32)

    def over_x(value):
        return lax.ppermute(value, "shard", [(0, 1), (1, 0)])

    def over_rep(value, distance):
        return lax.ppermute(value, "rep", [(r, r ^ distance) for r in range(reps)])

    CORE, Y, Z = 1, 2, 4

    first = first_message(timestep_embed, labels, ada_bias, qv_bias, out_bias, up_bias, down_bias)
    got_first = over_x(first)
    send_a0, send_m0 = pack(
        0, False, 2, meta, qkv_weight, out_weight, up_weight, down_weight, (), "pack_first"
    )
    classes = class_table.shape[0]
    mine_part, send_part = condition_step(
        meta, first, got_first, class_table, ada_weight, (send_m0,)
    )
    send_a1, send_m1 = pack(
        1, True, 4, meta, qkv_weight, out_weight, up_weight, down_weight, (send_part,), "pack_rest"
    )

    def fetch(send, distance):
        got = over_x(send)
        if distance is None:
            return [got, over_rep(got, CORE)]
        next_got = over_rep(got, distance)
        return [got, next_got, over_rep(got, CORE), over_rep(next_got, CORE)]

    pieces_a0 = fetch(send_a0, None)
    vecs_all = vectors_step(meta, first, got_first, mine_part, over_x(send_part))
    pieces_m0 = fetch(send_m0, Y)
    pieces_a1 = fetch(send_a1, Y)
    pieces_m1 = fetch(send_m1, Z)
    vecs = [vecs_all[layer] for layer in range(LAYERS)]

    distances = [Z]
    while 2 * distances[-1] < reps:
        distances.append(2 * distances[-1])

    stream = latents[0]
    attn_weights = (qkv_weight, out_weight)
    mlp_weights = (up_weight, down_weight)
    *kept_a0, middle0 = attn_fwd(0, False, meta, stream, vecs[0], *attn_weights, pieces_a0)
    stream1, *kept_m0 = mlp_fwd(
        0, False, False, meta, middle0, vecs[0], *mlp_weights, pieces_m0
    )
    *kept_a1, middle1 = attn_fwd(1, False, meta, stream1, vecs[1], *attn_weights, pieces_a1)
    activations, *kept_m1 = mlp_fwd(1, True, True, meta, middle1, vecs[1], *mlp_weights, pieces_m1)

    last = [vecs_all]

    def deps():
        return (last[0],)

    def ran(result):
        last[0] = result[-1] if isinstance(result, (tuple, list)) else result
        return result

    def reduce_chunk(keep, sent, sums):
        got = over_rep(sent, CORE)
        yield
        keep, sent = ran(first_split(meta, keep, got, sums, deps()))
        got = over_x(sent)
        yield
        keep, sent = ran(next_split(2, meta, keep, sent, got, deps()))
        got = over_rep(sent, Y)
        yield
        steps = distances
        if sums is None:
            keep, sent = ran(next_split(5, meta, keep, sent, got, deps()))
            got = over_rep(sent, Z)
            steps = distances[1:]
            yield
        rows = keep.shape[0]
        for distance in steps:
            (sent,) = ran(add_join(keep, sent, got, rows, False, deps()))
            keep = sent
            got = over_rep(sent, distance)
            yield
        mine, *rides = ran(add_join(keep, sent, got, rows, True, deps()))
        if sums is None:
            got = over_rep(mine, Z)
            yield
            mine = ran(join(meta, mine, got, deps()))
        next_mine = over_rep(mine, Y)
        result = (mine, next_mine, over_rep(mine, CORE), over_rep(next_mine, CORE))
        if rides:
            rides = (rides[0], over_rep(rides[0], CORE))
        yield result, rides

    def advance(chunk, times=1):
        result = None
        for _ in range(times):
            result = next(chunk)
        return result

    more = len(distances) - 1

    keep, sent, grad, part_sums = mlp_bwd(
        1, True, True, meta, cotangent[0], vecs[1], (middle1, *kept_m1), *mlp_weights, pieces_m1, deps()
    )
    m1 = reduce_chunk(keep, sent, None)
    advance(m1)
    keep, sent, grad, sums1 = ran(
        attn_bwd(
            1, False, 16, meta, grad, vecs[1], stream1, kept_a1, part_sums, *attn_weights, pieces_a1
        )
    )
    a1 = reduce_chunk(keep, sent, sums1)
    advance(a1)
    advance(m1)
    keep, sent, grad, part_sums = ran(
        mlp_bwd(
            0, False, False, meta, grad, vecs[0], (middle0, *kept_m0), *mlp_weights, pieces_m0, deps()
        )
    )
    m0 = reduce_chunk(keep, sent, None)
    advance(m0)
    advance(a1)
    keep, sent, grad_stream, sums0 = ran(
        attn_bwd(
            0,
            False,
            16,
            meta,
            grad,
            vecs[0],
            stream,
            kept_a0,
            part_sums,
            *attn_weights,
            pieces_a0,
            deps(),
        )
    )
    a0 = reduce_chunk(keep, sent, sums0)
    advance(a0)
    for chunk in (m1, m0, a1, a0, m1, a1):
        advance(chunk)
    advance(m1, more)
    advance(m0)
    advance(a1, more)
    advance(a0)
    advance(m1)
    advance(m0)
    advance(a0)
    result_m1, _ = advance(m1)
    advance(m0, more)
    result_a1, rides1 = advance(a1)
    advance(a0, more)
    ada_grad, cond1, condition, sums1 = ran(ada_result(1, meta, None, *rides1, ada_weight, (), deps()))
    advance(m0)
    *mlp_grads, _ = ran(mlp_result(1, meta, result_m1, (), deps()))
    *attn_grads, _ = ran(attn_result(1, meta, result_a1, (), deps()))
    result_a0, rides0 = advance(a0)
    result_m0, _ = advance(m0)
    ada_grad, cond0, labels_all, sums0 = ran(
        ada_result(0, meta, condition, *rides0, ada_weight, (ada_grad,), deps())
    )
    table_grad, mine_cond, send_cond, *bias_grads = ran(
        condition_result(
            meta, condition, labels_all, (cond0, cond1), (sums0, sums1), classes, deps()
        )
    )
    other_cond = over_x(send_cond)
    qkv_grad, out_grad, _ = ran(attn_result(0, meta, result_a0, attn_grads, deps()))
    up_grad, down_grad, _ = ran(mlp_result(0, meta, result_m0, mlp_grads, deps()))
    cond_grad = both_halves(meta, mine_cond, other_cond)
    ada_b, qv_b, out_b, up_b, down_b = bias_grads

    return (
        activations[None],
        grad_stream[None],
        cond_grad,
        table_grad.T,
        ada_grad,
        ada_b,
        qkv_grad,
        qv_b,
        out_grad,
        out_b,
        up_grad,
        up_b,
        down_grad,
        down_b,
    )


def solution(mesh):
    reps = mesh.shape["rep"]
    both = ("rep", "shard")
    in_specs = (
        P(both, None, None),
        P(both, None),
        P(both),
        P(both),
        P(None, "shard"),
    ) + (P(None, "shard", None), P(None, "shard")) * 5 + (P(both, None, None),)
    out_specs = (
        P(both, None, None),
        P(both, None, None),
        P(both, None),
        P(None, "shard"),
    ) + (P(None, "shard", None), P(None, "shard")) * 5
    return jax.shard_map(
        functools.partial(on_device, reps),
        mesh=mesh,
        in_specs=in_specs,
        out_specs=out_specs,
        check_vma=False,
    )
```

```python
import functools
import math

import jax
import jax.numpy as jnp
from jax import lax
from jax.experimental import pallas as pl
from jax.experimental.pallas import tpu as pltpu
from jax.sharding import PartitionSpec as P

D = 384
HEAD_DIM = 64
LAYERS = 2
F32 = jnp.float32
BF16 = jnp.bfloat16

norm_eps = 1e-06
gelu_coeff = math.sqrt(2.0 / math.pi)
gelu_cubic = 0.044715

VMEM = pl.BlockSpec(memory_space=pltpu.VMEM)
SMEM = pl.BlockSpec(memory_space=pltpu.SMEM)
ANY = pl.BlockSpec(memory_space=pl.ANY)
HBM = pl.BlockSpec(memory_space=pltpu.HBM)
LIMIT = 16 * 1024 * 1024
SMALL = 8 * 1024 * 1024
WIDE = 56 * 1024 * 1024


def sds(shape, dtype):
    return jax.ShapeDtypeStruct(shape, dtype)


def norm_rows(values):
    centered = values - jnp.mean(values, axis=-1, keepdims=True)
    inv_dev = lax.rsqrt(jnp.mean(centered * centered, axis=-1, keepdims=True) + norm_eps)
    return (centered * inv_dev, inv_dev)


def norm_back(grad_normed, normed, inv_dev):
    return (
        grad_normed
        - jnp.mean(grad_normed, axis=-1, keepdims=True)
        - normed * jnp.mean(grad_normed * normed, axis=-1, keepdims=True)
    ) * inv_dev


def gelu_parts(pre_act):
    square = pre_act * pre_act
    inner_arg = gelu_coeff * pre_act * (1.0 + gelu_cubic * square)
    tanh_val = jnp.tanh(inner_arg)
    half_up = 0.5 * (1.0 + tanh_val)
    value_out = pre_act * half_up
    slope_out = half_up + 0.5 * pre_act * (1.0 - tanh_val * tanh_val) * (
        gelu_coeff + (3.0 * gelu_cubic * gelu_coeff) * square
    )
    return (value_out, slope_out)


def dot(a, b):
    return jnp.dot(a, b, preferred_element_type=F32)


def dot_nt(a, b):
    return lax.dot_general(a, b, (((1,), (1,)), ((), ())), preferred_element_type=F32)


def dot_tn(a, b):
    return lax.dot_general(a, b, (((0,), (0,)), ((), ())), preferred_element_type=F32)


def head_masks():
    lane = lax.broadcasted_iota(jnp.int32, (1, 2 * HEAD_DIM), 1)
    first = lane < HEAD_DIM
    return first, jnp.logical_not(first)


def keep_lanes(values, mask):
    return jnp.where(mask, values, jnp.zeros_like(values))


def rows_of(start, size):
    return pl.ds(pl.multiple_of(start, 16), size)


def attn_weight_copies(meta, layer, qkv_hbm, out_hbm, pieces, offsets, w_qkv, w_out, sems):
    half = qkv_hbm.shape[1]
    x = meta[0]
    copies = [
        (qkv_hbm.at[layer], w_qkv.at[rows_of(x * half, half), :]),
        (out_hbm.at[layer], w_out.at[rows_of(x * half, half), :]),
    ]
    for piece, offset in zip(pieces, offsets):
        size = piece.shape[0]
        start = (1 - x) * half + offset * size
        copies.append((piece.at[:, pl.ds(0, 3 * D)], w_qkv.at[rows_of(start, size), :]))
        copies.append((piece.at[:, pl.ds(3 * D, D)], w_out.at[rows_of(start, size), :]))
    return [pltpu.make_async_copy(s, d, sems.at[i]) for i, (s, d) in enumerate(copies)]


def mlp_weight_copies(meta, layer, up_hbm, down_hbm, pieces, offsets, w_up, w_down, sems):
    half = up_hbm.shape[1]
    tall = down_hbm.shape[1]
    blocks = tall // half
    x = meta[0]
    copies = [
        (up_hbm.at[layer], w_up.at[rows_of(x * half, half), :]),
        (down_hbm.at[layer], w_down.at[rows_of(x * tall, tall), :]),
    ]
    count = len(pieces) // 2
    for up_piece, down_piece, offset in zip(pieces[:count], pieces[count:], offsets):
        size = up_piece.shape[0]
        start = (1 - x) * half + offset * size
        copies.append((up_piece, w_up.at[rows_of(start, size), :]))
        for b in range(blocks):
            start = (1 - x) * tall + offset * (blocks * size) + b * size
            copies.append((down_piece.at[:, pl.ds(b * D, D)], w_down.at[rows_of(start, size), :]))
    return [pltpu.make_async_copy(s, d, sems.at[i]) for i, (s, d) in enumerate(copies)]


def piece_offsets(meta, count, far):
    core, y, z = meta[1], meta[2], meta[3]
    if count == 2:
        return [core, 1 - core]
    near = z % 2 if far else y
    return [
        near * 2 + core,
        (1 - near) * 2 + core,
        near * 2 + (1 - core),
        (1 - near) * 2 + (1 - core),
    ]


def call(body, ins, in_specs, out_shape, out_specs, name, scratch=(), deps=(), limit=SMALL, **more):
    given, late = len(ins), len(deps)

    def kernel(*refs):
        body(*refs[:given], *refs[given + late :])

    return pl.pallas_call(
        kernel,
        out_shape=out_shape,
        in_specs=list(in_specs) + [ANY] * late,
        out_specs=out_specs,
        scratch_shapes=list(scratch),
        compiler_params=pltpu.CompilerParams(vmem_limit_bytes=limit),
        cost_estimate=pl.CostEstimate(flops=10000000000, bytes_accessed=0, transcendentals=0),
        name=name,
        **more,
    )(*ins, *deps)


def pack_attn_copies(send, layer, parts, offset, qkv, out):
    size = qkv.shape[1] // parts
    rows = rows_of(offset * size, size)
    return [
        (qkv.at[layer, rows, :], send.at[:, pl.ds(0, 3 * D)]),
        (out.at[layer, rows, :], send.at[:, pl.ds(3 * D, D)]),
    ]


def pack_mlp_copies(send_up, send_down, layer, offset, up, down):
    size = up.shape[1] // 4
    blocks = down.shape[1] // up.shape[1]
    copies = [(up.at[layer, rows_of(offset * size, size), :], send_up)]
    for b in range(blocks):
        rows = rows_of(offset * (blocks * size) + b * size, size)
        copies.append((down.at[layer, rows, :], send_down.at[:, pl.ds(b * D, D)]))
    return copies


def pack(layer, far, parts, meta, qkv, out, up, down, deps, name):
    half = qkv.shape[1]
    size = half // 4

    def body(meta, qkv, out, up, down, send_attn, send_up, send_down, sems):
        copies = pack_attn_copies(send_attn, layer, parts, piece_offsets(meta, parts, False)[0], qkv, out)
        copies += pack_mlp_copies(send_up, send_down, layer, piece_offsets(meta, 4, far)[0], up, down)
        copies = [pltpu.make_async_copy(s, d, sems.at[i]) for i, (s, d) in enumerate(copies)]
        for copy in copies:
            copy.start()
        for copy in copies:
            copy.wait()

    return call(
        body,
        (meta, qkv, out, up, down),
        [SMEM] + [HBM] * 4,
        (sds((half // parts, 4 * D), BF16),) + (sds((size, 4 * D), BF16),) * 2,
        (VMEM,) * 3,
        name,
        scratch=[pltpu.SemaphoreType.DMA((8,))],
        deps=deps,
        limit=WIDE,
    )


def first_messages(meta, timestep, labels, biases, qkv, out, up, down):
    ins = (timestep,) + biases
    half = qkv.shape[1]

    def body(meta, labels, *refs):
        small, weights, outs, held, sems = refs[:6], refs[6:10], refs[10:14], refs[14:20], refs[20]
        send, send_attn, send_up, send_down = outs
        pairs = list(zip(small, held))
        pairs += pack_attn_copies(send_attn, 0, 2, piece_offsets(meta, 2, False)[0], *weights[:2])
        pairs += pack_mlp_copies(
            send_up, send_down, 0, piece_offsets(meta, 4, False)[0], *weights[2:]
        )
        copies = [pltpu.make_async_copy(s, d, sems.at[i]) for i, (s, d) in enumerate(pairs)]
        for copy in copies:
            copy.start()
        send[...] = jnp.zeros_like(send)
        send[4:5, D : D + 128] = jnp.full((1, 128), labels[0], jnp.int32).astype(F32)
        for copy in copies[:6]:
            copy.wait()
        time, ada, qv, out_b, up_b, down_b = held
        send[0:2, 0 : 3 * D] = ada[...].astype(F32)
        send[0:2, 3 * D : 4 * D] = qv[...].astype(F32)
        send[2:4, 0 : 2 * D] = up_b[...].astype(F32)
        send[2:4, 2 * D : 2 * D + D // 2] = out_b[...].astype(F32)
        send[2:4, 1024 : 1024 + D // 2] = down_b[...].astype(F32)
        send[4:5, 0:D] = time[...]
        for copy in copies[6:]:
            copy.wait()

    return call(
        body,
        (meta, labels) + ins + (qkv, out, up, down),
        [SMEM, SMEM] + [HBM] * 10,
        (sds((8, 4 * D), F32), sds((half // 2, 4 * D), BF16)) + (sds((half // 4, 4 * D), BF16),) * 2,
        (VMEM,) * 4,
        "first_messages",
        scratch=[pltpu.VMEM(member.shape, member.dtype) for member in ins]
        + [pltpu.SemaphoreType.DMA((16,))],
        limit=WIDE,
    )


def condition_kernel(meta, own, got, table_ref, ada, mine_out, send_out, table):
    half = D // 2
    x = meta[0]
    classes = table_ref.shape[1]
    aligned = classes // 128 * 128
    table[:, aligned:] = jnp.zeros((half, table.shape[1] - aligned), BF16)
    table[:, 0:classes] = table_ref[...]
    row = lax.broadcasted_iota(jnp.int32, (8, 1), 0)
    timestep = jnp.where(row == 0, own[4:5, 0:D], got[4:5, 0:D])
    label = jnp.where(row == 0, own[4:5, D : D + 1], got[4:5, D : D + 1])
    timestep = jnp.where(x == 0, timestep[:, :half], timestep[:, half:])
    classes = lax.broadcasted_iota(jnp.int32, (8, table.shape[1]), 1).astype(F32)
    one_hot = jnp.where(classes == label, 1.0, 0.0).astype(BF16)
    condition = timestep + dot_nt(one_hot, table[...])
    act = (condition * (1.0 / (1.0 + jnp.exp(-condition)))).astype(BF16)
    for ref, index in ((mine_out, 0), (send_out, 1)):
        ref[2:3, 0:half] = condition[index : index + 1, :]
        ref[2:3, half:] = jnp.zeros((1, 6 * D - half), F32)
    for layer in range(LAYERS):
        part = dot(act, ada[layer])
        mine_out[layer : layer + 1, :] = part[0:1, :]
        send_out[layer : layer + 1, :] = part[1:2, :]


def condition_step(meta, own, got, table, ada, deps):
    return call(
        condition_kernel,
        (meta, own, got, table.T, ada),
        [SMEM] + [VMEM] * 4,
        (sds((LAYERS + 1, 6 * D), F32),) * 2,
        (VMEM,) * 2,
        "condition",
        scratch=[pltpu.VMEM((D // 2, -(-table.shape[0] // 128) * 128), BF16)],
        deps=deps,
    )


def vectors_kernel(meta, own, got, mine_part, got_part, out):
    x = meta[0]
    low = jnp.where(x == 0, own[...], got[...])
    high = jnp.where(x == 0, got[...], own[...])
    modul = mine_part[...] + got_part[...]
    half = D // 2
    mine_cond, got_cond = mine_part[2:3, 0:half], got_part[2:3, 0:half]
    condition = jnp.concatenate(
        [jnp.where(x == 0, mine_cond, got_cond), jnp.where(x == 0, got_cond, mine_cond)], axis=1
    )
    label = jnp.broadcast_to(own[4:5, D : D + 1], (1, D))
    for layer in range(LAYERS):
        out[layer, 14:15, :] = condition
        out[layer, 15:16, :] = label
        rows = slice(layer, layer + 1)
        for member in range(6):
            side = low if member < 3 else high
            col = (member % 3) * D
            out[layer, member : member + 1, :] = (
                modul[rows, member * D : (member + 1) * D] + side[rows, col : col + D]
            )
        out[layer, 6:7, :] = low[rows, 3 * D : 4 * D]
        out[layer, 7:8, :] = high[rows, 3 * D : 4 * D]
        rows = slice(2 + layer, 3 + layer)
        for index, start in ((8, 2 * D), (9, 1024)):
            out[layer, index : index + 1, :] = jnp.concatenate(
                [low[rows, start : start + half], high[rows, start : start + half]], axis=1
            )
        for index, side, col in ((10, low, 0), (11, low, D), (12, high, 0), (13, high, D)):
            out[layer, index : index + 1, :] = side[rows, col : col + D]


def vectors_step(meta, own, got, mine_part, got_part):
    return call(
        vectors_kernel,
        (meta, own, got, mine_part, got_part),
        [SMEM] + [VMEM] * 4,
        sds((LAYERS, 16, D), F32),
        VMEM,
        "vectors",
    )


def attn_fwd_kernel(layer, far, count, *refs):
    meta, x_ref, vecs, qkv_hbm, out_hbm = refs[:5]
    pieces = refs[5 : 5 + count]
    modulated_out, qkv_out, prob_out, att_out, branch_out, w_qkv, w_out, middle_out = refs[
        5 + count : 13 + count
    ]
    sems = refs[13 + count]
    copies = attn_weight_copies(
        meta, layer, qkv_hbm, out_hbm, pieces, piece_offsets(meta, count, far), w_qkv, w_out, sems
    )
    for copy in copies:
        copy.start()
    stream = x_ref[...].astype(F32)
    normed, _ = norm_rows(stream)
    modulated = (normed * (1.0 + vecs[1:2, :]) + vecs[0:1, :]).astype(BF16)
    modulated_out[...] = modulated
    for copy in copies:
        copy.wait()
    for part in range(3):
        cols = slice(part * D, (part + 1) * D)
        value = dot(modulated, w_qkv[:, cols])
        if part == 0:
            value = value + vecs[6:7, :]
        if part == 2:
            value = value + vecs[7:8, :]
        qkv_out[:, cols] = value.astype(BF16)
    masks = head_masks()
    tokens = stream.shape[0]
    for pair in range(D // (2 * HEAD_DIM)):
        lanes = slice(pair * 2 * HEAD_DIM, (pair + 1) * 2 * HEAD_DIM)
        query = qkv_out[:, lanes]
        key = qkv_out[:, pair * 128 + D : (pair + 1) * 128 + D]
        value = qkv_out[:, pair * 128 + 2 * D : (pair + 1) * 128 + 2 * D]
        attended = None
        for member in range(2):
            head = 2 * pair + member
            scores = dot_nt(query, keep_lanes(key, masks[member])) * HEAD_DIM ** (-0.5)
            top = jnp.max(scores, axis=-1, keepdims=True)
            expo = jnp.exp(scores - top)
            prob = (expo * (1.0 / jnp.sum(expo, axis=-1, keepdims=True))).astype(BF16)
            prob_out[head * tokens : (head + 1) * tokens, :] = prob
            part = dot(prob, keep_lanes(value, masks[member]))
            attended = part if attended is None else attended + part
        att_out[:, lanes] = attended.astype(BF16)
    branch = dot(att_out[...], w_out[...]) + vecs[8:9, :]
    branch_out[...] = branch
    middle_out[...] = stream + vecs[2:3, :] * branch


def attn_fwd(layer, far, meta, x, vecs, qkv, out, pieces):
    tokens = x.shape[0]
    count = len(pieces)
    heads = D // HEAD_DIM
    return pl.pallas_call(
        functools.partial(attn_fwd_kernel, layer, far, count),
        out_shape=(
            sds((tokens, D), BF16),
            sds((tokens, 3 * D), BF16),
            sds((heads * tokens, tokens), BF16),
            sds((tokens, D), BF16),
            sds((tokens, D), F32),
            sds((D, 3 * D), BF16),
            sds((D, D), BF16),
            sds((tokens, D), F32),
        ),
        in_specs=[SMEM, VMEM, VMEM] + [HBM] * 2 + [ANY] * count,
        out_specs=(VMEM,) * 8,
        scratch_shapes=[
            pltpu.SemaphoreType.DMA((2 + 2 * count,)),
        ],
        compiler_params=pltpu.CompilerParams(vmem_limit_bytes=LIMIT),
        cost_estimate=pl.CostEstimate(flops=10000000000, bytes_accessed=0, transcendentals=0),
        name="attn_fwd",
    )(meta, x, vecs, qkv, out, *pieces)


def mlp_fwd_kernel(layer, far, count, last, late, *refs):
    refs = refs[:3] + refs[3 + late :]
    meta, middle_ref, vecs, up_hbm, down_hbm = refs[:5]
    pieces = refs[5 : 5 + count]
    x_out, mod_out, act_out, slope_out, branch_out, w_up, w_down, sems = refs[5 + count :]
    copies = mlp_weight_copies(
        meta, layer, up_hbm, down_hbm, pieces, piece_offsets(meta, count // 2, far), w_up, w_down, sems
    )
    for copy in copies:
        copy.start()
    middle = middle_ref[...]
    normed, _ = norm_rows(middle)
    mod_two = (normed * (1.0 + vecs[4:5, :]) + vecs[3:4, :]).astype(BF16)
    mod_out[...] = mod_two
    for copy in copies:
        copy.wait()
    branch = None
    for part in range(4):
        cols = slice(part * D, (part + 1) * D)
        pre_act = dot(mod_two, w_up[:, cols]) + vecs[10 + part : 11 + part, :]
        value, slope = gelu_parts(pre_act)
        value = value.astype(BF16)
        act_out[:, cols] = value
        slope_out[:, cols] = slope.astype(BF16)
        term = dot(value, w_down[cols, :])
        branch = term if branch is None else branch + term
    branch = branch + vecs[9:10, :]
    branch_out[...] = branch
    result = middle + vecs[5:6, :] * branch
    if last:
        live = meta[4].astype(F32)
        result = result * live
    x_out[...] = result.astype(x_out.dtype)


def mlp_fwd(layer, far, last, meta, middle, vecs, up, down, pieces, deps=()):
    tokens = middle.shape[0]
    count = len(pieces)
    return pl.pallas_call(
        functools.partial(mlp_fwd_kernel, layer, far, count, last, len(deps)),
        out_shape=(
            sds((tokens, D), BF16 if last else F32),
            sds((tokens, D), BF16),
            sds((tokens, 4 * D), BF16),
            sds((tokens, 4 * D), BF16),
            sds((tokens, D), F32),
            sds((D, 4 * D), BF16),
            sds((4 * D, D), BF16),
        ),
        in_specs=[SMEM, VMEM, VMEM] + [ANY] * len(deps) + [HBM] * 2 + [ANY] * count,
        out_specs=(VMEM,) * 7,
        scratch_shapes=[
            pltpu.SemaphoreType.DMA((2 + 5 * count,)),
        ],
        compiler_params=pltpu.CompilerParams(vmem_limit_bytes=LIMIT),
        cost_estimate=pl.CostEstimate(flops=10000000000, bytes_accessed=0, transcendentals=0),
        name="mlp_fwd",
    )(meta, middle, vecs, *deps, up, down, *pieces)


def split_store(core, value, half, keep, send, rows):
    @pl.when(core == half)
    def _():
        keep[rows, :] = value

    @pl.when(core != half)
    def _():
        send[rows, :] = value


def mlp_bwd_kernel(masked, late, *refs):
    meta, grad_ref, vecs, middle_ref, branch_ref, act_ref, slope_ref, mod_ref, w_up, w_down = refs[:10]
    keep, send, grad_out, sums_out = refs[10 + late :]
    core = meta[1]
    grad = grad_ref[...].astype(F32)
    if masked:
        grad = grad * meta[4].astype(F32)
    sums_out[...] = jnp.zeros_like(sums_out)
    sums_out[5:6, :] = jnp.sum(grad * branch_ref[...], axis=0, keepdims=True)
    grad_branch = grad * vecs[5:6, :]
    sums_out[9:10, :] = jnp.sum(grad_branch, axis=0, keepdims=True)
    branch_bf = grad_branch.astype(BF16)
    half = D // 2
    for part in range(4):
        value = dot_tn(act_ref[:, part * D : (part + 1) * D], branch_bf).astype(BF16)
        base = (part // 2) * 4 * half + 2 * half
        split_store(core, value, part % 2, keep, send, slice(base, base + D))
    mod_two = mod_ref[...]
    grad_mod = None
    for part in range(4):
        cols = slice(part * D, (part + 1) * D)
        grad_pre = dot_nt(branch_bf, w_down[cols, :]) * slope_ref[:, cols].astype(F32)
        sums_out[10 + part : 11 + part, :] = jnp.sum(grad_pre, axis=0, keepdims=True)
        pre = grad_pre.astype(BF16)
        value = dot_tn(mod_two, pre).astype(BF16)
        for side in range(2):
            base = side * 4 * half + (part % 2) * half
            split_store(
                core,
                value[side * half : (side + 1) * half, :],
                part // 2,
                keep,
                send,
                slice(base, base + half),
            )
        term = dot_nt(pre, w_up[:, cols])
        grad_mod = term if grad_mod is None else grad_mod + term
    normed, inv_dev = norm_rows(middle_ref[...])
    sums_out[3:4, :] = jnp.sum(grad_mod, axis=0, keepdims=True)
    sums_out[4:5, :] = jnp.sum(grad_mod * normed, axis=0, keepdims=True)
    grad_out[...] = grad + norm_back(grad_mod * (1.0 + vecs[4:5, :]), normed, inv_dev)


def mlp_bwd(masked, meta, grad, vecs, kept, deps=()):
    middle, mod_two, act, slope, branch, w_up, w_down = kept
    tokens = middle.shape[0]
    late = len(deps)
    return pl.pallas_call(
        functools.partial(mlp_bwd_kernel, masked, late),
        out_shape=(
            sds((4 * D, D), BF16),
            sds((4 * D, D), BF16),
            sds((tokens, D), F32),
            sds((16, D), F32),
        ),
        in_specs=[SMEM] + [VMEM] * 9 + [ANY] * late,
        out_specs=(VMEM,) * 4,
        compiler_params=pltpu.CompilerParams(vmem_limit_bytes=LIMIT),
        cost_estimate=pl.CostEstimate(flops=10000000000, bytes_accessed=0, transcendentals=0),
        name="mlp_bwd",
    )(meta, grad, vecs, middle, branch, act, slope, mod_two, w_up, w_down, *deps)


def attn_bwd_kernel(layer, extra, late, *refs):
    meta, grad_ref, vecs, x_ref, modulated_ref, qkv_ref, prob_ref, att_ref, branch_ref = refs[:9]
    w_qkv, w_out, part_sums = refs[9:12]
    keep, send, grad_out, sums_out, ga_ref, proj_ref = refs[12 + late :]
    core = meta[1]
    half = D // 2
    tokens = grad_ref.shape[0]
    sums = {}
    grad = grad_ref[...]
    sums[2] = jnp.sum(grad * branch_ref[...], axis=0, keepdims=True)
    grad_battn = grad * vecs[2:3, :]
    sums[8] = jnp.sum(grad_battn, axis=0, keepdims=True)
    battn_bf = grad_battn.astype(BF16)

    def store(value, block):
        for side in range(2):
            base = side * 2 * half + (block % 2) * half
            split_store(
                core,
                value[side * half : (side + 1) * half, :],
                block // 2,
                keep,
                send,
                slice(base, base + half),
            )

    store(dot_tn(att_ref[...], battn_bf).astype(BF16), 3)
    ga_ref[...] = dot_nt(battn_bf, w_out[...]).astype(BF16)
    masks = head_masks()
    grad_q_sums, grad_v_sums = [], []
    for pair in range(D // (2 * HEAD_DIM)):
        lanes = slice(pair * 128, (pair + 1) * 128)
        query = qkv_ref[:, lanes]
        key = qkv_ref[:, pair * 128 + D : (pair + 1) * 128 + D]
        value = qkv_ref[:, pair * 128 + 2 * D : (pair + 1) * 128 + 2 * D]
        grad_att = ga_ref[:, lanes]
        grad_q = grad_k = grad_v = None
        for member in range(2):
            head = 2 * pair + member
            mask = masks[member]
            prob_bf = prob_ref[head * tokens : (head + 1) * tokens, :]
            prob = prob_bf.astype(F32)
            grad_prob = dot_nt(grad_att, keep_lanes(value, mask))
            term_v = dot_tn(prob_bf, keep_lanes(grad_att, mask))
            weighted = prob * grad_prob
            row_dot = jnp.sum(weighted, axis=-1, keepdims=True)
            grad_scores = ((weighted - prob * row_dot) * HEAD_DIM ** (-0.5)).astype(BF16)
            term_q = dot(grad_scores, keep_lanes(key, mask))
            term_k = dot_tn(grad_scores, keep_lanes(query, mask))
            grad_q = term_q if grad_q is None else grad_q + term_q
            grad_k = term_k if grad_k is None else grad_k + term_k
            grad_v = term_v if grad_v is None else grad_v + term_v
        grad_q_sums.append(jnp.sum(grad_q, axis=0, keepdims=True))
        grad_v_sums.append(jnp.sum(grad_v, axis=0, keepdims=True))
        proj_ref[:, lanes] = grad_q.astype(BF16)
        proj_ref[:, pair * 128 + D : (pair + 1) * 128 + D] = grad_k.astype(BF16)
        proj_ref[:, pair * 128 + 2 * D : (pair + 1) * 128 + 2 * D] = grad_v.astype(BF16)
    sums[6] = jnp.concatenate(grad_q_sums, axis=1)
    sums[7] = jnp.concatenate(grad_v_sums, axis=1)
    modulated = modulated_ref[...]
    for block in range(3):
        store(dot_tn(modulated, proj_ref[:, block * D : (block + 1) * D]).astype(BF16), block)
    grad_mod = dot_nt(proj_ref[...], w_qkv[...])
    normed, inv_dev = norm_rows(x_ref[...].astype(F32))
    sums[0] = jnp.sum(grad_mod, axis=0, keepdims=True)
    sums[1] = jnp.sum(grad_mod * normed, axis=0, keepdims=True)
    grad_out[...] = grad + norm_back(grad_mod * (1.0 + vecs[1:2, :]), normed, inv_dev)
    if layer == 1:
        high = vecs[14:15, :].astype(BF16).astype(F32)
        sums[14], sums[15] = high, vecs[14:15, :] - high
    else:
        high = jnp.floor(vecs[15:16, :] * (1.0 / 32.0))
        sums[14], sums[15] = high, vecs[15:16, :] - high * 32.0
    row = lax.broadcasted_iota(jnp.int32, (16, 1), 0)
    total = part_sums[...]
    for index, value in sums.items():
        total = jnp.where(row == index, value, total)
    total = total.astype(BF16)
    sums_out[...] = total
    if extra:
        send[4 * half : 4 * half + 16, :] = total


def attn_bwd(layer, extra, meta, grad, vecs, x, kept, part_sums, deps=()):
    modulated, qkv_val, prob, att, branch, w_qkv, w_out = kept
    tokens = x.shape[0]
    late = len(deps)
    return pl.pallas_call(
        functools.partial(attn_bwd_kernel, layer, extra, late),
        out_shape=(
            sds((2 * D, D), BF16),
            sds((2 * D + extra, D), BF16),
            sds((tokens, D), F32),
            sds((16, D), BF16),
        ),
        in_specs=[SMEM] + [VMEM] * 11 + [ANY] * late,
        out_specs=(VMEM,) * 4,
        scratch_shapes=[pltpu.VMEM((tokens, D), BF16), pltpu.VMEM((tokens, 3 * D), BF16)],
        compiler_params=pltpu.CompilerParams(vmem_limit_bytes=LIMIT),
        cost_estimate=pl.CostEstimate(flops=10000000000, bytes_accessed=0, transcendentals=0),
        name="attn_bwd",
    )(meta, grad, vecs, x, modulated, qkv_val, prob, att, branch, w_qkv, w_out, part_sums, *deps)


def add_rows(a, a_rows, b, b_rows):
    return (a[a_rows, :].astype(F32) + b[b_rows, :].astype(F32)).astype(BF16)


def first_split(meta, keep, got, sums, deps):
    half = keep.shape[0] // 2
    extra = 0 if sums is None else sums.shape[0]

    def body(meta, keep, got, *refs):
        mine_out, send_out = refs[-2:]
        x = meta[0]
        mine, other = rows_of(x * half, half), rows_of((1 - x) * half, half)
        mine_out[...] = add_rows(keep, mine, got, mine)
        send_out[0:half, :] = add_rows(keep, other, got, other)
        if extra:
            own, far = refs[0][...], got[2 * half : 2 * half + extra, :]
            lanes = D // 2
            low = jnp.concatenate([own[:, :lanes], far[:, :lanes]], axis=1)
            high = jnp.concatenate([own[:, lanes:], far[:, lanes:]], axis=1)
            send_out[half : half + extra, :] = jnp.where(meta[1] == 0, low, high)

    rides = () if sums is None else (sums,)
    return call(
        body,
        (meta, keep, got) + rides,
        [SMEM] + [VMEM] * (2 + len(rides)),
        (sds((half, D), BF16), sds((half + extra, D), BF16)),
        (VMEM, VMEM),
        "first_split",
        deps=deps,
    )


def next_split(axis, meta, keep, sent, got, deps):
    whole = keep.shape[0]
    half = whole // 2
    extra = got.shape[0] - whole

    def body(meta, keep, sent, got, mine_out, send_out):
        place = meta[axis]
        mine, other = rows_of(place * half, half), rows_of((1 - place) * half, half)
        mine_out[...] = add_rows(keep, mine, got, mine)
        send_out[0:half, :] = add_rows(keep, other, got, other)
        if extra:
            send_out[half : half + extra, :] = sent[whole : whole + extra, :]
            send_out[half + extra : half + 2 * extra, :] = got[whole : whole + extra, :]

    return call(
        body,
        (meta, keep, sent, got),
        [SMEM] + [VMEM] * 3,
        (sds((half, D), BF16), sds((half + 2 * extra, D), BF16)),
        (VMEM, VMEM),
        "next_split",
        deps=deps,
    )


def add_join(keep, sent, got, rows, last, deps):
    extra = got.shape[0] - rows

    def body(keep, sent, got, *outs):
        everything = slice(0, rows)
        outs[0][0:rows, :] = add_rows(keep, everything, got, everything)
        if extra:
            out, start = (outs[1], 0) if last else (outs[0], rows)
            out[start : start + extra, :] = sent[rows : rows + extra, :]
            out[start + extra : start + 2 * extra, :] = got[rows : rows + extra, :]

    out_shape = (sds((rows + (0 if last else 2 * extra), D), BF16),)
    if last and extra:
        out_shape = out_shape + (sds((2 * extra, D), BF16),)
    return call(
        body,
        (keep, sent, got),
        [VMEM] * 3,
        out_shape,
        (VMEM,) * len(out_shape),
        "add_join",
        deps=deps,
    )


def join(meta, mine, got, deps):
    rows = mine.shape[0]

    def body(meta, mine, got, out):
        low = meta[5]
        out[rows_of(low * rows, rows), :] = mine[...]
        out[rows_of((1 - low) * rows, rows), :] = got[...]

    return call(
        body, (meta, mine, got), [SMEM, VMEM, VMEM], sds((2 * rows, D), BF16), VMEM, "join", deps=deps
    )


def gather_rows(meta, refs, scratch):
    core, y = meta[1], meta[2]
    rows = refs[0].shape[0]
    for index, (c, v) in enumerate(((core, y), (core, 1 - y), (1 - core, y), (1 - core, 1 - y))):
        scratch[c, rows_of(v * rows, rows), :] = refs[index][...]


def attn_result(layer, meta, parts, before, deps):
    half = D // 2

    def body(meta, *refs):
        qkv_out, out_out, scratch = refs[-3:]
        gather_rows(meta, refs[:4], scratch)
        for block in range(4):
            value = scratch[block // 2, (block % 2) * half : (block % 2 + 1) * half, :].astype(F32)
            if block < 3:
                qkv_out[0, :, block * D : (block + 1) * D] = value
            else:
                out_out[0, :, :] = value

    return result_call(
        body,
        (meta, *parts),
        before,
        ((LAYERS, half, 3 * D), (LAYERS, half, D)),
        layer,
        (2, 2 * half, D),
        "attn_result",
        deps,
    )


def mlp_result(layer, meta, parts, before, deps):
    half = D // 2

    def body(meta, *refs):
        up_out, down_out, scratch = refs[-3:]
        gather_rows(meta, refs[:4], scratch)
        for block in range(4):
            value = scratch[block // 2, (block % 2) * half : (block % 2 + 1) * half, :].astype(F32)
            up_out[0, :, block * D : (block + 1) * D] = value
        for core in range(2):
            down_out[0, core * D : (core + 1) * D, :] = scratch[core, D : 2 * D, :].astype(F32)

    return result_call(
        body,
        (meta, *parts),
        before,
        ((LAYERS, half, 4 * D), (LAYERS, 2 * D, D)),
        layer,
        (2, 2 * D, D),
        "mlp_result",
        deps,
    )


def result_call(body, ins, before, shapes, layer, scratch, name, deps):
    given, count = len(ins), len(shapes)

    def kernel(*refs):
        rest = refs[given + len(before) + len(deps) :]
        outs, blocks, held, sems = rest[:count], rest[count + 1 : 2 * count + 1], rest[-2], rest[-1]
        rest[count][...] = jnp.zeros((8, 128), F32)
        body(*refs[:given], *blocks, held)
        copies = [
            pltpu.make_async_copy(blocks[i], outs[i].at[pl.ds(layer, 1)], sems.at[i])
            for i in range(count)
        ]
        for copy in copies:
            copy.start()
        for copy in copies:
            copy.wait()

    return pl.pallas_call(
        kernel,
        out_shape=tuple(sds(shape, F32) for shape in shapes) + (sds((8, 128), F32),),
        in_specs=[SMEM] + [VMEM] * (given - 1) + [HBM] * len(before) + [ANY] * len(deps),
        out_specs=(HBM,) * count + (VMEM,),
        scratch_shapes=[pltpu.VMEM((1,) + shape[1:], F32) for shape in shapes]
        + [pltpu.VMEM(scratch, BF16), pltpu.SemaphoreType.DMA((count,))],
        input_output_aliases={given + index: index for index in range(len(before))},
        compiler_params=pltpu.CompilerParams(vmem_limit_bytes=LIMIT),
        cost_estimate=pl.CostEstimate(flops=100000000, bytes_accessed=0, transcendentals=0),
        name=name,
    )(*ins, *before, *deps)


def silu_bf16(condition):
    return (condition * (1.0 / (1.0 + jnp.exp(-condition)))).astype(BF16)


def ada_result(layer, meta, condition, rides, far, ada_weight, before, deps):
    given = () if condition is None else (condition,)
    slots = rides.shape[0] // 16
    half = D // 2

    def kernel(meta, rides, far, ada_hbm, *refs):
        ada_hbm_out, cond_out, known_out, sums_out, own_f32, far_f32, ada, ada_out, sems = refs[-9:]
        load = pltpu.make_async_copy(ada_hbm.at[pl.ds(layer, 1)], ada, sems.at[0])
        load.start()
        for block in range(D // 128):
            lanes = slice(block * 128, (block + 1) * 128)
            own_f32[block, :, :] = rides[:, lanes].astype(F32)
            far_f32[block, :, :] = far[:, lanes].astype(F32)
        first = meta[1] == 0
        grad_cond = jnp.zeros((2 * slots, half), F32)
        load.wait()
        sums_out[...] = jnp.zeros_like(sums_out)

        def latents_row(row):
            mine, other = (
                jnp.concatenate(
                    [held[block, pl.ds(row, slots, stride=16), :] for block in range(D // 128)], axis=1
                )
                for held in (own_f32, far_f32)
            )
            vectors = []
            for one, two in (
                (mine[:, :half], other[:, half:]),
                (mine[:, half:], other[:, :half]),
            ):
                vectors.append(
                    jnp.concatenate([jnp.where(first, one, two), jnp.where(first, two, one)], axis=1)
                )
            return jnp.concatenate(vectors, axis=0)

        if layer == 1:
            known = latents_row(14) + latents_row(15)
            known = jnp.where(meta[0] == 0, known[:, :half], known[:, half:])
            act = silu_bf16(known)
        else:
            known = (latents_row(14) * 32.0 + latents_row(15))[:, :half]
            act = silu_bf16(refs[0][...])
        known_out[...] = known
        for row in range(14):
            both = latents_row(row)
            sums_out[row : row + 1, :] = jnp.sum(both, axis=0, keepdims=True)
            if row < 6:
                cols = slice(row * D, (row + 1) * D)
                both = both.astype(BF16)
                ada_out[0, :, cols] = dot_tn(act, both)
                grad_cond = grad_cond + dot_nt(both, ada[0, :, cols])
        store = pltpu.make_async_copy(ada_out, ada_hbm_out.at[pl.ds(layer, 1)], sems.at[1])
        store.start()
        cond_out[...] = grad_cond
        store.wait()

    shape = ada_weight.shape
    return pl.pallas_call(
        kernel,
        out_shape=(sds(shape, F32),) + (sds((2 * slots, half), F32),) * 2 + (sds((16, D), F32),),
        in_specs=[SMEM, VMEM, VMEM, HBM]
        + [VMEM] * len(given)
        + [HBM] * len(before)
        + [ANY] * len(deps),
        out_specs=(HBM, VMEM, VMEM, VMEM),
        scratch_shapes=[pltpu.VMEM((D // 128, 16 * slots, 128), F32)] * 2
        + [
            pltpu.VMEM((1,) + shape[1:], BF16),
            pltpu.VMEM((1,) + shape[1:], F32),
            pltpu.SemaphoreType.DMA((2,)),
        ],
        input_output_aliases={4 + len(given): 0} if before else {},
        compiler_params=pltpu.CompilerParams(vmem_limit_bytes=LIMIT),
        cost_estimate=pl.CostEstimate(flops=100000000, bytes_accessed=0, transcendentals=0),
        name="ada_result",
    )(meta, rides, far, ada_weight, *given, *before, *deps)


def condition_result(meta, condition, labels, conds, sums, classes, deps):
    half = D // 2

    def body(meta, condition, labels, cond0, cond1, sums0, sums1, *outs):
        table, mine, send, ada, qv, out, up, down = outs
        condition = condition[...]
        sigmoid = 1.0 / (1.0 + jnp.exp(-condition))
        grads = (cond0[...] + cond1[...]) * sigmoid * (1.0 + condition * (1.0 - sigmoid))
        mine[...] = grads[0:1, :]
        send[...] = grads[1:2, :]
        labels = labels[:, 0:1]
        count = -(-classes // 128) * 128
        numbers = lax.broadcasted_iota(jnp.int32, (condition.shape[0], count), 1).astype(F32)
        one_hot = jnp.where(numbers == labels, 1.0, 0.0)
        total = lax.dot_general(
            grads,
            one_hot,
            (((0,), (0,)), ((), ())),
            precision=lax.Precision.HIGHEST,
            preferred_element_type=F32,
        )
        table[...] = total[:, 0:classes]
        low = meta[0] == 0
        for layer, rows in enumerate((sums0, sums1)):
            at = slice(layer, layer + 1)

            def pick(one, two):
                return jnp.where(low, rows[one : one + 1, :], rows[two : two + 1, :])

            for index in range(3):
                ada[at, index * D : (index + 1) * D] = pick(index, index + 3)
            qv[at, :] = pick(6, 7)
            for index in range(2):
                up[at, index * D : (index + 1) * D] = pick(10 + index, 12 + index)
            for ref, row in ((out, 8), (down, 9)):
                value = rows[row : row + 1, :]
                ref[at, :] = jnp.where(low, value[:, :half], value[:, half:])

    shapes = (
        (half, classes),
        (1, half),
        (1, half),
        (LAYERS, 3 * D),
        (LAYERS, D),
        (LAYERS, half),
        (LAYERS, 2 * D),
        (LAYERS, half),
    )
    return call(
        body,
        (meta, condition, labels, *conds, *sums),
        [SMEM] + [VMEM] * 6,
        tuple(sds(shape, F32) for shape in shapes),
        (VMEM,) * len(shapes),
        "condition_result",
        deps=deps,
    )


def both_halves(meta, mine, other):
    def body(meta, mine, other, out):
        low = meta[0] == 0
        a, b = mine[...], other[...]
        out[...] = jnp.concatenate([jnp.where(low, a, b), jnp.where(low, b, a)], axis=1)

    return call(
        body, (meta, mine, other), [SMEM, VMEM, VMEM], sds((1, D), F32), VMEM, "both_halves"
    )


def on_device(reps, *arguments):
    (
        latents,
        timestep_embed,
        labels,
        counts,
        class_table,
        ada_weight,
        ada_bias,
        qkv_weight,
        qv_bias,
        out_weight,
        out_bias,
        up_weight,
        up_bias,
        down_weight,
        down_bias,
        cotangent,
    ) = arguments
    half = D // 2
    rep = lax.axis_index("rep")
    x = lax.axis_index("shard")
    core, y, z = rep & 1, (rep >> 1) & 1, (rep >> 2) & 3
    meta = jnp.stack([x, core, y, z, jnp.minimum(counts[0], 1), z & 1]).astype(jnp.int32)

    def over_x(value):
        return lax.ppermute(value, "shard", [(0, 1), (1, 0)])

    def over_rep(value, distance):
        return lax.ppermute(value, "rep", [(r, r ^ distance) for r in range(reps)])

    CORE, Y, Z = 1, 2, 4

    first, send_a0, send_u0, send_d0 = first_messages(
        meta,
        timestep_embed,
        labels,
        (ada_bias, qv_bias, out_bias, up_bias, down_bias),
        qkv_weight,
        out_weight,
        up_weight,
        down_weight,
    )
    got_first = over_x(first)
    classes = class_table.shape[0]
    mine_part, send_part = condition_step(
        meta, first, got_first, class_table, ada_weight, (send_d0,)
    )
    send_a1, send_u1, send_d1 = pack(
        1, True, 4, meta, qkv_weight, out_weight, up_weight, down_weight, (send_part,), "pack_rest"
    )

    def relay(got, distance):
        if distance is None:
            return [got, over_rep(got, CORE)]
        next_got = over_rep(got, distance)
        return [got, next_got, over_rep(got, CORE), over_rep(next_got, CORE)]

    got_a0, got_u0, got_d0 = over_x(send_a0), over_x(send_u0), over_x(send_d0)
    got_a1, got_u1, got_d1 = over_x(send_a1), over_x(send_u1), over_x(send_d1)
    pieces_a0 = relay(got_a0, None)
    far_u0, far_d0 = over_rep(got_u0, Y), over_rep(got_d0, Y)
    got_part = over_x(send_part)
    got_part, far_u0, far_d0 = lax.optimization_barrier((got_part, far_u0, far_d0))
    vecs_all = vectors_step(meta, first, got_first, mine_part, got_part)
    pieces_m0 = []
    for near, far in ((got_u0, far_u0), (got_d0, far_d0)):
        pieces_m0 += [near, far, over_rep(near, CORE), over_rep(far, CORE)]
    vecs = [vecs_all[layer] for layer in range(LAYERS)]

    distances = [Z]
    while 2 * distances[-1] < reps:
        distances.append(2 * distances[-1])

    stream = latents[0]
    attn_weights = (qkv_weight, out_weight)
    mlp_weights = (up_weight, down_weight)
    *kept_a0, middle0 = attn_fwd(0, False, meta, stream, vecs[0], *attn_weights, pieces_a0)
    got_a1, got_u1, got_d1, middle0 = lax.optimization_barrier((got_a1, got_u1, got_d1, middle0))
    pieces_a1 = relay(got_a1, Y)
    pieces_m1 = relay(got_u1, Z) + relay(got_d1, Z)
    stream1, *kept_m0 = mlp_fwd(
        0, False, False, meta, middle0, vecs[0], *mlp_weights, pieces_m0
    )
    *kept_a1, middle1 = attn_fwd(1, False, meta, stream1, vecs[1], *attn_weights, pieces_a1)
    activations, *kept_m1 = mlp_fwd(1, True, True, meta, middle1, vecs[1], *mlp_weights, pieces_m1)

    last = [vecs_all]

    def deps():
        return (last[0],)

    def ran(result):
        last[0] = result[-1] if isinstance(result, (tuple, list)) else result
        return result

    def reduce_chunk(keep, sent, sums):
        got = over_rep(sent, CORE)
        yield
        keep, sent = ran(first_split(meta, keep, got, sums, deps()))
        got = over_x(sent)
        yield
        keep, sent = ran(next_split(2, meta, keep, sent, got, deps()))
        got = over_rep(sent, Y)
        yield
        steps = distances
        if sums is None:
            keep, sent = ran(next_split(5, meta, keep, sent, got, deps()))
            got = over_rep(sent, Z)
            steps = distances[1:]
            yield
        rows = keep.shape[0]
        for distance in steps:
            (sent,) = ran(add_join(keep, sent, got, rows, False, deps()))
            keep = sent
            got = over_rep(sent, distance)
            yield
        mine, *rides = ran(add_join(keep, sent, got, rows, True, deps()))
        if sums is None:
            got = over_rep(mine, Z)
            yield
            mine = ran(join(meta, mine, got, deps()))
        next_mine = over_rep(mine, Y)
        result = (mine, next_mine, over_rep(mine, CORE), over_rep(next_mine, CORE))
        if rides:
            rides = (rides[0], over_rep(rides[0], CORE))
        yield result, rides

    def advance(chunk, times=1):
        result = None
        for _ in range(times):
            result = next(chunk)
        return result

    more = len(distances) - 1

    keep, sent, grad, part_sums = mlp_bwd(
        True, meta, cotangent[0], vecs[1], (middle1, *kept_m1), deps()
    )
    m1 = reduce_chunk(keep, sent, None)
    advance(m1)
    keep, sent, grad, sums1 = ran(
        attn_bwd(1, 16, meta, grad, vecs[1], stream1, kept_a1, part_sums)
    )
    a1 = reduce_chunk(keep, sent, sums1)
    advance(a1)
    advance(m1)
    keep, sent, grad, part_sums = ran(
        mlp_bwd(False, meta, grad, vecs[0], (middle0, *kept_m0), deps())
    )
    m0 = reduce_chunk(keep, sent, None)
    advance(m0)
    advance(a1)
    keep, sent, grad_stream, sums0 = ran(
        attn_bwd(0, 16, meta, grad, vecs[0], stream, kept_a0, part_sums, deps())
    )
    a0 = reduce_chunk(keep, sent, sums0)
    advance(a0)
    for chunk in (m1, m0, a1, a0, m1, a1):
        advance(chunk)
    advance(m1, more)
    advance(m0)
    advance(a1, more)
    advance(a0)
    advance(m1)
    advance(m0)
    advance(a0)
    result_m1, _ = advance(m1)
    advance(m0, more)
    result_a1, rides1 = advance(a1)
    advance(a0, more)
    ada_grad, cond1, condition, sums1 = ran(ada_result(1, meta, None, *rides1, ada_weight, (), deps()))
    advance(m0)
    *mlp_grads, _ = ran(mlp_result(1, meta, result_m1, (), deps()))
    *attn_grads, _ = ran(attn_result(1, meta, result_a1, (), deps()))
    result_a0, rides0 = advance(a0)
    result_m0, _ = advance(m0)
    ada_grad, cond0, labels_all, sums0 = ran(
        ada_result(0, meta, condition, *rides0, ada_weight, (ada_grad,), deps())
    )
    table_grad, mine_cond, send_cond, *bias_grads = ran(
        condition_result(
            meta, condition, labels_all, (cond0, cond1), (sums0, sums1), classes, deps()
        )
    )
    other_cond = over_x(send_cond)
    qkv_grad, out_grad, _ = ran(attn_result(0, meta, result_a0, attn_grads, deps()))
    up_grad, down_grad, _ = ran(mlp_result(0, meta, result_m0, mlp_grads, deps()))
    cond_grad = both_halves(meta, mine_cond, other_cond)
    ada_b, qv_b, out_b, up_b, down_b = bias_grads

    return (
        activations[None],
        grad_stream[None],
        cond_grad,
        table_grad.T,
        ada_grad,
        ada_b,
        qkv_grad,
        qv_b,
        out_grad,
        out_b,
        up_grad,
        up_b,
        down_grad,
        down_b,
    )


def solution(mesh):
    reps = mesh.shape["rep"]
    both = ("rep", "shard")
    in_specs = (
        P(both, None, None),
        P(both, None),
        P(both),
        P(both),
        P(None, "shard"),
    ) + (P(None, "shard", None), P(None, "shard")) * 5 + (P(both, None, None),)
    out_specs = (
        P(both, None, None),
        P(both, None, None),
        P(both, None),
        P(None, "shard"),
    ) + (P(None, "shard", None), P(None, "shard")) * 5
    return jax.shard_map(
        functools.partial(on_device, reps),
        mesh=mesh,
        in_specs=in_specs,
        out_specs=out_specs,
        check_vma=False,
    )
```

```python
import functools
import math

import jax
import jax.numpy as jnp
from jax import lax
from jax.experimental import pallas as pl
from jax.experimental.pallas import tpu as pltpu
from jax.sharding import PartitionSpec as P

D = 384
HEAD_DIM = 64
LAYERS = 2
F32 = jnp.float32
BF16 = jnp.bfloat16

norm_eps = 1e-06
gelu_coeff = math.sqrt(2.0 / math.pi)
gelu_cubic = 0.044715

VMEM = pl.BlockSpec(memory_space=pltpu.VMEM)
SMEM = pl.BlockSpec(memory_space=pltpu.SMEM)
ANY = pl.BlockSpec(memory_space=pl.ANY)
HBM = pl.BlockSpec(memory_space=pltpu.HBM)
LIMIT = 16 * 1024 * 1024
SMALL = 8 * 1024 * 1024
WIDE = 56 * 1024 * 1024


def sds(shape, dtype):
    return jax.ShapeDtypeStruct(shape, dtype)


def norm_rows(values):
    centered = values - jnp.mean(values, axis=-1, keepdims=True)
    inv_dev = lax.rsqrt(jnp.mean(centered * centered, axis=-1, keepdims=True) + norm_eps)
    return (centered * inv_dev, inv_dev)


def norm_back(grad_normed, normed, inv_dev):
    return (
        grad_normed
        - jnp.mean(grad_normed, axis=-1, keepdims=True)
        - normed * jnp.mean(grad_normed * normed, axis=-1, keepdims=True)
    ) * inv_dev


def gelu_parts(pre_act):
    square = pre_act * pre_act
    inner_arg = gelu_coeff * pre_act * (1.0 + gelu_cubic * square)
    tanh_val = jnp.tanh(inner_arg)
    half_up = 0.5 * (1.0 + tanh_val)
    value_out = pre_act * half_up
    slope_out = half_up + 0.5 * pre_act * (1.0 - tanh_val * tanh_val) * (
        gelu_coeff + (3.0 * gelu_cubic * gelu_coeff) * square
    )
    return (value_out, slope_out)


def dot(a, b):
    return jnp.dot(a, b, preferred_element_type=F32)


def dot_nt(a, b):
    return lax.dot_general(a, b, (((1,), (1,)), ((), ())), preferred_element_type=F32)


def dot_tn(a, b):
    return lax.dot_general(a, b, (((0,), (0,)), ((), ())), preferred_element_type=F32)


def head_masks():
    lane = lax.broadcasted_iota(jnp.int32, (1, 2 * HEAD_DIM), 1)
    first = lane < HEAD_DIM
    return first, jnp.logical_not(first)


def keep_lanes(values, mask):
    return jnp.where(mask, values, jnp.zeros_like(values))


def rows_of(start, size):
    return pl.ds(pl.multiple_of(start, 16), size)


def attn_weight_copies(meta, layer, qkv_hbm, out_hbm, pieces, offsets, w_qkv, w_out, sems):
    half = qkv_hbm.shape[1]
    x = meta[0]
    copies = [
        (qkv_hbm.at[layer], w_qkv.at[rows_of(x * half, half), :]),
        (out_hbm.at[layer], w_out.at[rows_of(x * half, half), :]),
    ]
    for piece, offset in zip(pieces, offsets):
        size = piece.shape[0]
        start = (1 - x) * half + offset * size
        copies.append((piece.at[:, pl.ds(0, 3 * D)], w_qkv.at[rows_of(start, size), :]))
        copies.append((piece.at[:, pl.ds(3 * D, D)], w_out.at[rows_of(start, size), :]))
    return [pltpu.make_async_copy(s, d, sems.at[i]) for i, (s, d) in enumerate(copies)]


def mlp_weight_copies(meta, layer, up_hbm, down_hbm, pieces, offsets, w_up, w_down, sems):
    half = up_hbm.shape[1]
    tall = down_hbm.shape[1]
    blocks = tall // half
    x = meta[0]
    copies = [
        (up_hbm.at[layer], w_up.at[rows_of(x * half, half), :]),
        (down_hbm.at[layer], w_down.at[rows_of(x * tall, tall), :]),
    ]
    count = len(pieces) // 2
    for up_piece, down_piece, offset in zip(pieces[:count], pieces[count:], offsets):
        size = up_piece.shape[0]
        start = (1 - x) * half + offset * size
        copies.append((up_piece, w_up.at[rows_of(start, size), :]))
        for b in range(blocks):
            start = (1 - x) * tall + offset * (blocks * size) + b * size
            copies.append((down_piece.at[:, pl.ds(b * D, D)], w_down.at[rows_of(start, size), :]))
    return [pltpu.make_async_copy(s, d, sems.at[i]) for i, (s, d) in enumerate(copies)]


def piece_offsets(meta, count, far):
    core, y, z = meta[1], meta[2], meta[3]
    if count == 2:
        return [core, 1 - core]
    near = z % 2 if far else y
    return [
        near * 2 + core,
        (1 - near) * 2 + core,
        near * 2 + (1 - core),
        (1 - near) * 2 + (1 - core),
    ]


def call(body, ins, in_specs, out_shape, out_specs, name, scratch=(), deps=(), limit=SMALL, **more):
    given, late = len(ins), len(deps)

    def kernel(*refs):
        body(*refs[:given], *refs[given + late :])

    return pl.pallas_call(
        kernel,
        out_shape=out_shape,
        in_specs=list(in_specs) + [ANY] * late,
        out_specs=out_specs,
        scratch_shapes=list(scratch),
        compiler_params=pltpu.CompilerParams(vmem_limit_bytes=limit),
        cost_estimate=pl.CostEstimate(flops=10000000000, bytes_accessed=0, transcendentals=0),
        name=name,
        **more,
    )(*ins, *deps)


def pack_attn_copies(send, layer, parts, offset, qkv, out):
    size = qkv.shape[1] // parts
    rows = rows_of(offset * size, size)
    return [
        (qkv.at[layer, rows, :], send.at[:, pl.ds(0, 3 * D)]),
        (out.at[layer, rows, :], send.at[:, pl.ds(3 * D, D)]),
    ]


def pack_mlp_copies(send_up, send_down, layer, offset, up, down):
    size = up.shape[1] // 4
    blocks = down.shape[1] // up.shape[1]
    copies = [(up.at[layer, rows_of(offset * size, size), :], send_up)]
    for b in range(blocks):
        rows = rows_of(offset * (blocks * size) + b * size, size)
        copies.append((down.at[layer, rows, :], send_down.at[:, pl.ds(b * D, D)]))
    return copies


def pack(layer, far, parts, meta, qkv, out, up, down, deps, name):
    half = qkv.shape[1]
    size = half // 4

    def body(meta, qkv, out, up, down, send_attn, send_up, send_down, sems):
        copies = pack_attn_copies(send_attn, layer, parts, piece_offsets(meta, parts, False)[0], qkv, out)
        copies += pack_mlp_copies(send_up, send_down, layer, piece_offsets(meta, 4, far)[0], up, down)
        copies = [pltpu.make_async_copy(s, d, sems.at[i]) for i, (s, d) in enumerate(copies)]
        for copy in copies:
            copy.start()
        for copy in copies:
            copy.wait()

    return call(
        body,
        (meta, qkv, out, up, down),
        [SMEM] + [HBM] * 4,
        (sds((half // parts, 4 * D), BF16),) + (sds((size, 4 * D), BF16),) * 2,
        (VMEM,) * 3,
        name,
        scratch=[pltpu.SemaphoreType.DMA((8,))],
        deps=deps,
        limit=WIDE,
    )


def first_messages(meta, timestep, labels, biases, qkv, out, up, down):
    ins = (timestep,) + biases
    half = qkv.shape[1]

    def body(meta, labels, *refs):
        small, weights, outs, held, sems = refs[:6], refs[6:10], refs[10:14], refs[14:20], refs[20]
        send, send_attn, send_up, send_down = outs
        pairs = list(zip(small, held))
        pairs += pack_attn_copies(send_attn, 0, 2, piece_offsets(meta, 2, False)[0], *weights[:2])
        pairs += pack_mlp_copies(
            send_up, send_down, 0, piece_offsets(meta, 4, False)[0], *weights[2:]
        )
        copies = [pltpu.make_async_copy(s, d, sems.at[i]) for i, (s, d) in enumerate(pairs)]
        for copy in copies:
            copy.start()
        send[...] = jnp.zeros_like(send)
        send[4:5, D : D + 128] = jnp.full((1, 128), labels[0], jnp.int32).astype(F32)
        for copy in copies[:6]:
            copy.wait()
        time, ada, qv, out_b, up_b, down_b = held
        send[0:2, 0 : 3 * D] = ada[...].astype(F32)
        send[0:2, 3 * D : 4 * D] = qv[...].astype(F32)
        send[2:4, 0 : 2 * D] = up_b[...].astype(F32)
        send[2:4, 2 * D : 2 * D + D // 2] = out_b[...].astype(F32)
        send[2:4, 1024 : 1024 + D // 2] = down_b[...].astype(F32)
        send[4:5, 0:D] = time[...]
        for copy in copies[6:]:
            copy.wait()

    return call(
        body,
        (meta, labels) + ins + (qkv, out, up, down),
        [SMEM, SMEM] + [HBM] * 10,
        (sds((8, 4 * D), F32), sds((half // 2, 4 * D), BF16)) + (sds((half // 4, 4 * D), BF16),) * 2,
        (VMEM,) * 4,
        "first_messages",
        scratch=[pltpu.VMEM(member.shape, member.dtype) for member in ins]
        + [pltpu.SemaphoreType.DMA((16,))],
        limit=WIDE,
    )


def condition_kernel(meta, own, got, table_ref, ada, mine_out, send_out, table):
    half = D // 2
    x = meta[0]
    classes = table_ref.shape[1]
    aligned = classes // 128 * 128
    table[:, aligned:] = jnp.zeros((half, table.shape[1] - aligned), BF16)
    table[:, 0:classes] = table_ref[...]
    row = lax.broadcasted_iota(jnp.int32, (8, 1), 0)
    timestep = jnp.where(row == 0, own[4:5, 0:D], got[4:5, 0:D])
    label = jnp.where(row == 0, own[4:5, D : D + 1], got[4:5, D : D + 1])
    timestep = jnp.where(x == 0, timestep[:, :half], timestep[:, half:])
    classes = lax.broadcasted_iota(jnp.int32, (8, table.shape[1]), 1).astype(F32)
    one_hot = jnp.where(classes == label, 1.0, 0.0).astype(BF16)
    condition = timestep + dot_nt(one_hot, table[...])
    act = (condition * (1.0 / (1.0 + jnp.exp(-condition)))).astype(BF16)
    for ref, index in ((mine_out, 0), (send_out, 1)):
        ref[2:3, 0:half] = condition[index : index + 1, :]
        ref[2:3, half:] = jnp.zeros((1, 6 * D - half), F32)
    for layer in range(LAYERS):
        part = dot(act, ada[layer])
        mine_out[layer : layer + 1, :] = part[0:1, :]
        send_out[layer : layer + 1, :] = part[1:2, :]


def condition_step(meta, own, got, table, ada, deps):
    return call(
        condition_kernel,
        (meta, own, got, table.T, ada),
        [SMEM] + [VMEM] * 4,
        (sds((LAYERS + 1, 6 * D), F32),) * 2,
        (VMEM,) * 2,
        "condition",
        scratch=[pltpu.VMEM((D // 2, -(-table.shape[0] // 128) * 128), BF16)],
        deps=deps,
    )


def vectors_kernel(meta, own, got, mine_part, got_part, out):
    x = meta[0]
    low = jnp.where(x == 0, own[...], got[...])
    high = jnp.where(x == 0, got[...], own[...])
    modul = mine_part[...] + got_part[...]
    half = D // 2
    mine_cond, got_cond = mine_part[2:3, 0:half], got_part[2:3, 0:half]
    condition = jnp.concatenate(
        [jnp.where(x == 0, mine_cond, got_cond), jnp.where(x == 0, got_cond, mine_cond)], axis=1
    )
    label = jnp.broadcast_to(own[4:5, D : D + 1], (1, D))
    for layer in range(LAYERS):
        out[layer, 14:15, :] = condition
        out[layer, 15:16, :] = label
        rows = slice(layer, layer + 1)
        for member in range(6):
            side = low if member < 3 else high
            col = (member % 3) * D
            out[layer, member : member + 1, :] = (
                modul[rows, member * D : (member + 1) * D] + side[rows, col : col + D]
            )
        out[layer, 6:7, :] = low[rows, 3 * D : 4 * D]
        out[layer, 7:8, :] = high[rows, 3 * D : 4 * D]
        rows = slice(2 + layer, 3 + layer)
        for index, start in ((8, 2 * D), (9, 1024)):
            out[layer, index : index + 1, :] = jnp.concatenate(
                [low[rows, start : start + half], high[rows, start : start + half]], axis=1
            )
        for index, side, col in ((10, low, 0), (11, low, D), (12, high, 0), (13, high, D)):
            out[layer, index : index + 1, :] = side[rows, col : col + D]


def vectors_step(meta, own, got, mine_part, got_part):
    return call(
        vectors_kernel,
        (meta, own, got, mine_part, got_part),
        [SMEM] + [VMEM] * 4,
        sds((LAYERS, 16, D), F32),
        VMEM,
        "vectors",
    )


def attn_fwd_kernel(layer, far, count, *refs):
    meta, x_ref, vecs, qkv_hbm, out_hbm = refs[:5]
    pieces = refs[5 : 5 + count]
    modulated_out, qkv_out, prob_out, att_out, branch_out, w_qkv, w_out, middle_out = refs[
        5 + count : 13 + count
    ]
    sems = refs[13 + count]
    copies = attn_weight_copies(
        meta, layer, qkv_hbm, out_hbm, pieces, piece_offsets(meta, count, far), w_qkv, w_out, sems
    )
    for copy in copies:
        copy.start()
    stream = x_ref[...].astype(F32)
    normed, _ = norm_rows(stream)
    modulated = (normed * (1.0 + vecs[1:2, :]) + vecs[0:1, :]).astype(BF16)
    modulated_out[...] = modulated
    for copy in copies:
        copy.wait()
    for part in range(3):
        cols = slice(part * D, (part + 1) * D)
        value = dot(modulated, w_qkv[:, cols])
        if part == 0:
            value = value + vecs[6:7, :]
        if part == 2:
            value = value + vecs[7:8, :]
        qkv_out[:, cols] = value.astype(BF16)
    masks = head_masks()
    tokens = stream.shape[0]
    for pair in range(D // (2 * HEAD_DIM)):
        lanes = slice(pair * 2 * HEAD_DIM, (pair + 1) * 2 * HEAD_DIM)
        query = qkv_out[:, lanes]
        key = qkv_out[:, pair * 128 + D : (pair + 1) * 128 + D]
        value = qkv_out[:, pair * 128 + 2 * D : (pair + 1) * 128 + 2 * D]
        attended = None
        for member in range(2):
            head = 2 * pair + member
            scores = dot_nt(query, keep_lanes(key, masks[member])) * HEAD_DIM ** (-0.5)
            top = jnp.max(scores, axis=-1, keepdims=True)
            expo = jnp.exp(scores - top)
            prob = (expo * (1.0 / jnp.sum(expo, axis=-1, keepdims=True))).astype(BF16)
            prob_out[head * tokens : (head + 1) * tokens, :] = prob
            part = dot(prob, keep_lanes(value, masks[member]))
            attended = part if attended is None else attended + part
        att_out[:, lanes] = attended.astype(BF16)
    branch = dot(att_out[...], w_out[...]) + vecs[8:9, :]
    branch_out[...] = branch
    middle_out[...] = stream + vecs[2:3, :] * branch


def attn_fwd(layer, far, meta, x, vecs, qkv, out, pieces):
    tokens = x.shape[0]
    count = len(pieces)
    heads = D // HEAD_DIM
    return pl.pallas_call(
        functools.partial(attn_fwd_kernel, layer, far, count),
        out_shape=(
            sds((tokens, D), BF16),
            sds((tokens, 3 * D), BF16),
            sds((heads * tokens, tokens), BF16),
            sds((tokens, D), BF16),
            sds((tokens, D), F32),
            sds((D, 3 * D), BF16),
            sds((D, D), BF16),
            sds((tokens, D), F32),
        ),
        in_specs=[SMEM, VMEM, VMEM] + [HBM] * 2 + [ANY] * count,
        out_specs=(VMEM,) * 8,
        scratch_shapes=[
            pltpu.SemaphoreType.DMA((2 + 2 * count,)),
        ],
        compiler_params=pltpu.CompilerParams(vmem_limit_bytes=LIMIT),
        cost_estimate=pl.CostEstimate(flops=10000000000, bytes_accessed=0, transcendentals=0),
        name="attn_fwd",
    )(meta, x, vecs, qkv, out, *pieces)


def mlp_fwd_kernel(layer, far, count, last, late, *refs):
    refs = refs[:3] + refs[3 + late :]
    meta, middle_ref, vecs, up_hbm, down_hbm = refs[:5]
    pieces = refs[5 : 5 + count]
    x_out, mod_out, act_out, slope_out, branch_out, w_up, w_down, sems = refs[5 + count :]
    copies = mlp_weight_copies(
        meta, layer, up_hbm, down_hbm, pieces, piece_offsets(meta, count // 2, far), w_up, w_down, sems
    )
    for copy in copies:
        copy.start()
    middle = middle_ref[...]
    normed, _ = norm_rows(middle)
    mod_two = (normed * (1.0 + vecs[4:5, :]) + vecs[3:4, :]).astype(BF16)
    mod_out[...] = mod_two
    for copy in copies:
        copy.wait()
    for part in range(4):
        cols = slice(part * D, (part + 1) * D)
        pre_act = dot(mod_two, w_up[:, cols]) + vecs[10 + part : 11 + part, :]
        value, slope = gelu_parts(pre_act)
        act_out[:, cols] = value.astype(BF16)
        slope_out[:, cols] = slope.astype(BF16)
    branch = dot(act_out[...], w_down[...])
    branch = branch + vecs[9:10, :]
    branch_out[...] = branch
    result = middle + vecs[5:6, :] * branch
    if last:
        live = meta[4].astype(F32)
        result = result * live
    x_out[...] = result.astype(x_out.dtype)


def mlp_fwd(layer, far, last, meta, middle, vecs, up, down, pieces, deps=()):
    tokens = middle.shape[0]
    count = len(pieces)
    return pl.pallas_call(
        functools.partial(mlp_fwd_kernel, layer, far, count, last, len(deps)),
        out_shape=(
            sds((tokens, D), BF16 if last else F32),
            sds((tokens, D), BF16),
            sds((tokens, 4 * D), BF16),
            sds((tokens, 4 * D), BF16),
            sds((tokens, D), F32),
            sds((D, 4 * D), BF16),
            sds((4 * D, D), BF16),
        ),
        in_specs=[SMEM, VMEM, VMEM] + [ANY] * len(deps) + [HBM] * 2 + [ANY] * count,
        out_specs=(VMEM,) * 7,
        scratch_shapes=[
            pltpu.SemaphoreType.DMA((2 + 5 * count,)),
        ],
        compiler_params=pltpu.CompilerParams(vmem_limit_bytes=LIMIT),
        cost_estimate=pl.CostEstimate(flops=10000000000, bytes_accessed=0, transcendentals=0),
        name="mlp_fwd",
    )(meta, middle, vecs, *deps, up, down, *pieces)


def split_store(core, value, half, keep, send, rows):
    @pl.when(core == half)
    def _():
        keep[rows, :] = value

    @pl.when(core != half)
    def _():
        send[rows, :] = value


def mlp_bwd_kernel(masked, late, *refs):
    meta, grad_ref, vecs, middle_ref, branch_ref, act_ref, slope_ref, mod_ref, w_up, w_down = refs[:10]
    keep, send, grad_out, sums_out = refs[10 + late :]
    core = meta[1]
    grad = grad_ref[...].astype(F32)
    if masked:
        grad = grad * meta[4].astype(F32)
    sums_out[...] = jnp.zeros_like(sums_out)
    sums_out[5:6, :] = jnp.sum(grad * branch_ref[...], axis=0, keepdims=True)
    grad_branch = grad * vecs[5:6, :]
    sums_out[9:10, :] = jnp.sum(grad_branch, axis=0, keepdims=True)
    branch_bf = grad_branch.astype(BF16)
    half = D // 2
    for part in range(4):
        value = dot_tn(act_ref[:, part * D : (part + 1) * D], branch_bf).astype(BF16)
        base = (part // 2) * 4 * half + 2 * half
        split_store(core, value, part % 2, keep, send, slice(base, base + D))
    mod_two = mod_ref[...]
    grad_mod = None
    for part in range(4):
        cols = slice(part * D, (part + 1) * D)
        grad_pre = dot_nt(branch_bf, w_down[cols, :]) * slope_ref[:, cols].astype(F32)
        sums_out[10 + part : 11 + part, :] = jnp.sum(grad_pre, axis=0, keepdims=True)
        pre = grad_pre.astype(BF16)
        value = dot_tn(mod_two, pre).astype(BF16)
        for side in range(2):
            base = side * 4 * half + (part % 2) * half
            split_store(
                core,
                value[side * half : (side + 1) * half, :],
                part // 2,
                keep,
                send,
                slice(base, base + half),
            )
        term = dot_nt(pre, w_up[:, cols])
        grad_mod = term if grad_mod is None else grad_mod + term
    normed, inv_dev = norm_rows(middle_ref[...])
    sums_out[3:4, :] = jnp.sum(grad_mod, axis=0, keepdims=True)
    sums_out[4:5, :] = jnp.sum(grad_mod * normed, axis=0, keepdims=True)
    grad_out[...] = grad + norm_back(grad_mod * (1.0 + vecs[4:5, :]), normed, inv_dev)


def mlp_bwd(masked, meta, grad, vecs, kept, deps=()):
    middle, mod_two, act, slope, branch, w_up, w_down = kept
    tokens = middle.shape[0]
    late = len(deps)
    return pl.pallas_call(
        functools.partial(mlp_bwd_kernel, masked, late),
        out_shape=(
            sds((4 * D, D), BF16),
            sds((4 * D, D), BF16),
            sds((tokens, D), F32),
            sds((16, D), F32),
        ),
        in_specs=[SMEM] + [VMEM] * 9 + [ANY] * late,
        out_specs=(VMEM,) * 4,
        compiler_params=pltpu.CompilerParams(vmem_limit_bytes=LIMIT),
        cost_estimate=pl.CostEstimate(flops=10000000000, bytes_accessed=0, transcendentals=0),
        name="mlp_bwd",
    )(meta, grad, vecs, middle, branch, act, slope, mod_two, w_up, w_down, *deps)


def attn_bwd_kernel(layer, extra, late, *refs):
    meta, grad_ref, vecs, x_ref, modulated_ref, qkv_ref, prob_ref, att_ref, branch_ref = refs[:9]
    w_qkv, w_out, part_sums = refs[9:12]
    keep, send, grad_out, sums_out, ga_ref, proj_ref = refs[12 + late :]
    core = meta[1]
    half = D // 2
    tokens = grad_ref.shape[0]
    sums = {}
    grad = grad_ref[...]
    sums[2] = jnp.sum(grad * branch_ref[...], axis=0, keepdims=True)
    grad_battn = grad * vecs[2:3, :]
    sums[8] = jnp.sum(grad_battn, axis=0, keepdims=True)
    battn_bf = grad_battn.astype(BF16)

    def store(value, block):
        for side in range(2):
            base = side * 2 * half + (block % 2) * half
            split_store(
                core,
                value[side * half : (side + 1) * half, :],
                block // 2,
                keep,
                send,
                slice(base, base + half),
            )

    store(dot_tn(att_ref[...], battn_bf).astype(BF16), 3)
    ga_ref[...] = dot_nt(battn_bf, w_out[...]).astype(BF16)
    masks = head_masks()
    grad_q_sums, grad_v_sums = [], []
    for pair in range(D // (2 * HEAD_DIM)):
        lanes = slice(pair * 128, (pair + 1) * 128)
        query = qkv_ref[:, lanes]
        key = qkv_ref[:, pair * 128 + D : (pair + 1) * 128 + D]
        value = qkv_ref[:, pair * 128 + 2 * D : (pair + 1) * 128 + 2 * D]
        grad_att = ga_ref[:, lanes]
        grad_q = grad_k = grad_v = None
        for member in range(2):
            head = 2 * pair + member
            mask = masks[member]
            prob_bf = prob_ref[head * tokens : (head + 1) * tokens, :]
            prob = prob_bf.astype(F32)
            grad_prob = dot_nt(grad_att, keep_lanes(value, mask))
            term_v = dot_tn(prob_bf, keep_lanes(grad_att, mask))
            weighted = prob * grad_prob
            row_dot = jnp.sum(weighted, axis=-1, keepdims=True)
            grad_scores = ((weighted - prob * row_dot) * HEAD_DIM ** (-0.5)).astype(BF16)
            term_q = dot(grad_scores, keep_lanes(key, mask))
            term_k = dot_tn(grad_scores, keep_lanes(query, mask))
            grad_q = term_q if grad_q is None else grad_q + term_q
            grad_k = term_k if grad_k is None else grad_k + term_k
            grad_v = term_v if grad_v is None else grad_v + term_v
        grad_q_sums.append(jnp.sum(grad_q, axis=0, keepdims=True))
        grad_v_sums.append(jnp.sum(grad_v, axis=0, keepdims=True))
        proj_ref[:, lanes] = grad_q.astype(BF16)
        proj_ref[:, pair * 128 + D : (pair + 1) * 128 + D] = grad_k.astype(BF16)
        proj_ref[:, pair * 128 + 2 * D : (pair + 1) * 128 + 2 * D] = grad_v.astype(BF16)
    sums[6] = jnp.concatenate(grad_q_sums, axis=1)
    sums[7] = jnp.concatenate(grad_v_sums, axis=1)
    modulated = modulated_ref[...]
    for block in range(3):
        store(dot_tn(modulated, proj_ref[:, block * D : (block + 1) * D]).astype(BF16), block)
    grad_mod = dot_nt(proj_ref[...], w_qkv[...])
    normed, inv_dev = norm_rows(x_ref[...].astype(F32))
    sums[0] = jnp.sum(grad_mod, axis=0, keepdims=True)
    sums[1] = jnp.sum(grad_mod * normed, axis=0, keepdims=True)
    grad_out[...] = grad + norm_back(grad_mod * (1.0 + vecs[1:2, :]), normed, inv_dev)
    if layer == 1:
        high = vecs[14:15, :].astype(BF16).astype(F32)
        sums[14], sums[15] = high, vecs[14:15, :] - high
    else:
        high = jnp.floor(vecs[15:16, :] * (1.0 / 32.0))
        sums[14], sums[15] = high, vecs[15:16, :] - high * 32.0
    row = lax.broadcasted_iota(jnp.int32, (16, 1), 0)
    total = part_sums[...]
    for index, value in sums.items():
        total = jnp.where(row == index, value, total)
    total = total.astype(BF16)
    sums_out[...] = total
    if extra:
        send[4 * half : 4 * half + 16, :] = total


def attn_bwd(layer, extra, meta, grad, vecs, x, kept, part_sums, deps=()):
    modulated, qkv_val, prob, att, branch, w_qkv, w_out = kept
    tokens = x.shape[0]
    late = len(deps)
    return pl.pallas_call(
        functools.partial(attn_bwd_kernel, layer, extra, late),
        out_shape=(
            sds((2 * D, D), BF16),
            sds((2 * D + extra, D), BF16),
            sds((tokens, D), F32),
            sds((16, D), BF16),
        ),
        in_specs=[SMEM] + [VMEM] * 11 + [ANY] * late,
        out_specs=(VMEM,) * 4,
        scratch_shapes=[pltpu.VMEM((tokens, D), BF16), pltpu.VMEM((tokens, 3 * D), BF16)],
        compiler_params=pltpu.CompilerParams(vmem_limit_bytes=LIMIT),
        cost_estimate=pl.CostEstimate(flops=10000000000, bytes_accessed=0, transcendentals=0),
        name="attn_bwd",
    )(meta, grad, vecs, x, modulated, qkv_val, prob, att, branch, w_qkv, w_out, part_sums, *deps)


def add_rows(a, a_rows, b, b_rows):
    return (a[a_rows, :].astype(F32) + b[b_rows, :].astype(F32)).astype(BF16)


def first_split(meta, keep, got, sums, deps):
    half = keep.shape[0] // 2
    extra = 0 if sums is None else sums.shape[0]

    def body(meta, keep, got, *refs):
        mine_out, send_out = refs[-2:]
        x = meta[0]
        mine, other = rows_of(x * half, half), rows_of((1 - x) * half, half)
        mine_out[...] = add_rows(keep, mine, got, mine)
        send_out[0:half, :] = add_rows(keep, other, got, other)
        if extra:
            own, far = refs[0][...], got[2 * half : 2 * half + extra, :]
            lanes = D // 2
            low = jnp.concatenate([own[:, :lanes], far[:, :lanes]], axis=1)
            high = jnp.concatenate([own[:, lanes:], far[:, lanes:]], axis=1)
            send_out[half : half + extra, :] = jnp.where(meta[1] == 0, low, high)

    rides = () if sums is None else (sums,)
    return call(
        body,
        (meta, keep, got) + rides,
        [SMEM] + [VMEM] * (2 + len(rides)),
        (sds((half, D), BF16), sds((half + extra, D), BF16)),
        (VMEM, VMEM),
        "first_split",
        deps=deps,
    )


def next_split(axis, meta, keep, sent, got, deps):
    whole = keep.shape[0]
    half = whole // 2
    extra = got.shape[0] - whole

    def body(meta, keep, sent, got, mine_out, send_out):
        place = meta[axis]
        mine, other = rows_of(place * half, half), rows_of((1 - place) * half, half)
        mine_out[...] = add_rows(keep, mine, got, mine)
        send_out[0:half, :] = add_rows(keep, other, got, other)
        if extra:
            send_out[half : half + extra, :] = sent[whole : whole + extra, :]
            send_out[half + extra : half + 2 * extra, :] = got[whole : whole + extra, :]

    return call(
        body,
        (meta, keep, sent, got),
        [SMEM] + [VMEM] * 3,
        (sds((half, D), BF16), sds((half + 2 * extra, D), BF16)),
        (VMEM, VMEM),
        "next_split",
        deps=deps,
    )


def add_join(keep, sent, got, rows, last, deps):
    extra = got.shape[0] - rows

    def body(keep, sent, got, *outs):
        everything = slice(0, rows)
        outs[0][0:rows, :] = add_rows(keep, everything, got, everything)
        if extra:
            out, start = (outs[1], 0) if last else (outs[0], rows)
            out[start : start + extra, :] = sent[rows : rows + extra, :]
            out[start + extra : start + 2 * extra, :] = got[rows : rows + extra, :]

    out_shape = (sds((rows + (0 if last else 2 * extra), D), BF16),)
    if last and extra:
        out_shape = out_shape + (sds((2 * extra, D), BF16),)
    return call(
        body,
        (keep, sent, got),
        [VMEM] * 3,
        out_shape,
        (VMEM,) * len(out_shape),
        "add_join",
        deps=deps,
    )


def join(meta, mine, got, deps):
    rows = mine.shape[0]

    def body(meta, mine, got, out):
        low = meta[5]
        out[rows_of(low * rows, rows), :] = mine[...]
        out[rows_of((1 - low) * rows, rows), :] = got[...]

    return call(
        body, (meta, mine, got), [SMEM, VMEM, VMEM], sds((2 * rows, D), BF16), VMEM, "join", deps=deps
    )


def gather_rows(meta, refs, scratch):
    core, y = meta[1], meta[2]
    rows = refs[0].shape[0]
    for index, (c, v) in enumerate(((core, y), (core, 1 - y), (1 - core, y), (1 - core, 1 - y))):
        scratch[c, rows_of(v * rows, rows), :] = refs[index][...]


def attn_result(layer, meta, parts, before, deps):
    half = D // 2

    def body(meta, *refs):
        qkv_out, out_out, scratch = refs[-3:]
        gather_rows(meta, refs[:4], scratch)
        for block in range(4):
            value = scratch[block // 2, (block % 2) * half : (block % 2 + 1) * half, :].astype(F32)
            if block < 3:
                qkv_out[0, :, block * D : (block + 1) * D] = value
            else:
                out_out[0, :, :] = value

    return result_call(
        body,
        (meta, *parts),
        before,
        ((LAYERS, half, 3 * D), (LAYERS, half, D)),
        layer,
        (2, 2 * half, D),
        "attn_result",
        deps,
    )


def mlp_result(layer, meta, parts, before, deps):
    half = D // 2

    def body(meta, *refs):
        up_out, down_out, scratch = refs[-3:]
        gather_rows(meta, refs[:4], scratch)
        for block in range(4):
            value = scratch[block // 2, (block % 2) * half : (block % 2 + 1) * half, :].astype(F32)
            up_out[0, :, block * D : (block + 1) * D] = value
        for core in range(2):
            down_out[0, core * D : (core + 1) * D, :] = scratch[core, D : 2 * D, :].astype(F32)

    return result_call(
        body,
        (meta, *parts),
        before,
        ((LAYERS, half, 4 * D), (LAYERS, 2 * D, D)),
        layer,
        (2, 2 * D, D),
        "mlp_result",
        deps,
    )


def result_call(body, ins, before, shapes, layer, scratch, name, deps):
    given, count = len(ins), len(shapes)

    def kernel(*refs):
        rest = refs[given + len(before) + len(deps) :]
        outs, blocks, held, sems = rest[:count], rest[count + 1 : 2 * count + 1], rest[-2], rest[-1]
        rest[count][...] = jnp.zeros((8, 128), F32)
        body(*refs[:given], *blocks, held)
        copies = [
            pltpu.make_async_copy(blocks[i], outs[i].at[pl.ds(layer, 1)], sems.at[i])
            for i in range(count)
        ]
        for copy in copies:
            copy.start()
        for copy in copies:
            copy.wait()

    return pl.pallas_call(
        kernel,
        out_shape=tuple(sds(shape, F32) for shape in shapes) + (sds((8, 128), F32),),
        in_specs=[SMEM] + [VMEM] * (given - 1) + [HBM] * len(before) + [ANY] * len(deps),
        out_specs=(HBM,) * count + (VMEM,),
        scratch_shapes=[pltpu.VMEM((1,) + shape[1:], F32) for shape in shapes]
        + [pltpu.VMEM(scratch, BF16), pltpu.SemaphoreType.DMA((count,))],
        input_output_aliases={given + index: index for index in range(len(before))},
        compiler_params=pltpu.CompilerParams(vmem_limit_bytes=LIMIT),
        cost_estimate=pl.CostEstimate(flops=100000000, bytes_accessed=0, transcendentals=0),
        name=name,
    )(*ins, *before, *deps)


def silu_bf16(condition):
    return (condition * (1.0 / (1.0 + jnp.exp(-condition)))).astype(BF16)


def ada_result(layer, meta, condition, rides, far, ada_weight, before, deps):
    given = () if condition is None else (condition,)
    slots = rides.shape[0] // 16
    half = D // 2

    def kernel(meta, rides, far, ada_hbm, *refs):
        ada_hbm_out, cond_out, known_out, sums_out, own_f32, far_f32, ada, ada_out, sems = refs[-9:]
        load = pltpu.make_async_copy(ada_hbm.at[pl.ds(layer, 1)], ada, sems.at[0])
        load.start()
        for block in range(D // 128):
            lanes = slice(block * 128, (block + 1) * 128)
            own_f32[block, :, :] = rides[:, lanes].astype(F32)
            far_f32[block, :, :] = far[:, lanes].astype(F32)
        first = meta[1] == 0
        grad_cond = jnp.zeros((2 * slots, half), F32)
        load.wait()
        sums_out[...] = jnp.zeros_like(sums_out)

        def latents_row(row):
            mine, other = (
                jnp.concatenate(
                    [held[block, pl.ds(row, slots, stride=16), :] for block in range(D // 128)], axis=1
                )
                for held in (own_f32, far_f32)
            )
            vectors = []
            for one, two in (
                (mine[:, :half], other[:, half:]),
                (mine[:, half:], other[:, :half]),
            ):
                vectors.append(
                    jnp.concatenate([jnp.where(first, one, two), jnp.where(first, two, one)], axis=1)
                )
            return jnp.concatenate(vectors, axis=0)

        if layer == 1:
            known = latents_row(14) + latents_row(15)
            known = jnp.where(meta[0] == 0, known[:, :half], known[:, half:])
            act = silu_bf16(known)
        else:
            known = (latents_row(14) * 32.0 + latents_row(15))[:, :half]
            act = silu_bf16(refs[0][...])
        known_out[...] = known
        for row in range(14):
            both = latents_row(row)
            sums_out[row : row + 1, :] = jnp.sum(both, axis=0, keepdims=True)
            if row < 6:
                cols = slice(row * D, (row + 1) * D)
                both = both.astype(BF16)
                ada_out[0, :, cols] = dot_tn(act, both)
                grad_cond = grad_cond + dot_nt(both, ada[0, :, cols])
        store = pltpu.make_async_copy(ada_out, ada_hbm_out.at[pl.ds(layer, 1)], sems.at[1])
        store.start()
        cond_out[...] = grad_cond
        store.wait()

    shape = ada_weight.shape
    return pl.pallas_call(
        kernel,
        out_shape=(sds(shape, F32),) + (sds((2 * slots, half), F32),) * 2 + (sds((16, D), F32),),
        in_specs=[SMEM, VMEM, VMEM, HBM]
        + [VMEM] * len(given)
        + [HBM] * len(before)
        + [ANY] * len(deps),
        out_specs=(HBM, VMEM, VMEM, VMEM),
        scratch_shapes=[pltpu.VMEM((D // 128, 16 * slots, 128), F32)] * 2
        + [
            pltpu.VMEM((1,) + shape[1:], BF16),
            pltpu.VMEM((1,) + shape[1:], F32),
            pltpu.SemaphoreType.DMA((2,)),
        ],
        input_output_aliases={4 + len(given): 0} if before else {},
        compiler_params=pltpu.CompilerParams(vmem_limit_bytes=LIMIT),
        cost_estimate=pl.CostEstimate(flops=100000000, bytes_accessed=0, transcendentals=0),
        name="ada_result",
    )(meta, rides, far, ada_weight, *given, *before, *deps)


def condition_result(meta, condition, labels, conds, sums, classes, deps):
    half = D // 2

    def body(meta, condition, labels, cond0, cond1, sums0, sums1, *outs):
        table, mine, send, ada, qv, out, up, down = outs
        condition = condition[...]
        sigmoid = 1.0 / (1.0 + jnp.exp(-condition))
        grads = (cond0[...] + cond1[...]) * sigmoid * (1.0 + condition * (1.0 - sigmoid))
        mine[...] = grads[0:1, :]
        send[...] = grads[1:2, :]
        labels = labels[:, 0:1]
        count = -(-classes // 128) * 128
        numbers = lax.broadcasted_iota(jnp.int32, (condition.shape[0], count), 1).astype(F32)
        one_hot = jnp.where(numbers == labels, 1.0, 0.0)
        total = lax.dot_general(
            grads,
            one_hot,
            (((0,), (0,)), ((), ())),
            precision=lax.Precision.HIGHEST,
            preferred_element_type=F32,
        )
        table[...] = total[:, 0:classes]
        low = meta[0] == 0
        for layer, rows in enumerate((sums0, sums1)):
            at = slice(layer, layer + 1)

            def pick(one, two):
                return jnp.where(low, rows[one : one + 1, :], rows[two : two + 1, :])

            for index in range(3):
                ada[at, index * D : (index + 1) * D] = pick(index, index + 3)
            qv[at, :] = pick(6, 7)
            for index in range(2):
                up[at, index * D : (index + 1) * D] = pick(10 + index, 12 + index)
            for ref, row in ((out, 8), (down, 9)):
                value = rows[row : row + 1, :]
                ref[at, :] = jnp.where(low, value[:, :half], value[:, half:])

    shapes = (
        (half, classes),
        (1, half),
        (1, half),
        (LAYERS, 3 * D),
        (LAYERS, D),
        (LAYERS, half),
        (LAYERS, 2 * D),
        (LAYERS, half),
    )
    return call(
        body,
        (meta, condition, labels, *conds, *sums),
        [SMEM] + [VMEM] * 6,
        tuple(sds(shape, F32) for shape in shapes),
        (VMEM,) * len(shapes),
        "condition_result",
        deps=deps,
    )


def both_halves(meta, mine, other):
    def body(meta, mine, other, out):
        low = meta[0] == 0
        a, b = mine[...], other[...]
        out[...] = jnp.concatenate([jnp.where(low, a, b), jnp.where(low, b, a)], axis=1)

    return call(
        body, (meta, mine, other), [SMEM, VMEM, VMEM], sds((1, D), F32), VMEM, "both_halves"
    )


def on_device(reps, *arguments):
    (
        latents,
        timestep_embed,
        labels,
        counts,
        class_table,
        ada_weight,
        ada_bias,
        qkv_weight,
        qv_bias,
        out_weight,
        out_bias,
        up_weight,
        up_bias,
        down_weight,
        down_bias,
        cotangent,
    ) = arguments
    half = D // 2
    rep = lax.axis_index("rep")
    x = lax.axis_index("shard")
    core, y, z = rep & 1, (rep >> 1) & 1, (rep >> 2) & 3
    meta = jnp.stack([x, core, y, z, jnp.minimum(counts[0], 1), z & 1]).astype(jnp.int32)

    def over_x(value):
        return lax.ppermute(value, "shard", [(0, 1), (1, 0)])

    def over_rep(value, distance):
        return lax.ppermute(value, "rep", [(r, r ^ distance) for r in range(reps)])

    CORE, Y, Z = 1, 2, 4

    first, send_a0, send_u0, send_d0 = first_messages(
        meta,
        timestep_embed,
        labels,
        (ada_bias, qv_bias, out_bias, up_bias, down_bias),
        qkv_weight,
        out_weight,
        up_weight,
        down_weight,
    )
    got_first = over_x(first)
    classes = class_table.shape[0]
    mine_part, send_part = condition_step(
        meta, first, got_first, class_table, ada_weight, (send_a0,)
    )
    send_a1, send_u1, send_d1 = pack(
        1, True, 4, meta, qkv_weight, out_weight, up_weight, down_weight, (send_part,), "pack_rest"
    )

    def relay(got, distance):
        if distance is None:
            return [got, over_rep(got, CORE)]
        next_got = over_rep(got, distance)
        return [got, next_got, over_rep(got, CORE), over_rep(next_got, CORE)]

    send_u0, send_d0, send_part = lax.optimization_barrier((send_u0, send_d0, send_part))
    got_a0 = over_x(send_a0)
    got_part = over_x(send_part)
    got_u0, got_d0 = over_x(send_u0), over_x(send_d0)
    got_a1, got_u1, got_d1 = over_x(send_a1), over_x(send_u1), over_x(send_d1)
    pieces_a0 = relay(got_a0, None)
    far_u0, far_d0 = over_rep(got_u0, Y), over_rep(got_d0, Y)
    got_part, got_u0 = lax.optimization_barrier((got_part, got_u0))
    vecs_all = vectors_step(meta, first, got_first, mine_part, got_part)
    pieces_m0 = []
    for near, far in ((got_u0, far_u0), (got_d0, far_d0)):
        pieces_m0 += [near, far, over_rep(near, CORE), over_rep(far, CORE)]
    vecs = [vecs_all[layer] for layer in range(LAYERS)]

    distances = [Z]
    while 2 * distances[-1] < reps:
        distances.append(2 * distances[-1])

    stream = latents[0]
    attn_weights = (qkv_weight, out_weight)
    mlp_weights = (up_weight, down_weight)
    *kept_a0, middle0 = attn_fwd(0, False, meta, stream, vecs[0], *attn_weights, pieces_a0)
    got_a1, got_u1, got_d1, middle0 = lax.optimization_barrier((got_a1, got_u1, got_d1, middle0))
    pieces_a1 = relay(got_a1, Y)
    pieces_m1 = relay(got_u1, Z) + relay(got_d1, Z)
    stream1, *kept_m0 = mlp_fwd(
        0, False, False, meta, middle0, vecs[0], *mlp_weights, pieces_m0
    )
    *kept_a1, middle1 = attn_fwd(1, False, meta, stream1, vecs[1], *attn_weights, pieces_a1)
    activations, *kept_m1 = mlp_fwd(1, True, True, meta, middle1, vecs[1], *mlp_weights, pieces_m1)

    last = [vecs_all]

    def deps():
        return (last[0],)

    def ran(result):
        last[0] = result[-1] if isinstance(result, (tuple, list)) else result
        return result

    def reduce_chunk(keep, sent, sums, halve):
        got = over_rep(sent, CORE)
        yield
        keep, sent = ran(first_split(meta, keep, got, sums, deps()))
        got = over_x(sent)
        yield
        keep, sent = ran(next_split(2, meta, keep, sent, got, deps()))
        got = over_rep(sent, Y)
        yield
        steps = distances
        if halve:
            keep, sent = ran(next_split(5, meta, keep, sent, got, deps()))
            got = over_rep(sent, Z)
            steps = distances[1:]
            yield
        rows = keep.shape[0]
        for distance in steps:
            (joined,) = ran(add_join(keep, sent, got, rows, False, deps()))
            keep = sent = joined
            got = over_rep(sent, distance)
            yield
        mine, *rides = ran(add_join(keep, sent, got, rows, True, deps()))
        if rides:
            rides = (rides[0], over_rep(rides[0], CORE))
        if halve:
            got = over_rep(mine, Z)
            yield rides
            mine = ran(join(meta, mine, got, deps()))
        next_mine = over_rep(mine, Y)
        yield (mine, next_mine, over_rep(mine, CORE), over_rep(next_mine, CORE)), rides

    def advance(chunk, times=1):
        result = None
        for _ in range(times):
            result = next(chunk)
        return result

    more = len(distances) - 1

    keep, sent, grad, part_sums = mlp_bwd(
        True, meta, cotangent[0], vecs[1], (middle1, *kept_m1), deps()
    )
    m1 = reduce_chunk(keep, sent, None, True)
    advance(m1)
    keep, sent, grad, sums1 = ran(
        attn_bwd(1, 16, meta, grad, vecs[1], stream1, kept_a1, part_sums)
    )
    a1 = reduce_chunk(keep, sent, sums1, True)
    advance(a1)
    advance(m1)
    keep, sent, grad, part_sums = ran(
        mlp_bwd(False, meta, grad, vecs[0], (middle0, *kept_m0), deps())
    )
    m0 = reduce_chunk(keep, sent, None, True)
    advance(m0)
    advance(a1)
    keep, sent, grad_stream, sums0 = ran(
        attn_bwd(0, 16, meta, grad, vecs[0], stream, kept_a0, part_sums, deps())
    )
    a0 = reduce_chunk(keep, sent, sums0, True)
    advance(a0)
    advance(m1)
    advance(m0)
    advance(a1)
    advance(m1)
    advance(a0)
    advance(a1)
    advance(m1, more)
    advance(m0)
    advance(a1, more)
    advance(a0)
    advance(m1)
    advance(m0)
    advance(a0)
    result_m1, _ = advance(m1)
    advance(m0, more)
    rides1 = advance(a1)
    advance(a0, more)
    result_a1, rides1 = advance(a1)
    ada_grad, cond1, condition, sums1 = ran(ada_result(1, meta, None, *rides1, ada_weight, (), deps()))
    advance(m0)
    *mlp_grads, _ = ran(mlp_result(1, meta, result_m1, (), deps()))
    *attn_grads, _ = ran(attn_result(1, meta, result_a1, (), deps()))
    rides0 = advance(a0)
    result_m0, _ = advance(m0)
    ada_grad, cond0, labels_all, sums0 = ran(
        ada_result(0, meta, condition, *rides0, ada_weight, (ada_grad,), deps())
    )
    result_a0, rides0 = advance(a0)
    table_grad, mine_cond, send_cond, *bias_grads = ran(
        condition_result(
            meta, condition, labels_all, (cond0, cond1), (sums0, sums1), classes, deps()
        )
    )
    other_cond = over_x(send_cond)
    qkv_grad, out_grad, _ = ran(attn_result(0, meta, result_a0, attn_grads, deps()))
    up_grad, down_grad, _ = ran(mlp_result(0, meta, result_m0, mlp_grads, deps()))
    cond_grad = both_halves(meta, mine_cond, other_cond)
    ada_b, qv_b, out_b, up_b, down_b = bias_grads

    return (
        activations[None],
        grad_stream[None],
        cond_grad,
        table_grad.T,
        ada_grad,
        ada_b,
        qkv_grad,
        qv_b,
        out_grad,
        out_b,
        up_grad,
        up_b,
        down_grad,
        down_b,
    )


def solution(mesh):
    reps = mesh.shape["rep"]
    both = ("rep", "shard")
    in_specs = (
        P(both, None, None),
        P(both, None),
        P(both),
        P(both),
        P(None, "shard"),
    ) + (P(None, "shard", None), P(None, "shard")) * 5 + (P(both, None, None),)
    out_specs = (
        P(both, None, None),
        P(both, None, None),
        P(both, None),
        P(None, "shard"),
    ) + (P(None, "shard", None), P(None, "shard")) * 5
    return jax.shard_map(
        functools.partial(on_device, reps),
        mesh=mesh,
        in_specs=in_specs,
        out_specs=out_specs,
        check_vma=False,
    )
```
